512 devices in a mesh: ctx: 16 (over y, z_hi), ep: 32 (over z_lo, x, core).
Axes of the slice: x: 4, y: 8, z: 8 (z_hi: 2, z_lo: 4; z = z_hi * 4 + z_lo), core: 2. Of those that a mesh axis runs over, the one named last changes fastest.
Arguments:
- queries: bfloat16 [32, 96, 5120], P('ep', 'ctx'), may hold values from -200 to 200
- new_kv: bfloat16 [2, 32, 96, 1024], P(None, 'ep', 'ctx'), may hold values from -8 to 8
- cached_key_value: bfloat16 [2, 32, 4096, 1024], P(None, 'ep', 'ctx'), may hold values from -6 to 6
- cache_len: int32 [32], P('ep'), may hold values from 1 to 4096, 81920 in all
- residual: bfloat16 [32, 96, 5120], P('ep', 'ctx'), may hold values from -6 to 6
- norm_gain: bfloat16 [5120], replicated, may hold values from 0.099609375 to 1.8984375
- route_logit: float32 [32, 96], P('ep', 'ctx'), may hold values from 0.5 to 4
- route_id: int32 [32, 96, 1], P('ep'), may hold values from 0 to 15; in each aligned block of 96 rows (0 to 95, 96 to 191, ..., all dimensions but the last counted through in order) at most 12 rows name the same one
- w_gate: bfloat16 [32, 5120, 2048], P('ep', None, 'ctx'), may hold values from -0.078125 to 0.078125
- w_up: bfloat16 [32, 5120, 2048], P('ep', None, 'ctx'), may hold values from -0.078125 to 0.078125
- w_down: bfloat16 [32, 2048, 5120], P('ep', 'ctx'), may hold values from -0.1875 to 0.1875
Outputs:
- mixed_out: bfloat16 [32, 96, 5120], P('ep', 'ctx')
The draws below stay inside these ranges and needn't reach their ends.
Inputs may be any that keep to these rules, and one draw needn't show every extreme that they name: `route_id`: in each request's 96 tokens at most 12 choose one expert.
All inputs are finite; a program needn't handle non-finite values. No bound on the sum of `cache_len` on one device may be relied on, other than what follows from the above.
Results may differ from the reference program's by a relative error of at most 0.023.
Values may be sent and summed in bfloat16 or wider, within the bound.
A program may use at most 64 MiB of HBM per device.

```python
import math
import jax
import jax.numpy as jnp
import numpy as np
from jax import lax

D = 5120
QUERY_HEADS = 40
KEY_VALUE_HEADS = 8
HEAD_WIDTH = 128
FF = 4096
NEW_TOKENS = 96
CACHE_SLOTS = 4096
REQUEST_COUNT = 32
EXPERTS = 16
CAP = 12
FF_DEV = 128
N_EP = 32


def base_keys(key):
    return jax.random.truncated_normal(key, -6.0, 6.0, (REQUEST_COUNT, NEW_TOKENS, KEY_VALUE_HEADS * HEAD_WIDTH), jnp.float32)


def draw_new_kv(key, part):
    fresh_keys = base_keys(key)
    key = jax.random.fold_in(key, 3)
    value_random_key = jax.random.fold_in(key, 0)
    fresh_values = jax.random.truncated_normal(value_random_key, -6.0, 6.0, (REQUEST_COUNT, NEW_TOKENS, KEY_VALUE_HEADS * HEAD_WIDTH), jnp.float32)
    return jnp.stack([fresh_keys, fresh_values]).astype(jnp.bfloat16)


def draw_queries(key, part):
    key = jax.random.fold_in(key, 5)
    queries = jax.random.truncated_normal(key, -6.0, 6.0, (REQUEST_COUNT, NEW_TOKENS, QUERY_HEADS * HEAD_WIDTH), jnp.float32)
    return queries.astype(jnp.bfloat16)


def block_levels(stream_key, dims, cuts, low, top_value):
    level = 1.0
    for position, parts in cuts:
        steps = jax.random.uniform(jax.random.fold_in(jax.random.fold_in(stream_key, 6), position), (parts,), jnp.float32, low / len(cuts), top_value / len(cuts))
        level = level * jnp.repeat(jnp.exp(steps), dims[position] // parts).reshape((-1,) + (1,) * (len(dims) - 1 - position))
    return level


def length_profile(amount, total, bound, lean):
    portions = [(1 << 20) // math.isqrt(rank ** lean) + 1 for rank in range(2, amount + 1)]
    spare, holding = total - bound - (amount - 1), [1] * (amount - 1)
    while spare > 0:
        candidates = [i for i in range(amount - 1) if holding[i] < bound]
        pool, budget = sum([portions[i] for i in candidates]), spare
        for i in candidates:
            addition = min(bound - holding[i], max(1, budget * portions[i] // pool), spare)
            holding[i] = holding[i] + addition
            spare = spare - addition
    return np.array([bound] + holding)


def uneven(own_key, amount, total, bound, lean):
    if amount == 2:
        one = jax.random.randint(own_key, (), max(1, total - bound), min(bound, total - 1) + 1)
        return jnp.stack([one, total - one])
    tallies = jnp.asarray(length_profile(amount, total, bound, lean), jnp.int32)
    pairs = (amount - 1) // 2
    source_of, sink = tallies[1:1 + 2 * pairs:2], tallies[2:2 + 2 * pairs:2]
    slack = jnp.minimum(source_of - 1, bound - sink)
    shifted = jax.random.randint(jax.random.fold_in(own_key, 1), (pairs,), 0, 1 << 20) % (slack + 1)
    tallies = tallies.at[1:1 + 2 * pairs:2].set(source_of - shifted).at[2:2 + 2 * pairs:2].set(sink + shifted)
    return tallies[jax.random.permutation(jax.random.fold_in(own_key, 2), amount)]


def deal_out(stream_key, own, number, rows, number_of, top, bound, slope):
    sequence = jax.random.permutation(stream_key, number_of)
    heavy_load, common = portions_of(number_of, rows * top, bound, slope, True), portions_of(number_of, rows * top, bound, slope, False)
    places = jnp.arange(number_of)

    def named(lengths, rotation):
        used = int((lengths > 0).sum())
        fixed = max(1, used // 4)
        moved = fixed + (places - fixed + rotation * (used - fixed)) % max(1, number_of - fixed)
        return jnp.zeros((number_of,), jnp.int32).at[sequence[jnp.where(places < fixed, places, moved)]].set(jnp.asarray(lengths, jnp.int32))

    lengths = jnp.where(number % 4 == 0, named(heavy_load, number // 4), named(common, number - number // 4 - 1))
    mixed = jax.random.permutation(jax.random.fold_in(own, 3), number_of)
    source_of, sink = mixed[0:number_of // 2 * 2:2], mixed[1:number_of // 2 * 2:2]
    margin = jnp.minimum(lengths[source_of] - 1, bound - lengths[sink]) // 2
    margin = jnp.where((source_of == sequence[0]) | (sink == sequence[0]) | (lengths[sink] == 0), 0, jnp.maximum(margin, 0))
    moved = jax.random.randint(jax.random.fold_in(own, 4), (number_of // 2,), 0, 1 << 20) % (margin + 1)
    lengths = lengths.at[source_of].add(-moved).at[sink].add(moved)
    labels = jnp.searchsorted(jnp.cumsum(lengths), jnp.arange(rows * top), side="right").astype(jnp.int32)
    grid = labels.reshape(top, rows).T
    grid = grid[jax.random.permutation(jax.random.fold_in(own, 1), rows)]
    rotation = jax.random.randint(jax.random.fold_in(own, 2), (rows, 1), 0, top)
    return jnp.take_along_axis(grid, (jnp.arange(top)[None, :] + rotation) % top, axis=1)


def portions_of(amount, total, most, slope, full):
    weights = [(1 << 20) // math.isqrt(grade ** slope) + 1 for grade in range(1, amount + 1)]
    largest = most if full else min(most, max(-(-total // amount), total * weights[0] // sum(weights)))
    least = 1 if total - largest >= amount - 1 else 0
    counts, spare = [largest] + [least] * (amount - 1), total - largest - least * (amount - 1)
    while spare > 0:
        movable = [i for i in range(1, amount) if counts[i] < largest] or [i for i in range(1, amount) if counts[i] < most]
        pool, remaining = sum([weights[i] for i in movable]), spare
        for i in movable:
            addition = min(most - counts[i], max(1, remaining * weights[i] // pool), spare)
            counts[i] = counts[i] + addition
            spare = spare - addition
    return np.array(counts)


def centred(rng, dims, spread, limit, shards=(), held_as=jnp.bfloat16):
    entries = jax.random.normal(rng, dims, jnp.float32) * spread
    if len(shards) > 0:
        entries = block_levels(rng, dims, shards, -0.22, 0.18) * entries
    return jnp.clip(entries, min=-limit, max=limit).astype(held_as)


def setup_inputs(seed: int = 0) -> dict:
    splits = jax.random.split(jax.random.key(seed), 12)
    queries = draw_queries(jax.random.fold_in(splits[11], 71), 0)
    new_kv = draw_new_kv(jax.random.fold_in(splits[11], 71), 0)
    cached_key_value = centred(splits[2], (2, REQUEST_COUNT, CACHE_SLOTS, KEY_VALUE_HEADS * HEAD_WIDTH), 1.0, 6.0, ((1, 32), (2, 16)))
    cache_len = uneven(splits[3], REQUEST_COUNT, REQUEST_COUNT * CACHE_SLOTS * 5 // 8, CACHE_SLOTS, 2).astype(jnp.int32)
    residual = centred(splits[4], (REQUEST_COUNT, NEW_TOKENS, D), 1.0, 6.0, ((0, 32), (1, 16)))
    norm_gain = jnp.clip(1.0 + 0.18 * jax.random.normal(splits[5], (D,), jnp.float32), 0.099609375, 1.8984375).astype(jnp.bfloat16)
    route_logit = jnp.clip(0.5 + 3.5 * jax.random.uniform(splits[6], (REQUEST_COUNT, NEW_TOKENS), jnp.float32) ** block_levels(splits[6], (REQUEST_COUNT, NEW_TOKENS), ((0, 32), (1, 16)), -0.2, 0.2), 0.5, 4.0)
    route_id_keys = jax.random.split(jax.random.fold_in(splits[7], 1), REQUEST_COUNT * NEW_TOKENS // NEW_TOKENS)
    route_id_turns = jax.random.permutation(jax.random.fold_in(splits[7], 3), REQUEST_COUNT * NEW_TOKENS // NEW_TOKENS)
    route_id = jax.vmap(lambda own, number: deal_out(jax.random.fold_in(splits[7], 2), own, number, NEW_TOKENS, EXPERTS, 1, CAP, 2))(route_id_keys, route_id_turns).reshape((REQUEST_COUNT, NEW_TOKENS, 1))
    w_gate = centred(splits[8], (N_EP, D, FF // 2), D ** -0.5, 0.078125, ((0, 32), (2, 16)))
    w_up = centred(splits[9], (N_EP, D, FF // 2), D ** -0.5, 0.078125, ((0, 32), (2, 16)))
    w_down = centred(splits[10], (N_EP, FF // 2, D), (FF // 4) ** -0.5, 0.1875, ((0, 32), (1, 16)))
    return dict(queries=queries, new_kv=new_kv, cached_key_value=cached_key_value, cache_len=cache_len, residual=residual, norm_gain=norm_gain, route_logit=route_logit, route_id=route_id, w_gate=w_gate, w_up=w_up, w_down=w_down)


NEG_LARGE = -1e+30

def attend_request(inputs):
    query_row_block, new_rows, cache_rows, length = inputs
    key_row_block = jnp.concatenate([cache_rows[0], new_rows[0]], axis=0)
    value_row_block = jnp.concatenate([cache_rows[1], new_rows[1]], axis=0)
    query_group_width = QUERY_HEADS // KEY_VALUE_HEADS
    total_key_count = CACHE_SLOTS + NEW_TOKENS
    query_head_rows = query_row_block.reshape(NEW_TOKENS, KEY_VALUE_HEADS, query_group_width, HEAD_WIDTH).astype(jnp.float32)
    key_head_rows = key_row_block.reshape(total_key_count, KEY_VALUE_HEADS, HEAD_WIDTH).astype(jnp.float32)
    value_head_rows = value_row_block.reshape(total_key_count, KEY_VALUE_HEADS, HEAD_WIDTH).astype(jnp.float32)
    scores = jnp.einsum('tgjd,lgd->gjtl', query_head_rows, key_head_rows) * HEAD_WIDTH ** (-0.5)
    cache_ok = jnp.arange(CACHE_SLOTS, dtype=jnp.int32) < length
    token_index = jnp.arange(NEW_TOKENS, dtype=jnp.int32)
    new_ok = token_index[None, :] <= token_index[:, None]
    allowed = jnp.concatenate([jnp.broadcast_to(cache_ok[None, :], (NEW_TOKENS, CACHE_SLOTS)), new_ok], axis=1)
    scores = jnp.where(allowed, scores, NEG_LARGE)
    top_score = lax.optimization_barrier(jnp.max(scores, axis=-1, keepdims=True))
    weights = jnp.where(allowed, jnp.exp(scores - top_score), 0.0)
    weight_total = lax.optimization_barrier(jnp.sum(weights, axis=-1))
    rounded = lax.optimization_barrier(weights.astype(jnp.bfloat16)).astype(jnp.float32)
    weighted = jnp.einsum('gjtl,lgd->tgjd', rounded, value_head_rows)
    totals = jnp.transpose(weight_total, (2, 0, 1))[..., None]
    return (weighted / totals).reshape(NEW_TOKENS, QUERY_HEADS * HEAD_WIDTH)

def expert_rows(inputs):
    rows_in, gate_pair, up_pair, down_full = inputs
    gate_full = jnp.concatenate([gate_pair[0], gate_pair[1]], axis=1)
    up_full = jnp.concatenate([up_pair[0], up_pair[1]], axis=1)
    gate_out = jnp.dot(rows_in, gate_full, preferred_element_type=jnp.float32)
    up_out = jnp.dot(rows_in, up_full, preferred_element_type=jnp.float32)
    act = (jax.nn.silu(gate_out) * up_out).astype(jnp.bfloat16)
    slices = FF // FF_DEV
    act_slices = jnp.transpose(act.reshape(rows_in.shape[0], slices, FF_DEV), (1, 0, 2))
    down_slices = down_full.reshape(slices, FF_DEV, D)

    def add_slice(running, pieces):
        piece_act, piece_down = pieces
        product = jnp.dot(piece_act, piece_down, preferred_element_type=jnp.float32).astype(jnp.bfloat16)
        product = lax.optimization_barrier(product)
        return (running + product.astype(jnp.float32), None)
    start_sum = jnp.zeros((rows_in.shape[0], D), jnp.float32)
    result, unused = lax.scan(add_slice, start_sum, (act_slices, down_slices))
    return result

def reference(queries, new_kv, cached_key_value, cache_len, residual, norm_gain, route_logit, route_id, w_gate, w_up, w_down):
    attended = lax.map(attend_request, (queries, jnp.transpose(new_kv, (1, 0, 2, 3)), jnp.transpose(cached_key_value, (1, 0, 2, 3)), cache_len))
    hidden_state = (residual.astype(jnp.float32) + attended).astype(jnp.bfloat16)
    hidden_f32 = hidden_state.astype(jnp.float32)
    inv_rms = lax.rsqrt(lax.optimization_barrier(jnp.mean(hidden_f32 * hidden_f32, axis=-1, keepdims=True)) + 1e-05)
    expert_in = (hidden_f32 * inv_rms * norm_gain.astype(jnp.float32) * jax.nn.sigmoid(route_logit)[..., None]).astype(jnp.bfloat16)
    expert_ids = route_id[..., 0].astype(jnp.int32)
    one_hot = (expert_ids[..., None] == jnp.arange(EXPERTS, dtype=jnp.int32)).astype(jnp.int32)
    slot_rank = lax.optimization_barrier(jnp.sum((jnp.cumsum(one_hot, axis=1) - one_hot) * one_hot, axis=-1)).astype(jnp.int32)
    slot_row = (jnp.arange(REQUEST_COUNT, dtype=jnp.int32)[:, None] * CAP + slot_rank).astype(jnp.int32)
    buffers = jnp.zeros((EXPERTS, REQUEST_COUNT * CAP, D), jnp.bfloat16).at[expert_ids, slot_row].set(expert_in)
    outputs = lax.map(expert_rows, (buffers, w_gate.reshape(EXPERTS, 2, D, FF // 2), w_up.reshape(EXPERTS, 2, D, FF // 2), w_down.reshape(EXPERTS, FF, D)))
    routed = outputs[expert_ids, slot_row]
    return (hidden_f32 + routed).astype(jnp.bfloat16)
```

```python
import jax
import jax.numpy as jnp
from jax import lax
from jax.experimental import pallas as pl
from jax.experimental.pallas import tpu as pltpu
from jax.sharding import PartitionSpec as P

MESH = pl.DeviceIdType.MESH
BF16 = jnp.bfloat16
F32 = jnp.float32

GROUPS = 8
PER_GROUP = 5
HEAD = 128
TOK = 6
WIDTH = 5120
CACHE = 256
KEYS = 384
NY = 8
PART = 640
QUART = 1280
NEG = -1e30
FLOOR = -1e29

Q_AG = 0
Q_RS = 17
X_AG = 25
GO = 42
SIB_X = 62
SIB_P = 66
BACK = 70
Y_RS = 90
N_SEM = 98
CLASSES = (0, 1, -1, 2)


def iota(shape, dim):
    return lax.broadcasted_iota(jnp.int32, shape, dim)


def item_of(index, third):
    rho = index & 15
    late = rho - 12 + 4 * third
    tok = jnp.where(rho < 6, rho, jnp.where(rho < 12, rho - 6, jnp.where(late < 6, late, late - 6)))
    eighth = jnp.where(
        rho < 6, 2 * third, jnp.where(rho < 12, 2 * third + 1, jnp.where(late < 6, 6, 7))
    )
    return (index >> 4) * TOK + tok, eighth


def slot_of(index, third, half):
    rho = index & 15
    slot = jnp.where(rho < 12, rho, rho - 12 + 4 * third)
    eighth = jnp.where(rho < 12, 2 * third + half, 6 + half)
    return (index >> 4) * 16 + slot, eighth


def thirds_for(third, half):
    return sorted({third, half, half + 1})


def kernel(
    q_ref,
    new_ref,
    cache_ref,
    len_ref,
    res_ref,
    gain_ref,
    logit_ref,
    rid_ref,
    wg_ref,
    wu_ref,
    wd_ref,
    out_ref,
    qf,
    qg,
    pw,
    rin,
    za,
    zo,
    zi,
    attf,
    hid,
    xrow,
    xf,
    xg,
    sb,
    rb,
    po,
    ps,
    qb,
    rtn,
    rsb,
    rsi,
    zo2,
    zi2,
    wgu,
    wdx,
    kx,
    vx,
    newf,
    bias,
    send,
    recv,
    local,
):
    ctx = lax.axis_index("ctx")
    ep = lax.axis_index("ep")
    y, zh = lax.div(ctx, 2), lax.rem(ctx, 2)
    zl, x, core = lax.div(ep, 8), lax.rem(lax.div(ep, 2), 4), lax.rem(ep, 2)
    z = zh * 4 + zl
    expert = zl * 4 + x

    def at(dy=0, dz=0, dx=0, flip=False):
        ny = lax.rem(y + dy + NY, NY)
        nz = lax.rem(z + dz + 8, 8)
        nx = lax.rem(x + dx + 4, 4)
        nc = 1 - core if flip else core
        return (ny * 2 + lax.div(nz, 4), lax.rem(nz, 4) * 8 + nx * 2 + nc)

    def remote(src, dst, sem, device):
        return pltpu.make_async_remote_copy(
            src_ref=src,
            dst_ref=dst,
            send_sem=send.at[sem],
            recv_sem=recv.at[sem],
            device_id=device,
            device_id_type=MESH,
        )

    copies = [
        pltpu.make_async_copy(wg_ref.at[0], wgu.at[:, 0:128], local.at[0]),
        pltpu.make_async_copy(wu_ref.at[0], wgu.at[:, 128:256], local.at[1]),
    ]
    for j in range(3):
        copies.append(
            pltpu.make_async_copy(
                wd_ref.at[0, :, j * QUART : (j + 1) * QUART], wdx.at[j, 0:128], local.at[2 + 2 * j]
            )
        )
        copies.append(
            pltpu.make_async_copy(
                wd_ref.at[0, :, 3 * QUART : 4 * QUART], wdx.at[j, 128:256], local.at[3 + 2 * j]
            )
        )
    cache_copies = []
    for g in range(GROUPS):
        cols = slice(g * HEAD, (g + 1) * HEAD)
        cache_copies.append(
            pltpu.make_async_copy(
                cache_ref.at[0, 0, :, cols], kx.at[g, 0:CACHE], local.at[8 + 2 * g]
            )
        )
        cache_copies.append(
            pltpu.make_async_copy(
                cache_ref.at[1, 0, :, cols], vx.at[g, 0:CACHE, 0:HEAD], local.at[9 + 2 * g]
            )
        )
    for copy in cache_copies + copies:
        copy.start()

    barrier = pltpu.get_barrier_semaphore()
    partners = [at(dy=d) for d in range(1, NY)] + [at(dz=4), at(flip=True)]
    for dz in (0, 1, -1, 2, -2):
        partners += [at(dz=dz, dx=dx) for dx in range(4) if (dz, dx) != (0, 0)]
    for device in partners:
        pl.semaphore_signal(barrier, inc=1, device_id=device, device_id_type=MESH)

    qf[...] = jnp.zeros_like(qf)
    queries = q_ref[0].astype(F32)
    for g in range(GROUPS):
        for j in range(PER_GROUP):
            h = g * PER_GROUP + j
            qf[g, j * TOK : (j + 1) * TOK, :] = queries[:, h * HEAD : (h + 1) * HEAD]
    qg[ctx] = qf[...].astype(BF16)

    pl.semaphore_wait(barrier, len(partners))

    def block_of(dy, a):
        return lax.rem(y + dy + NY, NY) * 2 + (zh if a == 0 else 1 - zh)

    def gather(buf, base, on_step):
        started = []
        links = {}

        def link(way, d, a):
            if (way, d, a) not in links:
                sign = 1 if way == 0 else -1
                block = buf.at[block_of(-sign * (d - 1), a)]
                links[way, d, a] = remote(
                    block, block, base + 1 + (way * 4 + d - 1) * 2 + a, at(dy=sign)
                )
            return links[way, d, a]

        def go(way, d, a):
            link(way, d, a).start()
            started.append(link(way, d, a))

        own = buf.at[ctx]
        across = remote(own, own, base, at(dz=4))
        across.start()
        go(0, 1, 0)
        go(1, 1, 0)
        across.wait_recv()
        go(0, 1, 1)
        go(1, 1, 1)
        on_step(0)
        for d in range(1, 5):
            for a in (0, 1):
                for way in (0, 1):
                    if d == 4 and way != a:
                        continue
                    link(way, d, a).wait_recv()
                    if d < 3 or (d == 3 and way == a):
                        go(way, d + 1, a)
            on_step(d)
        across.wait_send()
        for copy in started:
            copy.wait_send()

    newf[...] = jnp.zeros_like(newf)
    newf[0, 0:TOK, :] = new_ref[0, 0].astype(F32)
    newf[1, 0:TOK, :] = new_ref[1, 0].astype(F32)
    for g in range(GROUPS):
        cols = slice(g * HEAD, (g + 1) * HEAD)
        kx[g, CACHE : CACHE + 16, :] = newf[0, :, cols].astype(BF16)
        vx[g, CACHE : CACHE + 16, 0:HEAD] = newf[1, :, cols].astype(BF16)
        kx[g, CACHE + 16 : KEYS, :] = jnp.zeros((KEYS - CACHE - 16, HEAD), BF16)
        vx[g, CACHE + 16 : KEYS, 0:HEAD] = jnp.zeros((KEYS - CACHE - 16, HEAD), BF16)
        vx[g, :, HEAD : 2 * HEAD] = jnp.ones((KEYS, HEAD), BF16)

    ids = rid_ref[...]
    one_hot = (ids == iota((96, 128), 1)).astype(F32)
    before = (iota((96, 96), 1) < iota((96, 96), 0)).astype(BF16)
    counts = jnp.dot(before, one_hot.astype(BF16), preferred_element_type=F32)
    rank = jnp.sum(counts * one_hot, axis=1, keepdims=True)
    slot_col = ids.astype(F32) * 16.0 + rank
    slot_lane = jnp.sum(
        jnp.where(iota((96, 128), 0) == iota((96, 128), 1), slot_col, 0.0), axis=0, keepdims=True
    )

    for copy in cache_copies:
        copy.wait()

    limit = jnp.minimum(len_ref[0] - ctx * CACHE, CACHE)
    scale = HEAD ** (-0.5)

    def attend(blocks):
        count = len(blocks)
        rows = 32 * count
        row = iota((rows, KEYS), 0)
        lane = iota((rows, KEYS), 1)
        r = row & 31
        tok = r
        for edge in (6, 12, 18, 24):
            tok = tok - jnp.where(r >= edge, 6, 0)
        for i, block in enumerate(blocks):
            tok = tok + jnp.where((row >> 5) == i, block * TOK, 0)
        new_ok = (lane >= CACHE) & (lane < CACHE + TOK) & (ctx * TOK + lane - CACHE <= tok)
        bias[0:rows, :] = jnp.where((lane < limit) | new_ok, 0.0, NEG)

        def group(g, carry):
            q = jnp.concatenate([qg[block, g] for block in blocks], axis=0)
            scores = lax.dot_general(
                q, kx[g], (((1,), (1,)), ((), ())), preferred_element_type=F32
            )
            scores = scores * scale + bias[0:rows, :]
            top = jnp.maximum(jnp.max(scores, axis=1, keepdims=True), FLOOR)
            top = top.astype(BF16).astype(F32)
            weights = jnp.exp(scores - top).astype(BF16)
            sums = jnp.dot(weights, vx[g], preferred_element_type=F32)
            shape = (count, 32, HEAD)
            weighted = sums[:, 0:HEAD].reshape(shape)
            total = sums[:, HEAD : 2 * HEAD].reshape(shape)
            tops = jnp.broadcast_to(top, (rows, HEAD)).reshape(shape)
            on = (iota(shape, 2) & 31) == iota(shape, 1)
            top_row = jnp.sum(jnp.where(on, tops, 0.0), axis=1, keepdims=True)
            total_row = jnp.sum(jnp.where(on, total, 0.0), axis=1, keepdims=True)
            at_row = iota(shape, 1)
            packed = jnp.where(
                at_row == 30, top_row, jnp.where(at_row == 31, total_row, weighted)
            ).astype(BF16)
            for i, block in enumerate(blocks):
                pw[block, g] = packed[i]
            return carry

        lax.fori_loop(0, GROUPS, group, 0)

    scatters = []

    def pair_of(dy):
        return pl.ds(lax.rem(y + dy + NY, NY) * 2, 2)

    def scatter(src, dst, base, d):
        copy = remote(src.at[pair_of(d)], dst.at[y], base + (d + NY) % NY - 1, at(dy=d))
        copy.start()
        scatters.append(copy)

    def attend_step(d):
        if d == 0:
            attend([block_of(0, 0), block_of(0, 1)])
            rin[y] = pw[pair_of(0)]
        elif d == 4:
            attend([block_of(4, 0), block_of(4, 1)])
            scatter(pw, rin, Q_RS, 4)
        else:
            attend([block_of(-d, 0), block_of(-d, 1), block_of(d, 0), block_of(d, 1)])
            scatter(pw, rin, Q_RS, -d)
            scatter(pw, rin, Q_RS, d)

    gather(qg, Q_AG, attend_step)
    for copy in scatters:
        copy.wait()
    scatters.clear()

    def merge(stack, count, normalize):
        wide = stack.astype(F32)
        tops = wide[:, 30, :]
        totals = wide[:, 31, :]
        top = jnp.max(tops, axis=0, keepdims=True)
        factor = jnp.exp(tops - top)
        total = jnp.sum(factor * totals, axis=0, keepdims=True)
        if normalize:
            factor = factor / total
        lane = iota((32, 128), 1)
        row = iota((32, 128), 0)
        on = ((lane & 31) == row) & (row < 30)
        merged = jnp.zeros((32, HEAD), F32)
        for part in range(count // 4):
            spread = jnp.zeros((32, 128), F32)
            for i in range(4):
                spread = jnp.where((lane >> 5) == i, factor[4 * part + i : 4 * part + i + 1], spread)
            spread = jnp.where(on, spread, 0.0)
            high = spread.astype(BF16)
            low = (spread - high.astype(F32)).astype(BF16)
            rows = stack[4 * part : 4 * part + 4].reshape(128, HEAD)
            merged = merged + jnp.dot(high, rows, preferred_element_type=F32)
            merged = merged + jnp.dot(low, rows, preferred_element_type=F32)
        return merged, top, total

    def merge_y(block, dst):
        def group(g, carry):
            merged, top, total = merge(rin[:, block, g], NY, False)
            at_row = iota((32, HEAD), 0)
            dst[g] = jnp.where(
                at_row == 30, top, jnp.where(at_row == 31, total, merged)
            ).astype(BF16)
            return carry

        lax.fori_loop(0, GROUPS, group, 0)

    merge_y(1 - zh, zo)
    across = remote(zo, zi, Q_RS + 7, at(dz=4))
    across.start()
    merge_y(zh, za)
    across.wait()

    def merge_z(g, carry):
        own, other = za[g], zi[g]
        empty_row = iota((2, 32, HEAD), 1)
        empty = jnp.where(empty_row == 30, FLOOR, 0.0).astype(BF16)
        stack = jnp.concatenate([own[None], other[None], empty], axis=0)
        merged, _, _ = merge(stack, 4, True)
        attf[g] = merged
        return carry

    lax.fori_loop(0, GROUPS, merge_z, 0)

    for g in range(GROUPS):
        for j in range(PER_GROUP):
            h = g * PER_GROUP + j
            cols = slice(h * HEAD, (h + 1) * HEAD)
            state = res_ref[0, :, cols].astype(F32) + attf[g, j * TOK : (j + 1) * TOK, :]
            hid[0:TOK, cols] = state.astype(BF16).astype(F32)
    state = hid[0:TOK, :]
    inv_rms = lax.rsqrt(jnp.mean(state * state, axis=1, keepdims=True) + 1e-05)
    logit = jnp.broadcast_to(logit_ref[...], (TOK, TOK))
    logit = jnp.sum(
        jnp.where(iota((TOK, TOK), 0) == iota((TOK, TOK), 1), logit, 0.0), axis=1, keepdims=True
    )
    gate = 1.0 / (1.0 + jnp.exp(-logit))
    xrow[0:TOK, :] = state * inv_rms * gain_ref[...].astype(F32) * gate

    def pieces():
        for e in range(6):
            yield (e % 2 * 6, e // 2 * PART), (0, e * PART), 6
        yield (12, 0), (0, 6 * PART), 4
        yield (12, PART), (4, 6 * PART), 2
        yield (14, PART), (0, 7 * PART), 2
        yield (12, 2 * PART), (2, 7 * PART), 4

    for (pr, pc), (wr, wc), n in pieces():
        xf[pr : pr + n, pc : pc + PART] = xrow[wr : wr + n, wc : wc + PART]
    xg[ctx] = xf[...].astype(BF16)

    gather(xg, X_AG, lambda d: None)

    rows_in = [xg[:, :, k * PART : (k + 1) * PART].reshape(256, PART) for k in range(3)]
    lanes = iota((96, 256), 1)
    lane_slots = []
    for k in range(3):
        tok, _ = item_of(lanes, k)
        lane_slots.append(
            jnp.sum(jnp.where(iota((96, 256), 0) == tok, slot_col, 0.0), axis=0, keepdims=True)
        )
    for j in range(3):
        for half in range(2):
            target, eighth_row = slot_of(iota((256, 256), 0), j, half)
            target = target.astype(F32)
            total = jnp.zeros((256, PART), F32)
            for k in thirds_for(j, half):
                _, eighth_lane = item_of(iota((256, 256), 1), k)
                pick = (lane_slots[k] == target) & (eighth_lane == eighth_row)
                pick = jnp.where(pick, 1.0, 0.0).astype(BF16)
                total = total + jnp.dot(pick, rows_in[k], preferred_element_type=F32)
            start = j * QUART + half * PART
            sb[:, :, start : start + PART] = total.astype(BF16).reshape(16, 16, PART)

    own_block = pltpu.make_async_copy(sb.at[expert], rb.at[core, 0], local.at[24])
    own_block.start()
    HALF = 3 * QUART // 2

    def routes(cls):
        for dx in range(4):
            if cls == 3:
                yield 12 + dx, slice(0, HALF), 2, dx, 12 + 2 * dx
                yield 12 + dx, slice(HALF, 2 * HALF), -2, dx, 13 + 2 * dx
            elif (cls, dx) != (0, 0):
                yield cls * 4 + dx, slice(0, 2 * HALF), CLASSES[cls], dx, cls * 4 + dx

    sent = [[], [], [], []]
    for cls in (3, 1, 2, 0):
        for i, cols, dz, dx, sem in routes(cls):
            to = lax.rem(zl + dz + 4, 4) * 4 + lax.rem(x + dx, 4)
            copy = remote(
                sb.at[to, :, cols], rb.at[core, i, :, cols], GO + sem, at(dz=dz, dx=dx)
            )
            copy.start()
            sent[cls].append(copy)

    for copy in copies:
        copy.wait()

    def experts(rows):
        n = rows.shape[0]
        main = jnp.dot(rows, wgu[0 : 3 * QUART, :], preferred_element_type=F32)
        r = iota((n, 256), 0) & 15
        tail = None
        for j in (2, 1, 0):
            part = jnp.dot(
                rows[:, j * QUART : (j + 1) * QUART],
                wgu[3 * QUART : 4 * QUART, :],
                preferred_element_type=F32,
            )
            part = pltpu.roll(part, n - 12 + 4 * j, 0)
            tail = part if tail is None else jnp.where(r < 4 * (j + 1), part, tail)
        both = main + tail
        gate_out, up_out = both[:, 0:128], both[:, 128:256]
        act = gate_out / (1.0 + jnp.exp(-gate_out)) * up_out
        r = iota((n, 128), 0) & 15
        act = jnp.where(r < 12, act, 0.0).astype(BF16).astype(F32)
        results = []
        for j in range(3):
            late = jnp.where(r >= 12, pltpu.roll(act, 12 - 4 * j, 0), 0.0)
            left = jnp.concatenate([act, late], axis=1).astype(BF16)
            results.append(jnp.dot(left, wdx[j], preferred_element_type=F32).astype(BF16))
        return results

    def run_experts(src, dst):
        rows = src.reshape(64, 3 * QUART)
        for j, part in enumerate(experts(rows)):
            dst[:, :, j * QUART : (j + 1) * QUART] = part.reshape(4, 16, QUART)

    across_x = []
    for cls in range(4):
        for copy in sent[cls]:
            copy.wait_recv()
        if cls == 0:
            own_block.wait()
        blocks = rb.at[core, pl.ds(cls * 4, 4)]
        copy = remote(blocks, blocks, SIB_X + cls, at(flip=True))
        copy.start()
        across_x.append(copy)
        run_experts(rb[core, cls * 4 : cls * 4 + 4], po.at[cls * 4 : cls * 4 + 4])

    across_p = []
    for cls in range(4):
        across_x[cls].wait_recv()
        run_experts(rb[1 - core, cls * 4 : cls * 4 + 4], ps.at[cls * 4 : cls * 4 + 4])
        blocks = pl.ds(cls * 4, 4)
        copy = remote(ps.at[blocks], qb.at[blocks], SIB_P + cls, at(flip=True))
        copy.start()
        across_p.append(copy)

    back = []
    for cls in range(4):
        across_p[cls].wait_recv()
        blocks = slice(cls * 4, cls * 4 + 4)
        po[blocks] = (po[blocks].astype(F32) + qb[blocks].astype(F32)).astype(BF16)
        for i, cols, dz, dx, sem in routes(cls):
            copy = remote(
                po.at[i, :, cols], rtn.at[expert, :, cols], BACK + sem, at(dz=-dz, dx=-dx)
            )
            copy.start()
            back.append(copy)
        if cls == 0:
            own_back = pltpu.make_async_copy(po.at[0], rtn.at[expert], local.at[25])
            own_back.start()

    for cls in range(4):
        for copy in sent[cls]:
            copy.wait_send()
        across_x[cls].wait_send()
        across_p[cls].wait_send()
    own_back.wait()
    for copy in back:
        copy.wait()

    lanes = iota((256, 128), 1)
    for k in range(3):
        tok, _ = item_of(iota((256, 128), 0), k)
        row_slots = jnp.sum(jnp.where(lanes == tok, slot_lane, 0.0), axis=1, keepdims=True)
        _, eighth_row = item_of(iota((256, 256), 0), k)
        total = jnp.zeros((256, PART), F32)
        for j in range(3):
            for half in range(2):
                if k not in thirds_for(j, half):
                    continue
                target, eighth_lane = slot_of(iota((256, 256), 1), j, half)
                pick = (row_slots == target.astype(F32)) & (eighth_lane == eighth_row)
                pick = jnp.where(pick, 1.0, 0.0).astype(BF16)
                start = j * QUART + half * PART
                source = rtn[:, :, start : start + PART].reshape(256, PART)
                total = total + jnp.dot(pick, source, preferred_element_type=F32)
        rsb[:, :, k * PART : (k + 1) * PART] = total.astype(BF16).reshape(16, 16, PART)

    rsi[y] = rsb[pair_of(0)]
    for d in (4, 3, -3, 2, -2, 1, -1):
        scatter(rsb, rsi, Y_RS, d)
    for copy in scatters:
        copy.wait()

    def add_up(block):
        total = rsi[0, block].astype(F32)
        for i in range(1, NY):
            total = total + rsi[i, block].astype(F32)
        return total

    zo2[...] = add_up(1 - zh).astype(BF16)
    across = remote(zo2, zi2, Y_RS + 7, at(dz=4))
    across.start()
    xf[...] = add_up(zh)
    across.wait()
    xf[...] = xf[...] + zi2[...].astype(F32)
    for (pr, pc), (wr, wc), n in pieces():
        xrow[wr : wr + n, wc : wc + PART] = xf[pr : pr + n, pc : pc + PART]
    out_ref[0] = (hid[0:TOK, :] + xrow[0:TOK, :]).astype(BF16)


def body(
    queries,
    new_kv,
    cached_key_value,
    cache_len,
    residual,
    norm_gain,
    route_logit,
    route_id,
    w_gate,
    w_up,
    w_down,
):
    vmem = pl.BlockSpec(memory_space=pltpu.VMEM)
    smem = pl.BlockSpec(memory_space=pltpu.SMEM)
    hbm = pl.BlockSpec(memory_space=pl.ANY)
    block = (GROUPS, 32, HEAD)
    slots = (16, 16, 3 * QUART)
    return pl.pallas_call(
        kernel,
        out_shape=jax.ShapeDtypeStruct((1, TOK, WIDTH), BF16),
        in_specs=[vmem, vmem, hbm, smem, vmem, vmem, vmem, vmem, hbm, hbm, hbm],
        out_specs=vmem,
        scratch_shapes=[
            pltpu.VMEM(block, F32),
            pltpu.VMEM((16,) + block, BF16),
            pltpu.VMEM((16,) + block, BF16),
            pltpu.VMEM((NY, 2) + block, BF16),
            pltpu.VMEM(block, BF16),
            pltpu.VMEM(block, BF16),
            pltpu.VMEM(block, BF16),
            pltpu.VMEM(block, F32),
            pltpu.VMEM((8, WIDTH), F32),
            pltpu.VMEM((8, WIDTH), F32),
            pltpu.VMEM((16, 3 * PART), F32),
            pltpu.VMEM((16, 16, 3 * PART), BF16),
            pltpu.VMEM(slots, BF16),
            pltpu.VMEM((2,) + slots, BF16),
            pltpu.VMEM(slots, BF16),
            pltpu.VMEM(slots, BF16),
            pltpu.VMEM(slots, BF16),
            pltpu.VMEM(slots, BF16),
            pltpu.VMEM((16, 16, 3 * PART), BF16),
            pltpu.VMEM((NY, 2, 16, 3 * PART), BF16),
            pltpu.VMEM((16, 3 * PART), BF16),
            pltpu.VMEM((16, 3 * PART), BF16),
            pltpu.VMEM((WIDTH, 256), BF16),
            pltpu.VMEM((3, 256, QUART), BF16),
            pltpu.VMEM((GROUPS, KEYS, HEAD), BF16),
            pltpu.VMEM((GROUPS, KEYS, 2 * HEAD), BF16),
            pltpu.VMEM((2, 16, GROUPS * HEAD), F32),
            pltpu.VMEM((128, KEYS), F32),
            pltpu.SemaphoreType.DMA((N_SEM,)),
            pltpu.SemaphoreType.DMA((N_SEM,)),
            pltpu.SemaphoreType.DMA((26,)),
        ],
        compiler_params=pltpu.CompilerParams(
            collective_id=0, has_side_effects=True, vmem_limit_bytes=56 * 1024 * 1024
        ),
    )(
        queries,
        new_kv,
        cached_key_value,
        cache_len,
        residual,
        norm_gain.reshape(1, WIDTH),
        route_logit,
        route_id.reshape(96, 1),
        w_gate,
        w_up,
        w_down,
    )


def solution(mesh):
    placed = (
        P("ep", "ctx", None),
        P(None, "ep", "ctx", None),
        P(None, "ep", "ctx", None),
        P("ep"),
        P("ep", "ctx", None),
        P(),
        P("ep", "ctx"),
        P("ep", None, None),
        P("ep", None, "ctx"),
        P("ep", None, "ctx"),
        P("ep", "ctx", None),
    )
    return jax.shard_map(
        body, mesh=mesh, in_specs=placed, out_specs=P("ep", "ctx", None), check_vma=False
    )
```

```python
import jax
import jax.numpy as jnp
from jax import lax
from jax.experimental import pallas as pl
from jax.experimental.pallas import tpu as pltpu
from jax.sharding import PartitionSpec as P

MESH = pl.DeviceIdType.MESH
BF16 = jnp.bfloat16
F32 = jnp.float32

GROUPS = 8
PER_GROUP = 5
HEAD = 128
TOK = 6
WIDTH = 5120
CACHE = 256
KEYS = 384
NY = 8
PART = 640
QUART = 1280
NEG = -1e30
FLOOR = -1e29

Q_AG = 0
Q_RS = 17
X_AG = 28
GO = 45
SIB_X = 65
SIB_P = 69
BACK = 73
Y_RS = 93
N_SEM = 104
CLASSES = (0, 1, -1, 2)


def iota(shape, dim):
    return lax.broadcasted_iota(jnp.int32, shape, dim)


def item_of(index, third):
    rho = index & 15
    late = rho - 12 + 4 * third
    tok = jnp.where(rho < 6, rho, jnp.where(rho < 12, rho - 6, jnp.where(late < 6, late, late - 6)))
    eighth = jnp.where(
        rho < 6, 2 * third, jnp.where(rho < 12, 2 * third + 1, jnp.where(late < 6, 6, 7))
    )
    return (index >> 4) * TOK + tok, eighth


def slot_of(index, third, half):
    rho = index & 15
    slot = jnp.where(rho < 12, rho, rho - 12 + 4 * third)
    eighth = jnp.where(rho < 12, 2 * third + half, 6 + half)
    return (index >> 4) * 16 + slot, eighth


def thirds_for(third, half):
    return sorted({third, half, half + 1})


def kernel(
    q_ref,
    new_ref,
    cache_ref,
    len_ref,
    res_ref,
    gain_ref,
    logit_ref,
    rid_ref,
    wg_ref,
    wu_ref,
    wd_ref,
    out_ref,
    qf,
    qg,
    pw,
    rin,
    za,
    zo,
    zi,
    r3,
    r4,
    mg,
    attf,
    hid,
    xrow,
    xf,
    xg,
    sb,
    rb,
    pp,
    qb,
    rtn,
    rsb,
    rsi,
    f3,
    f4,
    fm,
    zo2,
    zi2,
    wgu,
    wdx,
    kx,
    vx,
    newf,
    bias,
    send,
    recv,
    local,
):
    ctx = lax.axis_index("ctx")
    ep = lax.axis_index("ep")
    y, zh = lax.div(ctx, 2), lax.rem(ctx, 2)
    zl, x, core = lax.div(ep, 8), lax.rem(lax.div(ep, 2), 4), lax.rem(ep, 2)
    z = zh * 4 + zl
    expert = zl * 4 + x

    def at(dy=0, dz=0, dx=0, flip=False):
        ny = lax.rem(y + dy + NY, NY)
        nz = lax.rem(z + dz + 8, 8)
        nx = lax.rem(x + dx + 4, 4)
        nc = 1 - core if flip else core
        return (ny * 2 + lax.div(nz, 4), lax.rem(nz, 4) * 8 + nx * 2 + nc)

    def remote(src, dst, sem, device):
        return pltpu.make_async_remote_copy(
            src_ref=src,
            dst_ref=dst,
            send_sem=send.at[sem],
            recv_sem=recv.at[sem],
            device_id=device,
            device_id_type=MESH,
        )

    copies = [
        pltpu.make_async_copy(wg_ref.at[0], wgu.at[:, 0:128], local.at[0]),
        pltpu.make_async_copy(wu_ref.at[0], wgu.at[:, 128:256], local.at[1]),
    ]
    for j in range(3):
        copies.append(
            pltpu.make_async_copy(
                wd_ref.at[0, :, j * QUART : (j + 1) * QUART], wdx.at[j, 0:128], local.at[2 + 2 * j]
            )
        )
        copies.append(
            pltpu.make_async_copy(
                wd_ref.at[0, :, 3 * QUART : 4 * QUART], wdx.at[j, 128:256], local.at[3 + 2 * j]
            )
        )
    cache_copies = []
    for g in range(GROUPS):
        cols = slice(g * HEAD, (g + 1) * HEAD)
        cache_copies.append(
            pltpu.make_async_copy(
                cache_ref.at[0, 0, :, cols], kx.at[g, 0:CACHE], local.at[8 + 2 * g]
            )
        )
        cache_copies.append(
            pltpu.make_async_copy(
                cache_ref.at[1, 0, :, cols], vx.at[g, 0:CACHE, 0:HEAD], local.at[9 + 2 * g]
            )
        )
    for copy in cache_copies + copies:
        copy.start()

    barrier = pltpu.get_barrier_semaphore()
    partners = [at(dy=d) for d in (1, -1, 2, -2)] + [at(dz=4), at(flip=True)]
    for dz in (0, 1, -1, 2, -2):
        partners += [at(dz=dz, dx=dx) for dx in range(4) if (dz, dx) != (0, 0)]
    for device in partners:
        pl.semaphore_signal(barrier, inc=1, device_id=device, device_id_type=MESH)

    qf[...] = jnp.zeros_like(qf)
    queries = q_ref[0].astype(F32)
    for g in range(GROUPS):
        for j in range(PER_GROUP):
            h = g * PER_GROUP + j
            qf[g, j * TOK : (j + 1) * TOK, :] = queries[:, h * HEAD : (h + 1) * HEAD]
    qg[ctx] = qf[...].astype(BF16)

    pl.semaphore_wait(barrier, len(partners))

    def block_of(dy, a):
        return lax.rem(y + dy + NY, NY) * 2 + (zh if a == 0 else 1 - zh)

    def gather(buf, base, on_step):
        started = []
        links = {}

        def link(way, d, a):
            if (way, d, a) not in links:
                sign = 1 if way == 0 else -1
                block = buf.at[block_of(-sign * (d - 1), a)]
                links[way, d, a] = remote(
                    block, block, base + 1 + (way * 4 + d - 1) * 2 + a, at(dy=sign)
                )
            return links[way, d, a]

        def go(way, d, a):
            link(way, d, a).start()
            started.append(link(way, d, a))

        own = buf.at[ctx]
        across = remote(own, own, base, at(dz=4))
        across.start()
        go(0, 1, 0)
        go(1, 1, 0)
        across.wait_recv()
        go(0, 1, 1)
        go(1, 1, 1)
        on_step(0)
        for d in range(1, 5):
            for a in (0, 1):
                for way in (0, 1):
                    if d == 4 and way != a:
                        continue
                    link(way, d, a).wait_recv()
                    if d < 3 or (d == 3 and way == a):
                        go(way, d + 1, a)
            on_step(d)
        across.wait_send()
        for copy in started:
            copy.wait_send()

    newf[...] = jnp.zeros_like(newf)
    fresh = new_ref[0].astype(F32)
    newf[0, 0:TOK, :] = fresh[:, 0, :]
    newf[1, 0:TOK, :] = fresh[:, 1, :]
    for g in range(GROUPS):
        cols = slice(g * HEAD, (g + 1) * HEAD)
        kx[g, CACHE : CACHE + 16, :] = newf[0, :, cols].astype(BF16)
        vx[g, CACHE : CACHE + 16, 0:HEAD] = newf[1, :, cols].astype(BF16)
        kx[g, CACHE + 16 : KEYS, :] = jnp.zeros((KEYS - CACHE - 16, HEAD), BF16)
        vx[g, CACHE + 16 : KEYS, 0:HEAD] = jnp.zeros((KEYS - CACHE - 16, HEAD), BF16)
        vx[g, :, HEAD : 2 * HEAD] = jnp.ones((KEYS, HEAD), BF16)

    ids = jnp.sum(
        jnp.where(iota((96, 96), 0) == iota((96, 96), 1), rid_ref[0], 0), axis=1, keepdims=True
    )
    one_hot = (ids == iota((96, 128), 1)).astype(F32)
    before = (iota((96, 96), 1) < iota((96, 96), 0)).astype(BF16)
    counts = jnp.dot(before, one_hot.astype(BF16), preferred_element_type=F32)
    rank = jnp.sum(counts * one_hot, axis=1, keepdims=True)
    slot_col = ids.astype(F32) * 16.0 + rank
    slot_lane = jnp.sum(
        jnp.where(iota((96, 128), 0) == iota((96, 128), 1), slot_col, 0.0), axis=0, keepdims=True
    )

    for copy in cache_copies:
        copy.wait()

    limit = jnp.minimum(len_ref[0] - ctx * CACHE, CACHE)
    scale = HEAD ** (-0.5)

    def attend(blocks):
        count = len(blocks)
        rows = 32 * count
        row = iota((rows, KEYS), 0)
        lane = iota((rows, KEYS), 1)
        r = row & 31
        tok = r
        for edge in (6, 12, 18, 24):
            tok = tok - jnp.where(r >= edge, 6, 0)
        for i, block in enumerate(blocks):
            tok = tok + jnp.where((row >> 5) == i, block * TOK, 0)
        new_ok = (lane >= CACHE) & (lane < CACHE + TOK) & (ctx * TOK + lane - CACHE <= tok)
        bias[0:rows, :] = jnp.where((lane < limit) | new_ok, 0.0, NEG)

        def group(g, carry):
            q = jnp.concatenate([qg[block, g] for block in blocks], axis=0)
            scores = lax.dot_general(
                q, kx[g], (((1,), (1,)), ((), ())), preferred_element_type=F32
            )
            scores = scores * scale + bias[0:rows, :]
            top = jnp.maximum(jnp.max(scores, axis=1, keepdims=True), FLOOR)
            top = top.astype(BF16).astype(F32)
            weights = jnp.exp(scores - top).astype(BF16)
            sums = jnp.dot(weights, vx[g], preferred_element_type=F32)
            shape = (count, 32, HEAD)
            weighted = sums[:, 0:HEAD].reshape(shape)
            total = sums[:, HEAD : 2 * HEAD].reshape(shape)
            tops = jnp.broadcast_to(top, (rows, HEAD)).reshape(shape)
            on = (iota(shape, 2) & 31) == iota(shape, 1)
            top_row = jnp.sum(jnp.where(on, tops, 0.0), axis=1, keepdims=True)
            total_row = jnp.sum(jnp.where(on, total, 0.0), axis=1, keepdims=True)
            at_row = iota(shape, 1)
            packed = jnp.where(
                at_row == 30, top_row, jnp.where(at_row == 31, total_row, weighted)
            ).astype(BF16)
            for i, block in enumerate(blocks):
                pw[block, g] = packed[i]
            return carry

        lax.fori_loop(0, GROUPS, group, 0)

    scatters = []

    def pair_of(dy):
        return pl.ds(lax.rem(y + dy + NY, NY) * 2, 2)

    def ship(src, dst, sem, d):
        copy = remote(src, dst, sem, at(dy=d))
        copy.start()
        scatters.append(copy)
        return copy

    def ship_near(src, dst, base):
        ship(src.at[pair_of(1)], dst.at[1], base, 1)
        ship(src.at[pair_of(-1)], dst.at[2], base + 1, -1)

    def ship_three(src, dst, base):
        up = ship(src.at[pair_of(3)], dst.at[0], base + 2, 1)
        down = ship(src.at[pair_of(-3)], dst.at[1], base + 3, -1)
        return up, down

    def ship_four(src, dst, base):
        up = ship(src.at[block_of(4, 0)], dst.at[0], base + 4, 2)
        down = ship(src.at[block_of(4, 1)], dst.at[1], base + 5, -2)
        return up, down

    far = {}

    def attend_step(d):
        if d == 0:
            attend([block_of(0, 0), block_of(0, 1)])
            rin[0] = pw[pair_of(0)]
        elif d == 4:
            attend([block_of(4, 0), block_of(4, 1)])
            far[4] = ship_four(pw, r4, Q_RS)
        else:
            attend([block_of(-d, 0), block_of(-d, 1), block_of(d, 0), block_of(d, 1)])
            if d == 1:
                ship_near(pw, rin, Q_RS)
            if d == 3:
                far[3] = ship_three(pw, r3, Q_RS)

    empty_row = iota((3, 32, HEAD), 1)
    empty = jnp.where(empty_row == 30, FLOOR, 0.0).astype(BF16)

    def settle_rin(g, carry):
        for i in range(3):
            for a in range(2):
                rin[5 + i, a, g] = empty[i]
        return carry

    lax.fori_loop(0, GROUPS, settle_rin, 0)
    gather(qg, Q_AG, attend_step)

    def merge(stack, count, normalize):
        wide = stack.astype(F32)
        tops = wide[:, 30, :]
        totals = wide[:, 31, :]
        top = jnp.max(tops, axis=0, keepdims=True)
        factor = jnp.exp(tops - top)
        total = jnp.sum(factor * totals, axis=0, keepdims=True)
        if normalize:
            factor = factor / total
        lane = iota((32, 128), 1)
        row = iota((32, 128), 0)
        on = ((lane & 31) == row) & (row < 30)
        merged = jnp.zeros((32, HEAD), F32)
        for part in range(count // 4):
            spread = jnp.zeros((32, 128), F32)
            for i in range(4):
                spread = jnp.where((lane >> 5) == i, factor[4 * part + i : 4 * part + i + 1], spread)
            spread = jnp.where(on, spread, 0.0)
            high = spread.astype(BF16)
            low = (spread - high.astype(F32)).astype(BF16)
            rows = stack[4 * part : 4 * part + 4].reshape(128, HEAD)
            merged = merged + jnp.dot(high, rows, preferred_element_type=F32)
            merged = merged + jnp.dot(low, rows, preferred_element_type=F32)
        return merged, top, total

    def merged_block(stack, count):
        merged, top, total = merge(stack, count, False)
        at_row = iota((32, HEAD), 0)
        return jnp.where(at_row == 30, top, jnp.where(at_row == 31, total, merged)).astype(BF16)

    for side in (0, 1):
        far[3][side].wait_recv()
        for a in (1 - side, side):
            if a == side:
                far[4][side].wait_recv()

            def group(g, carry, side=side, a=a):
                position = zh if a == 0 else 1 - zh
                own = pw[block_of(2 - 4 * side, a), g]
                third = r3[side, position, g]
                fourth = r4[side, g] if a == side else empty[0]
                stack = jnp.concatenate([own[None], third[None], fourth[None], empty[0:1]], axis=0)
                mg[side, a, g] = merged_block(stack, 4)
                return carry

            lax.fori_loop(0, GROUPS, group, 0)
            position = zh if a == 0 else 1 - zh
            ship(
                mg.at[side, a], rin.at[3 + side, position], Q_RS + 6 + 2 * side + a, 2 - 4 * side
            )
    for copy in scatters:
        copy.wait_send()
    for copy in scatters:
        if not any(copy is other for other in far[3] + far[4]):
            copy.wait_recv()
    scatters.clear()

    def merge_y(block, dst):
        def group(g, carry):
            dst[g] = merged_block(rin[:, block, g], NY)
            return carry

        lax.fori_loop(0, GROUPS, group, 0)

    merge_y(1 - zh, zo)
    across = remote(zo, zi, Q_RS + 10, at(dz=4))
    across.start()
    merge_y(zh, za)
    across.wait()

    def merge_z(g, carry):
        own, other = za[g], zi[g]
        stack = jnp.concatenate([own[None], other[None], empty[0:2]], axis=0)
        merged, _, _ = merge(stack, 4, True)
        attf[g] = merged
        return carry

    lax.fori_loop(0, GROUPS, merge_z, 0)

    for g in range(GROUPS):
        for j in range(PER_GROUP):
            h = g * PER_GROUP + j
            cols = slice(h * HEAD, (h + 1) * HEAD)
            state = res_ref[0, :, cols].astype(F32) + attf[g, j * TOK : (j + 1) * TOK, :]
            hid[0:TOK, cols] = state.astype(BF16).astype(F32)
    state = hid[0:TOK, :]
    inv_rms = lax.rsqrt(jnp.mean(state * state, axis=1, keepdims=True) + 1e-05)
    logit = jnp.broadcast_to(logit_ref[...], (TOK, TOK))
    logit = jnp.sum(
        jnp.where(iota((TOK, TOK), 0) == iota((TOK, TOK), 1), logit, 0.0), axis=1, keepdims=True
    )
    gate = 1.0 / (1.0 + jnp.exp(-logit))
    xrow[0:TOK, :] = state * inv_rms * gain_ref[...].reshape(1, WIDTH).astype(F32) * gate

    def pieces():
        for e in range(6):
            yield (e % 2 * 6, e // 2 * PART), (0, e * PART), 6
        yield (12, 0), (0, 6 * PART), 4
        yield (12, PART), (4, 6 * PART), 2
        yield (14, PART), (0, 7 * PART), 2
        yield (12, 2 * PART), (2, 7 * PART), 4

    for (pr, pc), (wr, wc), n in pieces():
        xf[pr : pr + n, pc : pc + PART] = xrow[wr : wr + n, wc : wc + PART]
    xg[ctx] = xf[...].astype(BF16)

    gather(xg, X_AG, lambda d: None)

    rows_in = [xg[:, :, k * PART : (k + 1) * PART].reshape(256, PART) for k in range(3)]
    lanes = iota((96, 256), 1)
    lane_slots = []
    for k in range(3):
        tok, _ = item_of(lanes, k)
        lane_slots.append(
            jnp.sum(jnp.where(iota((96, 256), 0) == tok, slot_col, 0.0), axis=0, keepdims=True)
        )
    for j in range(3):
        for half in range(2):
            target, eighth_row = slot_of(iota((256, 256), 0), j, half)
            target = target.astype(F32)
            total = jnp.zeros((256, PART), F32)
            for k in thirds_for(j, half):
                _, eighth_lane = item_of(iota((256, 256), 1), k)
                pick = (lane_slots[k] == target) & (eighth_lane == eighth_row)
                pick = jnp.where(pick, 1.0, 0.0).astype(BF16)
                total = total + jnp.dot(pick, rows_in[k], preferred_element_type=F32)
            start = j * QUART + half * PART
            sb[:, :, start : start + PART] = total.astype(BF16).reshape(16, 16, PART)

    own_block = pltpu.make_async_copy(sb.at[expert], rb.at[0, core, 0], local.at[24])
    own_block.start()
    HALF = 3 * QUART // 2

    def routes(cls):
        for dx in range(4):
            if cls == 3:
                yield slice(0, HALF), 2, dx, 12 + 2 * dx
                yield slice(HALF, 2 * HALF), -2, dx, 13 + 2 * dx
            elif (cls, dx) != (0, 0):
                yield slice(0, 2 * HALF), CLASSES[cls], dx, cls * 4 + dx

    sent = [[], [], [], []]
    for cls in range(4):
        for cols, dz, dx, sem in routes(cls):
            to = lax.rem(zl + dz + 4, 4) * 4 + lax.rem(x + dx, 4)
            copy = remote(
                sb.at[to, :, cols], rb.at[cls, core, dx, :, cols], GO + sem, at(dz=dz, dx=dx)
            )
            copy.start()
            sent[cls].append(copy)

    for copy in copies:
        copy.wait()

    def experts(rows):
        n = rows.shape[0]
        main = jnp.dot(rows, wgu[0 : 3 * QUART, :], preferred_element_type=F32)
        r = iota((n, 256), 0) & 15
        tail = None
        for j in (2, 1, 0):
            part = jnp.dot(
                rows[:, j * QUART : (j + 1) * QUART],
                wgu[3 * QUART : 4 * QUART, :],
                preferred_element_type=F32,
            )
            part = pltpu.roll(part, n - 12 + 4 * j, 0)
            tail = part if tail is None else jnp.where(r < 4 * (j + 1), part, tail)
        both = main + tail
        gate_out, up_out = both[:, 0:128], both[:, 128:256]
        act = gate_out / (1.0 + jnp.exp(-gate_out)) * up_out
        r = iota((n, 128), 0) & 15
        act = jnp.where(r < 12, act, 0.0).astype(BF16).astype(F32)
        results = []
        for j in range(3):
            late = jnp.where(r >= 12, pltpu.roll(act, 12 - 4 * j, 0), 0.0)
            left = jnp.concatenate([act, late], axis=1).astype(BF16)
            results.append(jnp.dot(left, wdx[j], preferred_element_type=F32).astype(BF16))
        return results

    back = []
    across_x = []
    across_p = []

    def send_back(cls):
        across_p[cls].wait_recv()
        pp[cls, core] = (pp[cls, core].astype(F32) + qb[cls].astype(F32)).astype(BF16)
        for cols, dz, dx, sem in routes(cls):
            copy = remote(
                pp.at[cls, core, dx, :, cols],
                rtn.at[expert, :, cols],
                BACK + sem,
                at(dz=-dz, dx=-dx),
            )
            copy.start()
            back.append(copy)

    for cls in range(4):
        for copy in sent[cls]:
            copy.wait_recv()
        if cls == 0:
            own_block.wait()
        blocks = rb.at[cls, core]
        copy = remote(blocks, blocks, SIB_X + cls, at(flip=True))
        copy.start()
        across_x.append(copy)
        if cls > 0:
            send_back(cls - 1)
        copy.wait_recv()
        for j, part in enumerate(experts(rb[cls].reshape(128, 3 * QUART))):
            pp[cls, :, :, :, j * QUART : (j + 1) * QUART] = part.reshape(2, 4, 16, QUART)
        copy = remote(pp.at[cls, 1 - core], qb.at[cls], SIB_P + cls, at(flip=True))
        copy.start()
        across_p.append(copy)
    send_back(3)
    own_back = pltpu.make_async_copy(pp.at[0, core, 0], rtn.at[expert], local.at[25])
    own_back.start()

    for cls in range(4):
        for copy in sent[cls]:
            copy.wait_send()
        across_x[cls].wait_send()
        across_p[cls].wait_send()
    own_back.wait()
    for copy in back:
        copy.wait()

    lanes = iota((256, 128), 1)
    for k in range(3):
        tok, _ = item_of(iota((256, 128), 0), k)
        row_slots = jnp.sum(jnp.where(lanes == tok, slot_lane, 0.0), axis=1, keepdims=True)
        _, eighth_row = item_of(iota((256, 256), 0), k)
        total = jnp.zeros((256, PART), F32)
        for j in range(3):
            for half in range(2):
                if k not in thirds_for(j, half):
                    continue
                target, eighth_lane = slot_of(iota((256, 256), 1), j, half)
                pick = (row_slots == target.astype(F32)) & (eighth_lane == eighth_row)
                pick = jnp.where(pick, 1.0, 0.0).astype(BF16)
                start = j * QUART + half * PART
                source = rtn[:, :, start : start + PART].reshape(256, PART)
                total = total + jnp.dot(pick, source, preferred_element_type=F32)
        rsb[:, :, k * PART : (k + 1) * PART] = total.astype(BF16).reshape(16, 16, PART)

    far[3] = ship_three(rsb, f3, Y_RS)
    far[4] = ship_four(rsb, f4, Y_RS)
    ship_near(rsb, rsi, Y_RS)
    rsi[0] = rsb[pair_of(0)]
    for side in (0, 1):
        far[3][side].wait_recv()
        for a in (1 - side, side):
            position = zh if a == 0 else 1 - zh
            total = rsb[block_of(2 - 4 * side, a)].astype(F32) + f3[side, position].astype(F32)
            if a == side:
                far[4][side].wait_recv()
                total = total + f4[side].astype(F32)
            fm[side, a] = total.astype(BF16)
            ship(
                fm.at[side, a], rsi.at[3 + side, position], Y_RS + 6 + 2 * side + a, 2 - 4 * side
            )
    for copy in scatters:
        copy.wait_send()
    for copy in scatters:
        if not any(copy is other for other in far[3] + far[4]):
            copy.wait_recv()

    def add_up(block):
        total = rsi[0, block].astype(F32)
        for i in range(1, 5):
            total = total + rsi[i, block].astype(F32)
        return total

    zo2[...] = add_up(1 - zh).astype(BF16)
    across = remote(zo2, zi2, Y_RS + 10, at(dz=4))
    across.start()
    xf[...] = add_up(zh)
    across.wait()
    xf[...] = xf[...] + zi2[...].astype(F32)
    for (pr, pc), (wr, wc), n in pieces():
        xrow[wr : wr + n, wc : wc + PART] = xf[pr : pr + n, pc : pc + PART]
    out_ref[0] = (hid[0:TOK, :] + xrow[0:TOK, :]).astype(BF16)


def body(
    queries,
    new_kv,
    cached_key_value,
    cache_len,
    residual,
    norm_gain,
    route_logit,
    route_id,
    w_gate,
    w_up,
    w_down,
):
    vmem = pl.BlockSpec(memory_space=pltpu.VMEM)
    smem = pl.BlockSpec(memory_space=pltpu.SMEM)
    hbm = pl.BlockSpec(memory_space=pl.ANY)
    block = (GROUPS, 32, HEAD)
    slots = (16, 16, 3 * QUART)
    return pl.pallas_call(
        kernel,
        out_shape=jax.ShapeDtypeStruct((1, TOK, WIDTH), BF16),
        in_specs=[vmem, vmem, hbm, smem, vmem, vmem, vmem, vmem, hbm, hbm, hbm],
        out_specs=vmem,
        scratch_shapes=[
            pltpu.VMEM(block, F32),
            pltpu.VMEM((16,) + block, BF16),
            pltpu.VMEM((16,) + block, BF16),
            pltpu.VMEM((NY, 2) + block, BF16),
            pltpu.VMEM(block, BF16),
            pltpu.VMEM(block, BF16),
            pltpu.VMEM(block, BF16),
            pltpu.VMEM((2, 2) + block, BF16),
            pltpu.VMEM((2,) + block, BF16),
            pltpu.VMEM((2, 2) + block, BF16),
            pltpu.VMEM(block, F32),
            pltpu.VMEM((8, WIDTH), F32),
            pltpu.VMEM((8, WIDTH), F32),
            pltpu.VMEM((16, 3 * PART), F32),
            pltpu.VMEM((16, 16, 3 * PART), BF16),
            pltpu.VMEM(slots, BF16),
            pltpu.VMEM((4, 2, 4, 16, 3 * QUART), BF16),
            pltpu.VMEM((4, 2, 4, 16, 3 * QUART), BF16),
            pltpu.VMEM((4, 4, 16, 3 * QUART), BF16),
            pltpu.VMEM(slots, BF16),
            pltpu.VMEM((16, 16, 3 * PART), BF16),
            pltpu.VMEM((5, 2, 16, 3 * PART), BF16),
            pltpu.VMEM((2, 2, 16, 3 * PART), BF16),
            pltpu.VMEM((2, 16, 3 * PART), BF16),
            pltpu.VMEM((2, 2, 16, 3 * PART), BF16),
            pltpu.VMEM((16, 3 * PART), BF16),
            pltpu.VMEM((16, 3 * PART), BF16),
            pltpu.VMEM((WIDTH, 256), BF16),
            pltpu.VMEM((3, 256, QUART), BF16),
            pltpu.VMEM((GROUPS, KEYS, HEAD), BF16),
            pltpu.VMEM((GROUPS, KEYS, 2 * HEAD), BF16),
            pltpu.VMEM((2, 16, GROUPS * HEAD), F32),
            pltpu.VMEM((128, KEYS), F32),
            pltpu.SemaphoreType.DMA((N_SEM,)),
            pltpu.SemaphoreType.DMA((N_SEM,)),
            pltpu.SemaphoreType.DMA((26,)),
        ],
        compiler_params=pltpu.CompilerParams(
            collective_id=0, has_side_effects=True, vmem_limit_bytes=56 * 1024 * 1024
        ),
    )(
        queries,
        jnp.transpose(new_kv, (1, 2, 0, 3)),
        cached_key_value,
        cache_len,
        residual,
        norm_gain,
        route_logit,
        jnp.transpose(route_id, (0, 2, 1)),
        w_gate,
        w_up,
        w_down,
    )


def solution(mesh):
    placed = (
        P("ep", "ctx", None),
        P(None, "ep", "ctx", None),
        P(None, "ep", "ctx", None),
        P("ep"),
        P("ep", "ctx", None),
        P(),
        P("ep", "ctx"),
        P("ep", None, None),
        P("ep", None, "ctx"),
        P("ep", None, "ctx"),
        P("ep", "ctx", None),
    )
    return jax.shard_map(
        body, mesh=mesh, in_specs=placed, out_specs=P("ep", "ctx", None), check_vma=False
    )
```

```python
import jax
import jax.numpy as jnp
from jax import lax
from jax.experimental import pallas as pl
from jax.experimental.pallas import tpu as pltpu
from jax.sharding import PartitionSpec as P

MESH = pl.DeviceIdType.MESH
BF16 = jnp.bfloat16
F32 = jnp.float32

GROUPS = 8
PER_GROUP = 5
HEAD = 128
TOK = 6
WIDTH = 5120
CACHE = 256
KEYS = 384
NY = 8
PART = 640
QUART = 1280
NEG = -1e30
FLOOR = -1e29

Q_AG = 0
Z_RES = 18
Q_RS = 20
Q_Z = 30
X_AG = 32
GO = 48
GO_Y = 57
SIB_X = 63
SIB_P = 67
BACK_Y = 71
BACK = 77
Y_RS = 86
Y_Z = 96
N_SEM = 97
CLASSES = (0, 1, -1, 2)


def iota(shape, dim):
    return lax.broadcasted_iota(jnp.int32, shape, dim)


def item_of(index, third):
    rho = index & 15
    late = rho - 12 + 4 * third
    tok = jnp.where(rho < 6, rho, jnp.where(rho < 12, rho - 6, jnp.where(late < 6, late, late - 6)))
    eighth = jnp.where(
        rho < 6, 2 * third, jnp.where(rho < 12, 2 * third + 1, jnp.where(late < 6, 6, 7))
    )
    return (index >> 4) * TOK + tok, eighth


def slot_of(index, third, half):
    rho = index & 15
    slot = jnp.where(rho < 12, rho, rho - 12 + 4 * third)
    eighth = jnp.where(rho < 12, 2 * third + half, 6 + half)
    return (index >> 4) * 16 + slot, eighth


def thirds_for(third, half):
    return sorted({third, half, half + 1})


def kernel(
    q_ref,
    new_ref,
    cache_ref,
    len_ref,
    res_ref,
    gain_ref,
    logit_ref,
    rid_ref,
    wg_ref,
    wu_ref,
    wd_ref,
    out_ref,
    qf,
    qg,
    pw,
    rin,
    za,
    zi,
    r3,
    r4,
    mg,
    attf,
    rown,
    rfar,
    lown,
    lfar,
    hid,
    hid2,
    xrow,
    xf,
    xg,
    sb,
    rb,
    pp,
    qb,
    yq,
    rtn,
    rsb,
    rsi,
    f3,
    f4,
    fm,
    zo2,
    zi2,
    wgu,
    wdx,
    kx,
    vx,
    newf,
    bias,
    send,
    recv,
    local,
):
    ctx = lax.axis_index("ctx")
    ep = lax.axis_index("ep")
    y, zh = lax.div(ctx, 2), lax.rem(ctx, 2)
    zl, x, core = lax.div(ep, 8), lax.rem(lax.div(ep, 2), 4), lax.rem(ep, 2)
    z = zh * 4 + zl
    expert = zl * 4 + x

    def at(dy=0, dz=0, dx=0, flip=False):
        ny = lax.rem(y + dy + NY, NY)
        nz = lax.rem(z + dz + 8, 8)
        nx = lax.rem(x + dx + 4, 4)
        nc = 1 - core if flip else core
        return (ny * 2 + lax.div(nz, 4), lax.rem(nz, 4) * 8 + nx * 2 + nc)

    def remote(src, dst, sem, device):
        return pltpu.make_async_remote_copy(
            src_ref=src,
            dst_ref=dst,
            send_sem=send.at[sem],
            recv_sem=recv.at[sem],
            device_id=device,
            device_id_type=MESH,
        )

    copies = [
        pltpu.make_async_copy(wg_ref.at[0], wgu.at[:, 0:128], local.at[0]),
        pltpu.make_async_copy(wu_ref.at[0], wgu.at[:, 128:256], local.at[1]),
    ]
    for j in range(3):
        copies.append(
            pltpu.make_async_copy(
                wd_ref.at[0, :, j * QUART : (j + 1) * QUART], wdx.at[j, 0:128], local.at[2 + 2 * j]
            )
        )
        copies.append(
            pltpu.make_async_copy(
                wd_ref.at[0, :, 3 * QUART : 4 * QUART], wdx.at[j, 128:256], local.at[3 + 2 * j]
            )
        )
    cache_copies = []
    for g in range(GROUPS):
        cols = slice(g * HEAD, (g + 1) * HEAD)
        cache_copies.append(
            pltpu.make_async_copy(
                cache_ref.at[0, 0, :, cols], kx.at[g, 0:CACHE], local.at[8 + 2 * g]
            )
        )
        cache_copies.append(
            pltpu.make_async_copy(
                cache_ref.at[1, 0, :, cols], vx.at[g, 0:CACHE, 0:HEAD], local.at[9 + 2 * g]
            )
        )
    for copy in cache_copies + copies:
        copy.start()

    barrier = pltpu.get_barrier_semaphore()
    partners = [at(dy=d) for d in (1, -1, 2, -2)] + [at(dz=4), at(dy=4, dz=4), at(flip=True)]
    for dz in (0, 1, -1, 2, -2):
        partners += [at(dz=dz, dx=dx) for dx in range(4) if (dz, dx) != (0, 0)]
    for device in partners:
        pl.semaphore_signal(barrier, inc=1, device_id=device, device_id_type=MESH)

    qf[...] = jnp.zeros_like(qf)
    queries = q_ref[0].astype(F32)
    for g in range(GROUPS):
        for j in range(PER_GROUP):
            h = g * PER_GROUP + j
            qf[g, j * TOK : (j + 1) * TOK, :] = queries[:, h * HEAD : (h + 1) * HEAD]
    qg[ctx] = qf[...].astype(BF16)

    pl.semaphore_wait(barrier, len(partners))

    def block_of(dy, a):
        return lax.rem(y + dy + NY, NY) * 2 + (zh if a == 0 else 1 - zh)

    class Ring:
        def __init__(self, buf, base):
            self.buf, self.base, self.copies = buf, base, {}

        def copy(self, way, d, a):
            if (way, d, a) not in self.copies:
                sign = 1 if way == 0 else -1
                block = self.buf.at[block_of(-sign * (d - 1), a)]
                sem = self.base + (way * 4 + d - 1) * 2 + a
                self.copies[way, d, a] = remote(block, block, sem, at(dy=sign))
            return self.copies[way, d, a]

        def go(self, d, a, ways=(0, 1)):
            for way in ways:
                self.copy(way, d, a).start()

        def got(self, d, a, ways=(0, 1)):
            for way in ways:
                self.copy(way, d, a).wait_recv()

        def pass_on(self, d, a, ways=(0, 1)):
            for way in ways:
                self.copy(way, d, a).wait_recv()
                self.copy(way, d + 1, a).start()

        def end(self):
            for copy in self.copies.values():
                copy.wait_send()

    own = qg.at[ctx]
    ring = Ring(qg, Q_AG + 2)
    ring.go(1, 0)
    near = remote(own, own, Q_AG, at(dz=4))
    near.start()
    opposite = remote(own, own, Q_AG + 1, at(dy=4, dz=4))
    opposite.start()

    def pieces():
        for e in range(6):
            yield (e % 2 * 6, e // 2 * PART), (0, e * PART), 6
        yield (12, 0), (0, 6 * PART), 4
        yield (12, PART), (4, 6 * PART), 2
        yield (14, PART), (0, 7 * PART), 2
        yield (12, 2 * PART), (2, 7 * PART), 4

    def pack():
        for (pr, pc), (wr, wc), n in pieces():
            xf[pr : pr + n, pc : pc + PART] = xrow[wr : wr + n, wc : wc + PART]

    def unpack():
        for (pr, pc), (wr, wc), n in pieces():
            xrow[wr : wr + n, wc : wc + PART] = xf[pr : pr + n, pc : pc + PART]

    xrow[0:TOK, :] = res_ref[0].astype(F32)
    pack()
    rown[...] = xf[...].astype(BF16)
    lown[...] = jnp.zeros_like(lown)
    lown[0:1, 0:TOK] = logit_ref[...]
    res_copy = remote(rown, rfar, Z_RES, at(dz=4))
    res_copy.start()
    logit_copy = remote(lown, lfar, Z_RES + 1, at(dz=4))
    logit_copy.start()
    rtn[...] = jnp.zeros_like(rtn)

    newf[...] = jnp.zeros_like(newf)
    fresh = new_ref[0].astype(F32)
    newf[0, 0:TOK, :] = fresh[:, 0, :]
    newf[1, 0:TOK, :] = fresh[:, 1, :]
    for g in range(GROUPS):
        cols = slice(g * HEAD, (g + 1) * HEAD)
        kx[g, CACHE : CACHE + 16, :] = newf[0, :, cols].astype(BF16)
        vx[g, CACHE : CACHE + 16, 0:HEAD] = newf[1, :, cols].astype(BF16)
        kx[g, CACHE + 16 : KEYS, :] = jnp.zeros((KEYS - CACHE - 16, HEAD), BF16)
        vx[g, CACHE + 16 : KEYS, 0:HEAD] = jnp.zeros((KEYS - CACHE - 16, HEAD), BF16)
        vx[g, :, HEAD : 2 * HEAD] = jnp.ones((KEYS, HEAD), BF16)

    ids = jnp.sum(
        jnp.where(iota((96, 96), 0) == iota((96, 96), 1), rid_ref[0], 0), axis=1, keepdims=True
    )
    one_hot = (ids == iota((96, 128), 1)).astype(F32)
    before = (iota((96, 96), 1) < iota((96, 96), 0)).astype(BF16)
    counts = jnp.dot(before, one_hot.astype(BF16), preferred_element_type=F32)
    rank = jnp.sum(counts * one_hot, axis=1, keepdims=True)
    slot_col = ids.astype(F32) * 16.0 + rank
    slot_lane = jnp.sum(
        jnp.where(iota((96, 128), 0) == iota((96, 128), 1), slot_col, 0.0), axis=0, keepdims=True
    )

    for copy in cache_copies:
        copy.wait()

    limit = jnp.minimum(len_ref[0] - ctx * CACHE, CACHE)
    scale = HEAD ** (-0.5)

    def attend(blocks):
        count = len(blocks)
        rows = 32 * count
        row = iota((rows, KEYS), 0)
        lane = iota((rows, KEYS), 1)
        r = row & 31
        tok = r
        for edge in (6, 12, 18, 24):
            tok = tok - jnp.where(r >= edge, 6, 0)
        for i, block in enumerate(blocks):
            tok = tok + jnp.where((row >> 5) == i, block * TOK, 0)
        new_ok = (lane >= CACHE) & (lane < CACHE + TOK) & (ctx * TOK + lane - CACHE <= tok)
        bias[0:rows, :] = jnp.where((lane < limit) | new_ok, 0.0, NEG)

        def group(g, carry):
            q = jnp.concatenate([qg[block, g] for block in blocks], axis=0)
            scores = lax.dot_general(
                q, kx[g], (((1,), (1,)), ((), ())), preferred_element_type=F32
            )
            scores = scores * scale + bias[0:rows, :]
            top = jnp.maximum(jnp.max(scores, axis=1, keepdims=True), FLOOR)
            top = top.astype(BF16).astype(F32)
            weights = jnp.exp(scores - top).astype(BF16)
            sums = jnp.dot(weights, vx[g], preferred_element_type=F32)
            shape = (count, 32, HEAD)
            weighted = sums[:, 0:HEAD].reshape(shape)
            total = sums[:, HEAD : 2 * HEAD].reshape(shape)
            tops = jnp.broadcast_to(top, (rows, HEAD)).reshape(shape)
            on = (iota(shape, 2) & 31) == iota(shape, 1)
            top_row = jnp.sum(jnp.where(on, tops, 0.0), axis=1, keepdims=True)
            total_row = jnp.sum(jnp.where(on, total, 0.0), axis=1, keepdims=True)
            at_row = iota(shape, 1)
            packed = jnp.where(
                at_row == 30, top_row, jnp.where(at_row == 31, total_row, weighted)
            ).astype(BF16)
            for i, block in enumerate(blocks):
                pw[block, g] = packed[i]
            return carry

        lax.fori_loop(0, GROUPS, group, 0, unroll=2)

    scatters = []

    def pair_of(dy):
        return pl.ds(lax.rem(y + dy + NY, NY) * 2, 2)

    def ship(src, dst, sem, d):
        copy = remote(src, dst, sem, at(dy=d))
        copy.start()
        scatters.append(copy)
        return copy

    def ship_near(src, dst, base):
        ship(src.at[pair_of(1)], dst.at[1], base, 1)
        ship(src.at[pair_of(-1)], dst.at[2], base + 1, -1)

    def ship_three(src, dst, base):
        up = ship(src.at[pair_of(3)], dst.at[0], base + 2, 1)
        down = ship(src.at[pair_of(-3)], dst.at[1], base + 3, -1)
        return up, down

    def ship_four(src, dst, base):
        up = ship(src.at[block_of(4, 0)], dst.at[0], base + 4, 2)
        down = ship(src.at[block_of(4, 1)], dst.at[1], base + 5, -2)
        return up, down

    far = {}

    empty_row = iota((3, 32, HEAD), 1)
    empty = jnp.where(empty_row == 30, FLOOR, 0.0).astype(BF16)

    def settle_rin(g, carry):
        for i in range(3):
            for a in range(2):
                rin[5 + i, a, g] = empty[i]
        return carry

    lax.fori_loop(0, GROUPS, settle_rin, 0)
    def both(d):
        return [block_of(d, 0), block_of(d, 1)]

    ring.pass_on(1, 0)
    near.wait_recv()
    ring.go(1, 1)
    ring.pass_on(2, 0)
    ring.pass_on(1, 1)
    opposite.wait_recv()
    beyond = []
    for way, sign in ((0, 1), (1, -1)):
        block = qg.at[block_of(4, 1)]
        copy = remote(block, block, Q_AG + 2 + (way * 4 + 2) * 2 + 1, at(dy=sign))
        copy.start()
        beyond.append(copy)
    attend(both(0) + both(-1) + both(1))
    rin[0] = pw[pair_of(0)]
    ship_near(pw, rin, Q_RS)
    ring.pass_on(3, 0, (0,))
    ring.got(3, 0, (1,))
    ring.got(2, 1)
    attend(both(-2) + both(2))
    for copy in beyond:
        copy.wait_recv()
    ring.got(4, 0, (0,))
    attend(both(-3) + both(3) + both(4))
    far[3] = ship_three(pw, r3, Q_RS)
    far[4] = ship_four(pw, r4, Q_RS)
    ring.end()
    for copy in beyond + [near, opposite, res_copy, logit_copy]:
        copy.wait_send()

    def merge(stack, count, normalize):
        wide = stack.astype(F32)
        tops = wide[:, 30, :]
        totals = wide[:, 31, :]
        top = jnp.max(tops, axis=0, keepdims=True)
        factor = jnp.exp(tops - top)
        total = jnp.sum(factor * totals, axis=0, keepdims=True)
        if normalize:
            factor = factor / total
        lane = iota((32, 128), 1)
        row = iota((32, 128), 0)
        on = ((lane & 31) == row) & (row < 30)
        merged = jnp.zeros((32, HEAD), F32)
        for part in range(count // 4):
            spread = jnp.zeros((32, 128), F32)
            for i in range(4):
                spread = jnp.where((lane >> 5) == i, factor[4 * part + i : 4 * part + i + 1], spread)
            spread = jnp.where(on, spread, 0.0)
            high = spread.astype(BF16)
            low = (spread - high.astype(F32)).astype(BF16)
            rows = stack[4 * part : 4 * part + 4].reshape(128, HEAD)
            merged = merged + jnp.dot(high, rows, preferred_element_type=F32)
            merged = merged + jnp.dot(low, rows, preferred_element_type=F32)
        return merged, top, total

    def merged_block(stack, count):
        merged, top, total = merge(stack, count, False)
        at_row = iota((32, HEAD), 0)
        return jnp.where(at_row == 30, top, jnp.where(at_row == 31, total, merged)).astype(BF16)

    for side in (0, 1):
        far[3][side].wait_recv()
        for a in (1 - side, side):
            if a == side:
                far[4][side].wait_recv()

            def group(g, carry, side=side, a=a):
                position = zh if a == 0 else 1 - zh
                own = pw[block_of(2 - 4 * side, a), g]
                third = r3[side, position, g]
                fourth = r4[side, g] if a == side else empty[0]
                stack = jnp.concatenate([own[None], third[None], fourth[None], empty[0:1]], axis=0)
                mg[side, a, g] = merged_block(stack, 4)
                return carry

            lax.fori_loop(0, GROUPS, group, 0)
            position = zh if a == 0 else 1 - zh
            ship(
                mg.at[side, a], rin.at[3 + side, position], Q_RS + 6 + 2 * side + a, 2 - 4 * side
            )
    for copy in scatters:
        copy.wait_send()
    for copy in scatters:
        if not any(copy is other for other in far[3] + far[4]):
            copy.wait_recv()
    scatters.clear()

    def merge_y(block):
        def group(g, carry):
            za[block, g] = merged_block(rin[:, block, g], NY)
            return carry

        lax.fori_loop(0, GROUPS, group, 0, unroll=2)

    across = []
    for a in (1, 0):
        position = zh if a == 0 else 1 - zh
        merge_y(position)
        copy = remote(za.at[position], zi.at[position], Q_Z + a, at(dz=4))
        copy.start()
        across.append(copy)

    def norm(position, logits, state_ref):
        def group(g, carry):
            stack = jnp.concatenate([za[position, g][None], zi[position, g][None], empty[0:2]], axis=0)
            merged, _, _ = merge(stack, 4, True)
            attf[g] = merged
            return carry

        lax.fori_loop(0, GROUPS, group, 0, unroll=2)
        for g in range(GROUPS):
            for j in range(PER_GROUP):
                h = g * PER_GROUP + j
                cols = slice(h * HEAD, (h + 1) * HEAD)
                state = xrow[0:TOK, cols] + attf[g, j * TOK : (j + 1) * TOK, :]
                state_ref[0:TOK, cols] = state.astype(BF16).astype(F32)
        state = state_ref[0:TOK, :]
        inv_rms = lax.rsqrt(jnp.mean(state * state, axis=1, keepdims=True) + 1e-05)
        logit = jnp.broadcast_to(logits, (TOK, 128))
        logit = jnp.sum(
            jnp.where(iota((TOK, 128), 0) == iota((TOK, 128), 1), logit, 0.0), axis=1, keepdims=True
        )
        gate = 1.0 / (1.0 + jnp.exp(-logit))
        xrow[0:TOK, :] = state * inv_rms * gain_ref[...].reshape(1, WIDTH).astype(F32) * gate
        pack()
        xg[y * 2 + position] = xf[...].astype(BF16)

    ring = Ring(xg, X_AG)
    xrow[0:TOK, :] = res_ref[0].astype(F32)
    across[0].wait_recv()
    norm(zh, lown[0:1, :], hid)
    ring.go(1, 0)
    res_copy.wait_recv()
    logit_copy.wait_recv()
    xf[...] = rfar[...].astype(F32)
    unpack()
    across[1].wait_recv()
    norm(1 - zh, lfar[0:1, :], hid2)
    ring.go(1, 1)
    for d in (1, 2):
        ring.pass_on(d, 0)
        ring.pass_on(d, 1)
    ring.pass_on(3, 0, (0,))
    ring.pass_on(3, 1, (1,))
    ring.got(3, 0, (1,))
    ring.got(3, 1, (0,))
    ring.got(4, 0, (0,))
    ring.got(4, 1, (1,))
    ring.end()
    for copy in across:
        copy.wait_send()

    rows_in = [xg[:, :, k * PART : (k + 1) * PART].reshape(256, PART) for k in range(3)]
    lanes = iota((96, 256), 1)
    lane_slots = []
    for k in range(3):
        tok, _ = item_of(lanes, k)
        lane_slots.append(
            jnp.sum(jnp.where(iota((96, 256), 0) == tok, slot_col, 0.0), axis=0, keepdims=True)
        )
    for j in range(3):
        for half in range(2):
            target, eighth_row = slot_of(iota((256, 256), 0), j, half)
            target = target.astype(F32)
            total = jnp.zeros((256, PART), F32)
            for k in thirds_for(j, half):
                _, eighth_lane = item_of(iota((256, 256), 1), k)
                pick = (lane_slots[k] == target) & (eighth_lane == eighth_row)
                pick = jnp.where(pick, 1.0, 0.0).astype(BF16)
                total = total + jnp.dot(pick, rows_in[k], preferred_element_type=F32)
            start = j * QUART + half * PART
            sb[:, :, start : start + PART] = total.astype(BF16).reshape(16, 16, PART)

    own_block = pltpu.make_async_copy(sb.at[expert], rb.at[0, core, 0], local.at[24])
    own_block.start()

    def parity(cls):
        return lax.rem(y + cls, 2)

    def routes(cls):
        if cls == 0:
            for dx in (1, 2, 3):
                yield 0, dx, dx - 1
        else:
            for i in (0, 1):
                dz = CLASSES[cls] if cls < 3 else 2 - 4 * i
                yield dz, 2 * i + parity(cls), 1 + 2 * cls + i

    sent = [[], [], [], []]
    for cls in (1, 2, 0, 3):
        for dz, dx, index in routes(cls):
            to = lax.rem(zl + dz + 4, 4) * 4 + lax.rem(x + dx, 4)
            copy = remote(sb.at[to], rb.at[cls, core, dx], GO + index, at(dz=dz, dx=dx))
            copy.start()
            sent[cls].append(copy)

    for copy in copies:
        copy.wait()

    def experts(rows):
        n = rows.shape[0]
        main = jnp.dot(rows, wgu[0 : 3 * QUART, :], preferred_element_type=F32)
        r = iota((n, 256), 0) & 15
        tail = None
        for j in (2, 1, 0):
            part = jnp.dot(
                rows[:, j * QUART : (j + 1) * QUART],
                wgu[3 * QUART : 4 * QUART, :],
                preferred_element_type=F32,
            )
            part = pltpu.roll(part, n - 12 + 4 * j, 0)
            tail = part if tail is None else jnp.where(r < 4 * (j + 1), part, tail)
        both = main + tail
        gate_out, up_out = both[:, 0:128], both[:, 128:256]
        act = gate_out / (1.0 + jnp.exp(-gate_out)) * up_out
        r = iota((n, 128), 0) & 15
        act = jnp.where(r < 12, act, 0.0).astype(BF16).astype(F32)
        results = []
        for j in range(3):
            late = jnp.where(r >= 12, pltpu.roll(act, 12 - 4 * j, 0), 0.0)
            left = jnp.concatenate([act, late], axis=1).astype(BF16)
            results.append(jnp.dot(left, wdx[j], preferred_element_type=F32).astype(BF16))
        return results

    back = []
    swaps = {}
    across_x = {}
    across_p = {}
    partial = {}

    def swap(cls):
        swaps[cls] = []
        for i, copy in enumerate(sent[cls]):
            copy.wait_recv()
            block = rb.at[cls, core, 2 * i + parity(cls)]
            onward = remote(block, block, GO_Y + 2 * (cls - 1) + i, at(dy=1 - 2 * i))
            onward.start()
            swaps[cls].append(onward)

    def share(cls):
        if cls == 0:
            for copy in sent[0]:
                copy.wait_recv()
            own_block.wait()
        else:
            for copy in swaps[cls]:
                copy.wait_recv()
        blocks = rb.at[cls, core]
        across_x[cls] = remote(blocks, blocks, SIB_X + cls, at(flip=True))
        across_x[cls].start()

    def run(cls):
        across_x[cls].wait_recv()
        for j, part in enumerate(experts(rb[cls].reshape(128, 3 * QUART))):
            pp[cls, :, :, :, j * QUART : (j + 1) * QUART] = part.reshape(2, 4, 16, QUART)
        across_p[cls] = remote(pp.at[cls, 1 - core], qb.at[cls], SIB_P + cls, at(flip=True))
        across_p[cls].start()

    def send_back(cls):
        for dz, dx, index in routes(cls):
            copy = remote(pp.at[cls, core, dx], rtn.at[expert], BACK + index, at(dz=-dz, dx=-dx))
            copy.start()
            back.append(copy)

    def add_cores(cls):
        across_p[cls].wait_recv()
        pp[cls, core] = (pp[cls, core].astype(F32) + qb[cls].astype(F32)).astype(BF16)
        if cls == 0:
            send_back(0)
            rtn[expert] = pp[0, core, 0]
            return
        partial[cls] = []
        for i in (0, 1):
            block = pp.at[cls, core, 2 * i + 1 - parity(cls)]
            copy = remote(
                block, yq.at[cls - 1, i], BACK_Y + 2 * (cls - 1) + i, at(dy=2 * i - 1)
            )
            copy.start()
            partial[cls].append(copy)

    def add_planes(cls):
        for i in (0, 1):
            partial[cls][i].wait_recv()
            dx = 2 * i + parity(cls)
            total = pp[cls, core, dx].astype(F32) + yq[cls - 1, i].astype(F32)
            pp[cls, core, dx] = total.astype(BF16)
        send_back(cls)

    swap(1)
    swap(2)
    share(0)
    run(0)
    share(1)
    swap(3)
    run(1)
    add_cores(0)
    share(2)
    run(2)
    add_cores(1)
    share(3)
    run(3)
    add_planes(1)
    add_cores(2)
    add_planes(2)
    add_cores(3)
    add_planes(3)

    for cls in range(4):
        for copy in sent[cls] + swaps.get(cls, []) + partial.get(cls, []):
            copy.wait_send()
        across_x[cls].wait_send()
        across_p[cls].wait_send()
    for copy in back:
        copy.wait()

    lanes = iota((256, 128), 1)
    for k in range(3):
        tok, _ = item_of(iota((256, 128), 0), k)
        row_slots = jnp.sum(jnp.where(lanes == tok, slot_lane, 0.0), axis=1, keepdims=True)
        _, eighth_row = item_of(iota((256, 256), 0), k)
        total = jnp.zeros((256, PART), F32)
        for j in range(3):
            for half in range(2):
                if k not in thirds_for(j, half):
                    continue
                target, eighth_lane = slot_of(iota((256, 256), 1), j, half)
                pick = (row_slots == target.astype(F32)) & (eighth_lane == eighth_row)
                pick = jnp.where(pick, 1.0, 0.0).astype(BF16)
                start = j * QUART + half * PART
                source = rtn[:, :, start : start + PART].reshape(256, PART)
                total = total + jnp.dot(pick, source, preferred_element_type=F32)
        rsb[:, :, k * PART : (k + 1) * PART] = total.astype(BF16).reshape(16, 16, PART)

    far[3] = ship_three(rsb, f3, Y_RS)
    far[4] = ship_four(rsb, f4, Y_RS)
    ship_near(rsb, rsi, Y_RS)
    rsi[0] = rsb[pair_of(0)]
    for side in (0, 1):
        far[3][side].wait_recv()
        for a in (1 - side, side):
            position = zh if a == 0 else 1 - zh
            total = rsb[block_of(2 - 4 * side, a)].astype(F32) + f3[side, position].astype(F32)
            if a == side:
                far[4][side].wait_recv()
                total = total + f4[side].astype(F32)
            fm[side, a] = total.astype(BF16)
            ship(
                fm.at[side, a], rsi.at[3 + side, position], Y_RS + 6 + 2 * side + a, 2 - 4 * side
            )
    for copy in scatters:
        copy.wait_send()
    for copy in scatters:
        if not any(copy is other for other in far[3] + far[4]):
            copy.wait_recv()

    def add_up(block):
        total = rsi[0, block].astype(F32)
        for i in range(1, 5):
            total = total + rsi[i, block].astype(F32)
        return total

    zo2[...] = add_up(1 - zh).astype(BF16)
    across = remote(zo2, zi2, Y_Z, at(dz=4))
    across.start()
    xf[...] = add_up(zh)
    across.wait()
    xf[...] = xf[...] + zi2[...].astype(F32)
    unpack()
    out_ref[0] = (hid[0:TOK, :] + xrow[0:TOK, :]).astype(BF16)


def body(
    queries,
    new_kv,
    cached_key_value,
    cache_len,
    residual,
    norm_gain,
    route_logit,
    route_id,
    w_gate,
    w_up,
    w_down,
):
    vmem = pl.BlockSpec(memory_space=pltpu.VMEM)
    smem = pl.BlockSpec(memory_space=pltpu.SMEM)
    hbm = pl.BlockSpec(memory_space=pl.ANY)
    block = (GROUPS, 32, HEAD)
    slots = (16, 16, 3 * QUART)
    return pl.pallas_call(
        kernel,
        out_shape=jax.ShapeDtypeStruct((1, TOK, WIDTH), BF16),
        in_specs=[vmem, vmem, hbm, smem, vmem, vmem, vmem, vmem, hbm, hbm, hbm],
        out_specs=vmem,
        scratch_shapes=[
            pltpu.VMEM(block, F32),
            pltpu.VMEM((16,) + block, BF16),
            pltpu.VMEM((16,) + block, BF16),
            pltpu.VMEM((NY, 2) + block, BF16),
            pltpu.VMEM((2,) + block, BF16),
            pltpu.VMEM((2,) + block, BF16),
            pltpu.VMEM((2, 2) + block, BF16),
            pltpu.VMEM((2,) + block, BF16),
            pltpu.VMEM((2, 2) + block, BF16),
            pltpu.VMEM(block, F32),
            pltpu.VMEM((16, 3 * PART), BF16),
            pltpu.VMEM((16, 3 * PART), BF16),
            pltpu.VMEM((8, 128), F32),
            pltpu.VMEM((8, 128), F32),
            pltpu.VMEM((8, WIDTH), F32),
            pltpu.VMEM((8, WIDTH), F32),
            pltpu.VMEM((8, WIDTH), F32),
            pltpu.VMEM((16, 3 * PART), F32),
            pltpu.VMEM((16, 16, 3 * PART), BF16),
            pltpu.VMEM(slots, BF16),
            pltpu.VMEM((4, 2, 4, 16, 3 * QUART), BF16),
            pltpu.VMEM((4, 2, 4, 16, 3 * QUART), BF16),
            pltpu.VMEM((4, 4, 16, 3 * QUART), BF16),
            pltpu.VMEM((3, 2, 16, 3 * QUART), BF16),
            pltpu.VMEM(slots, BF16),
            pltpu.VMEM((16, 16, 3 * PART), BF16),
            pltpu.VMEM((5, 2, 16, 3 * PART), BF16),
            pltpu.VMEM((2, 2, 16, 3 * PART), BF16),
            pltpu.VMEM((2, 16, 3 * PART), BF16),
            pltpu.VMEM((2, 2, 16, 3 * PART), BF16),
            pltpu.VMEM((16, 3 * PART), BF16),
            pltpu.VMEM((16, 3 * PART), BF16),
            pltpu.VMEM((WIDTH, 256), BF16),
            pltpu.VMEM((3, 256, QUART), BF16),
            pltpu.VMEM((GROUPS, KEYS, HEAD), BF16),
            pltpu.VMEM((GROUPS, KEYS, 2 * HEAD), BF16),
            pltpu.VMEM((2, 16, GROUPS * HEAD), F32),
            pltpu.VMEM((192, KEYS), F32),
            pltpu.SemaphoreType.DMA((N_SEM,)),
            pltpu.SemaphoreType.DMA((N_SEM,)),
            pltpu.SemaphoreType.DMA((26,)),
        ],
        compiler_params=pltpu.CompilerParams(
            collective_id=0, has_side_effects=True, vmem_limit_bytes=56 * 1024 * 1024
        ),
    )(
        queries,
        jnp.transpose(new_kv, (1, 2, 0, 3)),
        cached_key_value,
        cache_len,
        residual,
        norm_gain,
        route_logit,
        jnp.transpose(route_id, (0, 2, 1)),
        w_gate,
        w_up,
        w_down,
    )


def solution(mesh):
    placed = (
        P("ep", "ctx", None),
        P(None, "ep", "ctx", None),
        P(None, "ep", "ctx", None),
        P("ep"),
        P("ep", "ctx", None),
        P(),
        P("ep", "ctx"),
        P("ep", None, None),
        P("ep", None, "ctx"),
        P("ep", None, "ctx"),
        P("ep", "ctx", None),
    )
    return jax.shard_map(
        body, mesh=mesh, in_specs=placed, out_specs=P("ep", "ctx", None), check_vma=False
    )
```

```python
import jax
import jax.numpy as jnp
from jax import lax
from jax.experimental import pallas as pl
from jax.experimental.pallas import tpu as pltpu
from jax.sharding import PartitionSpec as P

MESH = pl.DeviceIdType.MESH
BF16 = jnp.bfloat16
F32 = jnp.float32

GROUPS = 8
PER_GROUP = 5
HEAD = 128
TOK = 6
WIDTH = 5120
CACHE = 256
KEYS = 384
NY = 8
PART = 640
QUART = 1280
NEG = -1e30
FLOOR = -1e29

Q_AG = 0
Z_RES = 18
Q_RS = 20
Q_Z = 30
X_AG = 32
GO = 48
GO_Y = 57
WEIGHTS = 63
BACK_Y = 71
BACK = 77
Y_RS = 86
N_SEM = 119
CLASSES = (0, 1, -1, 2)


def iota(shape, dim):
    return lax.broadcasted_iota(jnp.int32, shape, dim)


def item_of(index, third):
    rho = index & 15
    late = rho - 12 + 4 * third
    tok = jnp.where(rho < 6, rho, jnp.where(rho < 12, rho - 6, jnp.where(late < 6, late, late - 6)))
    eighth = jnp.where(
        rho < 6, 2 * third, jnp.where(rho < 12, 2 * third + 1, jnp.where(late < 6, 6, 7))
    )
    return (index >> 4) * TOK + tok, eighth


def slot_of(index, third, half):
    rho = index & 15
    slot = jnp.where(rho < 12, rho, rho - 12 + 4 * third)
    eighth = jnp.where(rho < 12, 2 * third + half, 6 + half)
    return (index >> 4) * 16 + slot, eighth


def thirds_for(third, half):
    return sorted({third, half, half + 1})


def kernel(
    q_ref,
    new_ref,
    cache_ref,
    len_ref,
    res_ref,
    gain_ref,
    logit_ref,
    rid_ref,
    wg_ref,
    wu_ref,
    wd_ref,
    out_ref,
    qf,
    qg,
    pw,
    rin,
    za,
    zi,
    r3,
    r4,
    mg,
    attf,
    rown,
    rfar,
    lown,
    lfar,
    hid,
    hid2,
    xrow,
    xf,
    xg,
    sb,
    rb,
    pp,
    yq,
    rtn,
    rsb,
    rsi,
    f3,
    f4,
    fm,
    zo2,
    zi2,
    wgu,
    wdx,
    kx,
    vx,
    newf,
    bias,
    send,
    recv,
    local,
):
    ctx = lax.axis_index("ctx")
    ep = lax.axis_index("ep")
    y, zh = lax.div(ctx, 2), lax.rem(ctx, 2)
    zl, x, core = lax.div(ep, 8), lax.rem(lax.div(ep, 2), 4), lax.rem(ep, 2)
    z = zh * 4 + zl
    expert = zl * 4 + x

    def at(dy=0, dz=0, dx=0, flip=False):
        ny = lax.rem(y + dy + NY, NY)
        nz = lax.rem(z + dz + 8, 8)
        nx = lax.rem(x + dx + 4, 4)
        nc = 1 - core if flip else core
        return (ny * 2 + lax.div(nz, 4), lax.rem(nz, 4) * 8 + nx * 2 + nc)

    def remote(src, dst, sem, device):
        return pltpu.make_async_remote_copy(
            src_ref=src,
            dst_ref=dst,
            send_sem=send.at[sem],
            recv_sem=recv.at[sem],
            device_id=device,
            device_id_type=MESH,
        )

    def of_core(start):
        return pl.ds(pl.multiple_of(start + core * 128, 128), 128)

    parts = [
        (wg_ref.at[0], wgu.at[:, of_core(0)]),
        (wu_ref.at[0], wgu.at[:, of_core(256)]),
    ]
    for j in range(3):
        parts.append((wd_ref.at[0, :, j * QUART : (j + 1) * QUART], wdx.at[j, of_core(0)]))
        parts.append((wd_ref.at[0, :, 3 * QUART : 4 * QUART], wdx.at[j, of_core(256)]))
    copies = [
        pltpu.make_async_copy(src, dst, local.at[i]) for i, (src, dst) in enumerate(parts)
    ]
    cache_copies = []
    for g in range(GROUPS):
        cols = slice(g * HEAD, (g + 1) * HEAD)
        cache_copies.append(
            pltpu.make_async_copy(
                cache_ref.at[0, 0, :, cols], kx.at[g, 0:CACHE], local.at[8 + 2 * g]
            )
        )
        cache_copies.append(
            pltpu.make_async_copy(
                cache_ref.at[1, 0, :, cols], vx.at[g, 0:CACHE, 0:HEAD], local.at[9 + 2 * g]
            )
        )
    for copy in cache_copies + copies:
        copy.start()

    barrier = pltpu.get_barrier_semaphore()
    partners = [at(dy=d) for d in (1, -1, 2, -2)] + [at(dz=4), at(dy=4, dz=4), at(flip=True)]
    for dz in (0, 1, -1, 2, -2):
        partners += [at(dz=dz, dx=dx) for dx in range(4) if (dz, dx) != (0, 0)]
    for device in partners:
        pl.semaphore_signal(barrier, inc=1, device_id=device, device_id_type=MESH)

    qf[...] = jnp.zeros_like(qf)
    queries = q_ref[0].astype(F32)
    for g in range(GROUPS):
        for j in range(PER_GROUP):
            h = g * PER_GROUP + j
            qf[g, j * TOK : (j + 1) * TOK, :] = queries[:, h * HEAD : (h + 1) * HEAD]
    qg[ctx] = qf[...].astype(BF16)

    pl.semaphore_wait(barrier, len(partners))

    def block_of(dy, a):
        return lax.rem(y + dy + NY, NY) * 2 + (zh if a == 0 else 1 - zh)

    class Ring:
        def __init__(self, buf, base):
            self.buf, self.base, self.copies = buf, base, {}

        def copy(self, way, d, a):
            if (way, d, a) not in self.copies:
                sign = 1 if way == 0 else -1
                block = self.buf.at[block_of(-sign * (d - 1), a)]
                sem = self.base + (way * 4 + d - 1) * 2 + a
                self.copies[way, d, a] = remote(block, block, sem, at(dy=sign))
            return self.copies[way, d, a]

        def go(self, d, a, ways=(0, 1)):
            for way in ways:
                self.copy(way, d, a).start()

        def got(self, d, a, ways=(0, 1)):
            for way in ways:
                self.copy(way, d, a).wait_recv()

        def pass_on(self, d, a, ways=(0, 1)):
            for way in ways:
                self.copy(way, d, a).wait_recv()
                self.copy(way, d + 1, a).start()

        def end(self):
            for copy in self.copies.values():
                copy.wait_send()

    own = qg.at[ctx]
    ring = Ring(qg, Q_AG + 2)
    ring.go(1, 0)
    near = remote(own, own, Q_AG, at(dz=4))
    near.start()
    opposite = remote(own, own, Q_AG + 1, at(dy=4, dz=4))
    opposite.start()

    def pieces():
        for e in range(6):
            yield (e % 2 * 6, e // 2 * PART), (0, e * PART), 6
        yield (12, 0), (0, 6 * PART), 4
        yield (12, PART), (4, 6 * PART), 2
        yield (14, PART), (0, 7 * PART), 2
        yield (12, 2 * PART), (2, 7 * PART), 4

    def pack():
        for (pr, pc), (wr, wc), n in pieces():
            xf[pr : pr + n, pc : pc + PART] = xrow[wr : wr + n, wc : wc + PART]

    def unpack():
        for (pr, pc), (wr, wc), n in pieces():
            xrow[wr : wr + n, wc : wc + PART] = xf[pr : pr + n, pc : pc + PART]

    xrow[0:TOK, :] = res_ref[0].astype(F32)
    pack()
    rown[...] = xf[...].astype(BF16)
    lown[...] = jnp.zeros_like(lown)
    lown[0:1, 0:TOK] = logit_ref[...]
    res_copy = remote(rown, rfar, Z_RES, at(dz=4))
    res_copy.start()
    logit_copy = remote(lown, lfar, Z_RES + 1, at(dz=4))
    logit_copy.start()
    rtn[...] = jnp.zeros_like(rtn)

    newf[...] = jnp.zeros_like(newf)
    fresh = new_ref[0].astype(F32)
    newf[0, 0:TOK, :] = fresh[:, 0, :]
    newf[1, 0:TOK, :] = fresh[:, 1, :]
    for g in range(GROUPS):
        cols = slice(g * HEAD, (g + 1) * HEAD)
        kx[g, CACHE : CACHE + 16, :] = newf[0, :, cols].astype(BF16)
        vx[g, CACHE : CACHE + 16, 0:HEAD] = newf[1, :, cols].astype(BF16)
        kx[g, CACHE + 16 : KEYS, :] = jnp.zeros((KEYS - CACHE - 16, HEAD), BF16)
        vx[g, CACHE + 16 : KEYS, 0:HEAD] = jnp.zeros((KEYS - CACHE - 16, HEAD), BF16)
        vx[g, :, HEAD : 2 * HEAD] = jnp.ones((KEYS, HEAD), BF16)

    ids = jnp.sum(
        jnp.where(iota((96, 96), 0) == iota((96, 96), 1), rid_ref[0], 0), axis=1, keepdims=True
    )
    one_hot = (ids == iota((96, 128), 1)).astype(F32)
    before = (iota((96, 96), 1) < iota((96, 96), 0)).astype(BF16)
    counts = jnp.dot(before, one_hot.astype(BF16), preferred_element_type=F32)
    rank = jnp.sum(counts * one_hot, axis=1, keepdims=True)
    slot_col = ids.astype(F32) * 16.0 + rank
    slot_lane = jnp.sum(
        jnp.where(iota((96, 128), 0) == iota((96, 128), 1), slot_col, 0.0), axis=0, keepdims=True
    )

    for copy in cache_copies:
        copy.wait()

    limit = jnp.minimum(len_ref[0] - ctx * CACHE, CACHE)
    scale = HEAD ** (-0.5)

    def attend(blocks):
        count = len(blocks)
        rows = 32 * count
        row = iota((rows, KEYS), 0)
        lane = iota((rows, KEYS), 1)
        r = row & 31
        tok = r
        for edge in (6, 12, 18, 24):
            tok = tok - jnp.where(r >= edge, 6, 0)
        for i, block in enumerate(blocks):
            tok = tok + jnp.where((row >> 5) == i, block * TOK, 0)
        new_ok = (lane >= CACHE) & (lane < CACHE + TOK) & (ctx * TOK + lane - CACHE <= tok)
        bias[0:rows, :] = jnp.where((lane < limit) | new_ok, 0.0, NEG)

        def group(g, carry):
            q = jnp.concatenate([qg[block, g] for block in blocks], axis=0)
            scores = lax.dot_general(
                q, kx[g], (((1,), (1,)), ((), ())), preferred_element_type=F32
            )
            scores = scores * scale + bias[0:rows, :]
            top = jnp.maximum(jnp.max(scores, axis=1, keepdims=True), FLOOR)
            top = top.astype(BF16).astype(F32)
            weights = jnp.exp(scores - top).astype(BF16)
            sums = jnp.dot(weights, vx[g], preferred_element_type=F32)
            shape = (count, 32, HEAD)
            weighted = sums[:, 0:HEAD].reshape(shape)
            total = sums[:, HEAD : 2 * HEAD].reshape(shape)
            tops = jnp.broadcast_to(top, (rows, HEAD)).reshape(shape)
            on = (iota(shape, 2) & 31) == iota(shape, 1)
            top_row = jnp.sum(jnp.where(on, tops, 0.0), axis=1, keepdims=True)
            total_row = jnp.sum(jnp.where(on, total, 0.0), axis=1, keepdims=True)
            at_row = iota(shape, 1)
            packed = jnp.where(
                at_row == 30, top_row, jnp.where(at_row == 31, total_row, weighted)
            ).astype(BF16)
            for i, block in enumerate(blocks):
                pw[block, g] = packed[i]
            return carry

        lax.fori_loop(0, GROUPS, group, 0, unroll=2)

    scatters = []

    def pair_of(dy):
        return pl.ds(lax.rem(y + dy + NY, NY) * 2, 2)

    def ship(src, dst, sem, d):
        copy = remote(src, dst, sem, at(dy=d))
        copy.start()
        scatters.append(copy)
        return copy

    def ship_near(src, dst, base):
        up = ship(src.at[pair_of(1)], dst.at[1], base, 1)
        down = ship(src.at[pair_of(-1)], dst.at[2], base + 1, -1)
        return [up, down]

    def ship_three(src, dst, base):
        up = ship(src.at[pair_of(3)], dst.at[0], base + 2, 1)
        down = ship(src.at[pair_of(-3)], dst.at[1], base + 3, -1)
        return up, down

    def ship_four(src, dst, base):
        up = ship(src.at[block_of(4, 0)], dst.at[0], base + 4, 2)
        down = ship(src.at[block_of(4, 1)], dst.at[1], base + 5, -2)
        return up, down

    far = {}

    empty_row = iota((3, 32, HEAD), 1)
    empty = jnp.where(empty_row == 30, FLOOR, 0.0).astype(BF16)

    def settle_rin(g, carry):
        for i in range(3):
            for a in range(2):
                rin[5 + i, a, g] = empty[i]
        return carry

    lax.fori_loop(0, GROUPS, settle_rin, 0)
    ring.pass_on(1, 0)
    attend([block_of(0, 0), block_of(-1, 0), block_of(1, 0)])
    ring.pass_on(2, 0)
    near.wait_recv()
    ring.go(1, 1)
    weight_copies = []
    for i, (src, dst) in enumerate(parts):
        weight_copies.append(remote(src, dst, WEIGHTS + i, at(flip=True)))
        weight_copies[i].start()
    attend([block_of(-2, 0), block_of(2, 0), block_of(0, 1)])
    rin[0] = pw[pair_of(0)]
    ring.pass_on(3, 0, (0,))
    ring.got(3, 0, (1,))
    ring.pass_on(1, 1)
    opposite.wait_recv()
    beyond = []
    for way, sign in ((0, 1), (1, -1)):
        block = qg.at[block_of(4, 1)]
        copy = remote(block, block, Q_AG + 2 + (way * 4 + 2) * 2 + 1, at(dy=sign))
        copy.start()
        beyond.append(copy)
    attend([block_of(-3, 0), block_of(3, 0), block_of(-1, 1), block_of(1, 1)])
    ship_near(pw, rin, Q_RS)
    ring.got(4, 0, (0,))
    for copy in beyond:
        copy.wait_recv()
    attend([block_of(4, 0), block_of(4, 1), block_of(-3, 1), block_of(3, 1)])
    far[3] = ship_three(pw, r3, Q_RS)
    far[4] = ship_four(pw, r4, Q_RS)
    ring.got(2, 1)
    attend([block_of(-2, 1), block_of(2, 1)])
    ring.end()
    for copy in beyond + [near, opposite, res_copy, logit_copy]:
        copy.wait_send()

    def merge(stack, count, normalize):
        wide = stack.astype(F32)
        tops = wide[:, 30, :]
        totals = wide[:, 31, :]
        top = jnp.max(tops, axis=0, keepdims=True)
        factor = jnp.exp(tops - top)
        total = jnp.sum(factor * totals, axis=0, keepdims=True)
        if normalize:
            factor = factor / total
        lane = iota((32, 128), 1)
        row = iota((32, 128), 0)
        on = ((lane & 31) == row) & (row < 30)
        merged = jnp.zeros((32, HEAD), F32)
        for part in range(count // 4):
            spread = jnp.zeros((32, 128), F32)
            for i in range(4):
                spread = jnp.where((lane >> 5) == i, factor[4 * part + i : 4 * part + i + 1], spread)
            spread = jnp.where(on, spread, 0.0)
            high = spread.astype(BF16)
            low = (spread - high.astype(F32)).astype(BF16)
            rows = stack[4 * part : 4 * part + 4].reshape(128, HEAD)
            merged = merged + jnp.dot(high, rows, preferred_element_type=F32)
            merged = merged + jnp.dot(low, rows, preferred_element_type=F32)
        return merged, top, total

    def merged_block(stack, count):
        merged, top, total = merge(stack, count, False)
        at_row = iota((32, HEAD), 0)
        return jnp.where(at_row == 30, top, jnp.where(at_row == 31, total, merged)).astype(BF16)

    for side in (0, 1):
        far[3][side].wait_recv()
        for a in (1 - side, side):
            if a == side:
                far[4][side].wait_recv()

            def group(g, carry, side=side, a=a):
                position = zh if a == 0 else 1 - zh
                own = pw[block_of(2 - 4 * side, a), g]
                third = r3[side, position, g]
                fourth = r4[side, g] if a == side else empty[0]
                stack = jnp.concatenate([own[None], third[None], fourth[None], empty[0:1]], axis=0)
                mg[side, a, g] = merged_block(stack, 4)
                return carry

            lax.fori_loop(0, GROUPS, group, 0)
            position = zh if a == 0 else 1 - zh
            ship(
                mg.at[side, a], rin.at[3 + side, position], Q_RS + 6 + 2 * side + a, 2 - 4 * side
            )
    for copy in scatters:
        copy.wait_send()
    for copy in scatters:
        if not any(copy is other for other in far[3] + far[4]):
            copy.wait_recv()
    scatters.clear()

    def merge_y(block):
        def group(g, carry):
            za[block, g] = merged_block(rin[:, block, g], NY)
            return carry

        lax.fori_loop(0, GROUPS, group, 0, unroll=2)

    across = []
    for a in (1, 0):
        position = zh if a == 0 else 1 - zh
        merge_y(position)
        copy = remote(za.at[position], zi.at[position], Q_Z + a, at(dz=4))
        copy.start()
        across.append(copy)

    def norm(position, logits, state_ref):
        def group(g, carry):
            stack = jnp.concatenate([za[position, g][None], zi[position, g][None], empty[0:2]], axis=0)
            merged, _, _ = merge(stack, 4, True)
            attf[g] = merged
            return carry

        lax.fori_loop(0, GROUPS, group, 0, unroll=2)
        for g in range(GROUPS):
            for j in range(PER_GROUP):
                h = g * PER_GROUP + j
                cols = slice(h * HEAD, (h + 1) * HEAD)
                state = xrow[0:TOK, cols] + attf[g, j * TOK : (j + 1) * TOK, :]
                state_ref[0:TOK, cols] = state.astype(BF16).astype(F32)
        state = state_ref[0:TOK, :]
        inv_rms = lax.rsqrt(jnp.mean(state * state, axis=1, keepdims=True) + 1e-05)
        logit = jnp.broadcast_to(logits, (TOK, 128))
        logit = jnp.sum(
            jnp.where(iota((TOK, 128), 0) == iota((TOK, 128), 1), logit, 0.0), axis=1, keepdims=True
        )
        gate = 1.0 / (1.0 + jnp.exp(-logit))
        xrow[0:TOK, :] = state * inv_rms * gain_ref[...].reshape(1, WIDTH).astype(F32) * gate
        pack()
        xg[y * 2 + position] = xf[...].astype(BF16)

    ring = Ring(xg, X_AG)
    xrow[0:TOK, :] = res_ref[0].astype(F32)
    across[0].wait_recv()
    norm(zh, lown[0:1, :], hid)
    ring.go(1, 0)
    res_copy.wait_recv()
    logit_copy.wait_recv()
    xf[...] = rfar[...].astype(F32)
    unpack()
    across[1].wait_recv()
    norm(1 - zh, lfar[0:1, :], hid2)
    ring.go(1, 1)
    for d in (1, 2):
        ring.pass_on(d, 0)
        ring.pass_on(d, 1)
    ring.pass_on(3, 0, (0,))
    ring.pass_on(3, 1, (1,))
    ring.got(3, 0, (1,))
    ring.got(3, 1, (0,))
    ring.got(4, 0, (0,))
    ring.got(4, 1, (1,))
    ring.end()
    for copy in across:
        copy.wait_send()

    rows_in = [xg[:, :, k * PART : (k + 1) * PART].reshape(256, PART) for k in range(3)]
    lanes = iota((96, 256), 1)
    lane_slots = []
    for k in range(3):
        tok, _ = item_of(lanes, k)
        lane_slots.append(
            jnp.sum(jnp.where(iota((96, 256), 0) == tok, slot_col, 0.0), axis=0, keepdims=True)
        )
    for j in range(3):
        for half in range(2):
            target, eighth_row = slot_of(iota((256, 256), 0), j, half)
            target = target.astype(F32)
            total = jnp.zeros((256, PART), F32)
            for k in thirds_for(j, half):
                _, eighth_lane = item_of(iota((256, 256), 1), k)
                pick = (lane_slots[k] == target) & (eighth_lane == eighth_row)
                pick = jnp.where(pick, 1.0, 0.0).astype(BF16)
                total = total + jnp.dot(pick, rows_in[k], preferred_element_type=F32)
            start = j * QUART + half * PART
            sb[:, :, start : start + PART] = total.astype(BF16).reshape(16, 16, PART)

    own_block = pltpu.make_async_copy(sb.at[expert], rb.at[0, 0], local.at[24])
    own_block.start()

    def parity(cls):
        return lax.rem(y + cls, 2)

    def routes(cls):
        if cls == 0:
            for dx in (1, 2, 3):
                yield 0, dx, dx - 1
        else:
            for i in (0, 1):
                dz = CLASSES[cls] if cls < 3 else 2 - 4 * i
                yield dz, 2 * i + parity(cls), 1 + 2 * cls + i

    sent = [[], [], [], []]
    for cls in (1, 2, 0, 3):
        for dz, dx, index in routes(cls):
            to = lax.rem(zl + dz + 4, 4) * 4 + lax.rem(x + dx, 4)
            copy = remote(sb.at[to], rb.at[cls, dx], GO + index, at(dz=dz, dx=dx))
            copy.start()
            sent[cls].append(copy)

    for copy in copies + weight_copies:
        copy.wait()

    def experts(rows):
        n = rows.shape[0]
        main = jnp.dot(rows, wgu[0 : 3 * QUART, :], preferred_element_type=F32)
        r = iota((n, 512), 0) & 15
        tail = None
        for j in (2, 1, 0):
            part = jnp.dot(
                rows[:, j * QUART : (j + 1) * QUART],
                wgu[3 * QUART : 4 * QUART, :],
                preferred_element_type=F32,
            )
            part = pltpu.roll(part, n - 12 + 4 * j, 0)
            tail = part if tail is None else jnp.where(r < 4 * (j + 1), part, tail)
        both = main + tail
        gate_out, up_out = both[:, 0:256], both[:, 256:512]
        act = gate_out / (1.0 + jnp.exp(-gate_out)) * up_out
        r = iota((n, 256), 0) & 15
        act = jnp.where(r < 12, act, 0.0).astype(BF16).astype(F32)
        results = []
        for j in range(3):
            late = jnp.where(r >= 12, pltpu.roll(act, 12 - 4 * j, 0), 0.0)
            left = jnp.concatenate([act, late], axis=1).astype(BF16)
            results.append(jnp.dot(left, wdx[j], preferred_element_type=F32).astype(BF16))
        return results

    back = []
    swaps = {}
    partial = {}

    def swap(cls):
        swaps[cls] = []
        for i, copy in enumerate(sent[cls]):
            copy.wait_recv()
            block = rb.at[cls, 2 * i + parity(cls)]
            onward = remote(block, block, GO_Y + 2 * (cls - 1) + i, at(dy=1 - 2 * i))
            onward.start()
            swaps[cls].append(onward)

    def run(first, count):
        rows = rb[first : first + count].reshape(64 * count, 3 * QUART)
        for j, part in enumerate(experts(rows)):
            pp[first : first + count, :, :, j * QUART : (j + 1) * QUART] = part.reshape(
                count, 4, 16, QUART
            )

    def send_back(cls):
        for dz, dx, index in routes(cls):
            copy = remote(pp.at[cls, dx], rtn.at[expert], BACK + index, at(dz=-dz, dx=-dx))
            copy.start()
            back.append(copy)

    def give(cls):
        partial[cls] = []
        for i in (0, 1):
            block = pp.at[cls, 2 * i + 1 - parity(cls)]
            copy = remote(
                block, yq.at[cls - 1, i], BACK_Y + 2 * (cls - 1) + i, at(dy=2 * i - 1)
            )
            copy.start()
            partial[cls].append(copy)

    def add_planes(cls):
        for i in (0, 1):
            partial[cls][i].wait_recv()
            dx = 2 * i + parity(cls)
            total = pp[cls, dx].astype(F32) + yq[cls - 1, i].astype(F32)
            pp[cls, dx] = total.astype(BF16)
        send_back(cls)

    swap(1)
    swap(2)
    for copy in sent[0]:
        copy.wait_recv()
    own_block.wait()
    run(0, 1)
    send_back(0)
    rtn[expert] = pp[0, 0]
    swap(3)
    for cls in (1, 2):
        for copy in swaps[cls]:
            copy.wait_recv()
    run(1, 2)
    give(1)
    give(2)
    for copy in swaps[3]:
        copy.wait_recv()
    run(3, 1)
    give(3)
    add_planes(1)
    add_planes(2)
    add_planes(3)

    for cls in range(4):
        for copy in sent[cls] + swaps.get(cls, []) + partial.get(cls, []):
            copy.wait_send()
    for copy in back:
        copy.wait()

    due = []
    lanes = iota((256, 128), 1)
    for k in range(3):
        tok, _ = item_of(iota((256, 128), 0), k)
        row_slots = jnp.sum(jnp.where(lanes == tok, slot_lane, 0.0), axis=1, keepdims=True)
        _, eighth_row = item_of(iota((256, 256), 0), k)
        total = jnp.zeros((256, PART), F32)
        for j in range(3):
            for half in range(2):
                if k not in thirds_for(j, half):
                    continue
                target, eighth_lane = slot_of(iota((256, 256), 1), j, half)
                pick = (row_slots == target.astype(F32)) & (eighth_lane == eighth_row)
                pick = jnp.where(pick, 1.0, 0.0).astype(BF16)
                start = j * QUART + half * PART
                source = rtn[:, :, start : start + PART].reshape(256, PART)
                total = total + jnp.dot(pick, source, preferred_element_type=F32)
        rsb[k] = total.astype(BF16).reshape(16, 16, PART)
        base = Y_RS + 11 * k
        far[3, k] = ship_three(rsb.at[k], f3.at[k], base)
        far[4, k] = ship_four(rsb.at[k], f4.at[k], base)
        due.append([])
        due[k] += ship_near(rsb.at[k], rsi.at[k], base)
        rsi[k, 0] = rsb[k, pair_of(0)]

    for k in range(3):
        for side in (0, 1):
            far[3, k][side].wait_recv()
            for a in (1 - side, side):
                position = zh if a == 0 else 1 - zh
                total = rsb[k, block_of(2 - 4 * side, a)].astype(F32)
                total = total + f3[k, side, position].astype(F32)
                if a == side:
                    far[4, k][side].wait_recv()
                    total = total + f4[k, side].astype(F32)
                fm[k, side, a] = total.astype(BF16)
                copy = ship(
                    fm.at[k, side, a],
                    rsi.at[k, 3 + side, position],
                    Y_RS + 11 * k + 6 + 2 * side + a,
                    2 - 4 * side,
                )
                due[k].append(copy)

    def add_up(k, block):
        total = rsi[k, 0, block].astype(F32)
        for i in range(1, 5):
            total = total + rsi[k, i, block].astype(F32)
        return total

    across = []
    for k in range(3):
        for copy in due[k]:
            copy.wait_recv()
        zo2[k] = add_up(k, 1 - zh).astype(BF16)
        across.append(remote(zo2.at[k], zi2.at[k], Y_RS + 11 * k + 10, at(dz=4)))
        across[k].start()
    for k in range(3):
        total = add_up(k, zh)
        across[k].wait_recv()
        xf[:, k * PART : (k + 1) * PART] = total + zi2[k].astype(F32)
    unpack()
    out_ref[0] = (hid[0:TOK, :] + xrow[0:TOK, :]).astype(BF16)
    for copy in scatters + across:
        copy.wait_send()


def body(
    queries,
    new_kv,
    cached_key_value,
    cache_len,
    residual,
    norm_gain,
    route_logit,
    route_id,
    w_gate,
    w_up,
    w_down,
):
    vmem = pl.BlockSpec(memory_space=pltpu.VMEM)
    smem = pl.BlockSpec(memory_space=pltpu.SMEM)
    hbm = pl.BlockSpec(memory_space=pl.ANY)
    block = (GROUPS, 32, HEAD)
    slots = (16, 16, 3 * QUART)
    return pl.pallas_call(
        kernel,
        out_shape=jax.ShapeDtypeStruct((1, TOK, WIDTH), BF16),
        in_specs=[vmem, vmem, hbm, smem, vmem, vmem, vmem, vmem, hbm, hbm, hbm],
        out_specs=vmem,
        scratch_shapes=[
            pltpu.VMEM(block, F32),
            pltpu.VMEM((16,) + block, BF16),
            pltpu.VMEM((16,) + block, BF16),
            pltpu.VMEM((NY, 2) + block, BF16),
            pltpu.VMEM((2,) + block, BF16),
            pltpu.VMEM((2,) + block, BF16),
            pltpu.VMEM((2, 2) + block, BF16),
            pltpu.VMEM((2,) + block, BF16),
            pltpu.VMEM((2, 2) + block, BF16),
            pltpu.VMEM(block, F32),
            pltpu.VMEM((16, 3 * PART), BF16),
            pltpu.VMEM((16, 3 * PART), BF16),
            pltpu.VMEM((8, 128), F32),
            pltpu.VMEM((8, 128), F32),
            pltpu.VMEM((8, WIDTH), F32),
            pltpu.VMEM((8, WIDTH), F32),
            pltpu.VMEM((8, WIDTH), F32),
            pltpu.VMEM((16, 3 * PART), F32),
            pltpu.VMEM((16, 16, 3 * PART), BF16),
            pltpu.VMEM(slots, BF16),
            pltpu.VMEM((4, 4, 16, 3 * QUART), BF16),
            pltpu.VMEM((4, 4, 16, 3 * QUART), BF16),
            pltpu.VMEM((3, 2, 16, 3 * QUART), BF16),
            pltpu.VMEM(slots, BF16),
            pltpu.VMEM((3, 16, 16, PART), BF16),
            pltpu.VMEM((3, 5, 2, 16, PART), BF16),
            pltpu.VMEM((3, 2, 2, 16, PART), BF16),
            pltpu.VMEM((3, 2, 16, PART), BF16),
            pltpu.VMEM((3, 2, 2, 16, PART), BF16),
            pltpu.VMEM((3, 16, PART), BF16),
            pltpu.VMEM((3, 16, PART), BF16),
            pltpu.VMEM((WIDTH, 512), BF16),
            pltpu.VMEM((3, 512, QUART), BF16),
            pltpu.VMEM((GROUPS, KEYS, HEAD), BF16),
            pltpu.VMEM((GROUPS, KEYS, 2 * HEAD), BF16),
            pltpu.VMEM((2, 16, GROUPS * HEAD), F32),
            pltpu.VMEM((128, KEYS), F32),
            pltpu.SemaphoreType.DMA((N_SEM,)),
            pltpu.SemaphoreType.DMA((N_SEM,)),
            pltpu.SemaphoreType.DMA((26,)),
        ],
        compiler_params=pltpu.CompilerParams(
            collective_id=0, has_side_effects=True, vmem_limit_bytes=56 * 1024 * 1024
        ),
    )(
        queries,
        jnp.transpose(new_kv, (1, 2, 0, 3)),
        cached_key_value,
        cache_len,
        residual,
        norm_gain,
        route_logit,
        jnp.transpose(route_id, (0, 2, 1)),
        w_gate,
        w_up,
        w_down,
    )


def solution(mesh):
    placed = (
        P("ep", "ctx", None),
        P(None, "ep", "ctx", None),
        P(None, "ep", "ctx", None),
        P("ep"),
        P("ep", "ctx", None),
        P(),
        P("ep", "ctx"),
        P("ep", None, None),
        P("ep", None, "ctx"),
        P("ep", None, "ctx"),
        P("ep", "ctx", None),
    )
    return jax.shard_map(
        body, mesh=mesh, in_specs=placed, out_specs=P("ep", "ctx", None), check_vma=False
    )
```

```python
import jax
import jax.numpy as jnp
from jax import lax
from jax.experimental import pallas as pl
from jax.experimental.pallas import tpu as pltpu
from jax.sharding import PartitionSpec as P

MESH = pl.DeviceIdType.MESH
BF16 = jnp.bfloat16
F32 = jnp.float32

GROUPS = 8
PER_GROUP = 5
HEAD = 128
TOK = 6
WIDTH = 5120
CACHE = 256
KEYS = 384
NY = 8
PART = 640
QUART = 1280
NEG = -1e30
FLOOR = -1e29

Q_AG = 0
Z_RES = 18
Q_RS = 20
Q_Z = 30
X_AG = 32
GO = 48
GO_Y = 57
WEIGHTS = 63
BACK_Y = 71
BACK = 77
Y_RS = 86
N_SEM = 119
CLASSES = (0, 1, -1, 2)


def iota(shape, dim):
    return lax.broadcasted_iota(jnp.int32, shape, dim)


def item_of(index, third):
    rho = index & 15
    late = rho - 12 + 4 * third
    tok = jnp.where(rho < 6, rho, jnp.where(rho < 12, rho - 6, jnp.where(late < 6, late, late - 6)))
    eighth = jnp.where(
        rho < 6, 2 * third, jnp.where(rho < 12, 2 * third + 1, jnp.where(late < 6, 6, 7))
    )
    return (index >> 4) * TOK + tok, eighth


def slot_of(index, third, half):
    rho = index & 15
    slot = jnp.where(rho < 12, rho, rho - 12 + 4 * third)
    eighth = jnp.where(rho < 12, 2 * third + half, 6 + half)
    return (index >> 4) * 16 + slot, eighth


def thirds_for(third, half):
    return sorted({third, half, half + 1})


def kernel(
    q_ref,
    new_ref,
    cache_ref,
    len_ref,
    res_ref,
    gain_ref,
    logit_ref,
    rid_ref,
    wg_ref,
    wu_ref,
    wd_ref,
    out_ref,
    qf,
    qg,
    pw,
    rin,
    za,
    zi,
    r3,
    r4,
    mg,
    attf,
    rown,
    rfar,
    lown,
    lfar,
    hid,
    hid2,
    xrow,
    xf,
    xg,
    sb,
    rb,
    pp,
    yq,
    rtn,
    rsb,
    rsi,
    f3,
    f4,
    fm,
    zo2,
    zi2,
    wgu,
    wdx,
    kx,
    vx,
    newf,
    bias,
    send,
    recv,
    local,
    know,
):
    ctx = lax.axis_index("ctx")
    ep = lax.axis_index("ep")
    y, zh = lax.div(ctx, 2), lax.rem(ctx, 2)
    zl, x, core = lax.div(ep, 8), lax.rem(lax.div(ep, 2), 4), lax.rem(ep, 2)
    z = zh * 4 + zl
    expert = zl * 4 + x

    def at(dy=0, dz=0, dx=0, flip=False):
        ny = lax.rem(y + dy + NY, NY)
        nz = lax.rem(z + dz + 8, 8)
        nx = lax.rem(x + dx + 4, 4)
        nc = 1 - core if flip else core
        return (ny * 2 + lax.div(nz, 4), lax.rem(nz, 4) * 8 + nx * 2 + nc)

    def remote(src, dst, sem, device):
        return pltpu.make_async_remote_copy(
            src_ref=src,
            dst_ref=dst,
            send_sem=send.at[sem],
            recv_sem=recv.at[sem],
            device_id=device,
            device_id_type=MESH,
        )

    def of_core(start):
        return pl.ds(pl.multiple_of(start + core * 128, 128), 128)

    parts = [
        (wg_ref.at[0], wgu.at[:, of_core(0)]),
        (wu_ref.at[0], wgu.at[:, of_core(256)]),
    ]
    for j in range(3):
        parts.append((wd_ref.at[0, :, j * QUART : (j + 1) * QUART], wdx.at[j, of_core(0)]))
        parts.append((wd_ref.at[0, :, 3 * QUART : 4 * QUART], wdx.at[j, of_core(256)]))
    copies = [
        pltpu.make_async_copy(src, dst, local.at[i]) for i, (src, dst) in enumerate(parts)
    ]
    cache_copies = []
    for g in range(GROUPS):
        cols = slice(g * HEAD, (g + 1) * HEAD)
        cache_copies.append(
            pltpu.make_async_copy(
                cache_ref.at[0, 0, :, cols], kx.at[g, 0:CACHE], local.at[8 + 2 * g]
            )
        )
        cache_copies.append(
            pltpu.make_async_copy(
                cache_ref.at[1, 0, :, cols], vx.at[g, 0:CACHE, 0:HEAD], local.at[9 + 2 * g]
            )
        )
    for copy in cache_copies + copies:
        copy.start()

    barrier = pltpu.get_barrier_semaphore()
    beside_x = [at(dx=1), at(dx=-1)]
    beside_z = [at(dz=1), at(dz=-1)]
    beside_y = [at(dy=1), at(dy=-1)]
    partners = [at(dz=4), at(dy=4)] + beside_y + beside_x + beside_z + [at(flip=True)]
    for device in partners:
        pl.semaphore_signal(barrier, inc=1, device_id=device, device_id_type=MESH)

    def tell(step, devices):
        for device in devices:
            pl.semaphore_signal(know.at[step], inc=1, device_id=device, device_id_type=MESH)

    qf[...] = jnp.zeros_like(qf)
    queries = q_ref[0].astype(F32)
    for g in range(GROUPS):
        for j in range(PER_GROUP):
            h = g * PER_GROUP + j
            qf[g, j * TOK : (j + 1) * TOK, :] = queries[:, h * HEAD : (h + 1) * HEAD]
    qg[ctx] = qf[...].astype(BF16)

    pl.semaphore_wait(barrier, len(partners))

    def block_of(dy, a):
        return lax.rem(y + dy + NY, NY) * 2 + (zh if a == 0 else 1 - zh)

    class Ring:
        def __init__(self, buf, base):
            self.buf, self.base, self.copies = buf, base, {}

        def copy(self, way, d, a):
            if (way, d, a) not in self.copies:
                sign = 1 if way == 0 else -1
                block = self.buf.at[block_of(-sign * (d - 1), a)]
                sem = self.base + (way * 4 + d - 1) * 2 + a
                self.copies[way, d, a] = remote(block, block, sem, at(dy=sign))
            return self.copies[way, d, a]

        def go(self, d, a, ways=(0, 1)):
            for way in ways:
                self.copy(way, d, a).start()

        def got(self, d, a, ways=(0, 1)):
            for way in ways:
                self.copy(way, d, a).wait_recv()

        def pass_on(self, d, a, ways=(0, 1)):
            for way in ways:
                self.copy(way, d, a).wait_recv()
                self.copy(way, d + 1, a).start()

        def end(self):
            for copy in self.copies.values():
                copy.wait_send()

    own = qg.at[ctx]
    ring = Ring(qg, Q_AG + 2)
    ring.go(1, 0)
    near = remote(own, own, Q_AG, at(dz=4))
    near.start()
    partner_block = qg.at[block_of(0, 1)]
    opposite = remote(partner_block, partner_block, Q_AG + 1, at(dy=4))
    tell(0, beside_y + beside_x + beside_z)

    def pieces():
        for e in range(6):
            yield (e % 2 * 6, e // 2 * PART), (0, e * PART), 6
        yield (12, 0), (0, 6 * PART), 4
        yield (12, PART), (4, 6 * PART), 2
        yield (14, PART), (0, 7 * PART), 2
        yield (12, 2 * PART), (2, 7 * PART), 4

    def pack():
        for (pr, pc), (wr, wc), n in pieces():
            xf[pr : pr + n, pc : pc + PART] = xrow[wr : wr + n, wc : wc + PART]

    def unpack():
        for (pr, pc), (wr, wc), n in pieces():
            xrow[wr : wr + n, wc : wc + PART] = xf[pr : pr + n, pc : pc + PART]

    xrow[0:TOK, :] = res_ref[0].astype(F32)
    pack()
    rown[...] = xf[...].astype(BF16)
    lown[...] = jnp.zeros_like(lown)
    lown[0:1, 0:TOK] = logit_ref[...]
    res_copy = remote(rown, rfar, Z_RES, at(dz=4))
    res_copy.start()
    logit_copy = remote(lown, lfar, Z_RES + 1, at(dz=4))
    logit_copy.start()
    rtn[...] = jnp.zeros_like(rtn)

    newf[...] = jnp.zeros_like(newf)
    fresh = new_ref[0].astype(F32)
    newf[0, 0:TOK, :] = fresh[:, 0, :]
    newf[1, 0:TOK, :] = fresh[:, 1, :]
    for g in range(GROUPS):
        cols = slice(g * HEAD, (g + 1) * HEAD)
        kx[g, CACHE : CACHE + 16, :] = newf[0, :, cols].astype(BF16)
        vx[g, CACHE : CACHE + 16, 0:HEAD] = newf[1, :, cols].astype(BF16)
        kx[g, CACHE + 16 : KEYS, :] = jnp.zeros((KEYS - CACHE - 16, HEAD), BF16)
        vx[g, CACHE + 16 : KEYS, 0:HEAD] = jnp.zeros((KEYS - CACHE - 16, HEAD), BF16)
        vx[g, :, HEAD : 2 * HEAD] = jnp.ones((KEYS, HEAD), BF16)

    ids = jnp.sum(
        jnp.where(iota((96, 96), 0) == iota((96, 96), 1), rid_ref[0], 0), axis=1, keepdims=True
    )
    one_hot = (ids == iota((96, 128), 1)).astype(F32)
    before = (iota((96, 96), 1) < iota((96, 96), 0)).astype(BF16)
    counts = jnp.dot(before, one_hot.astype(BF16), preferred_element_type=F32)
    rank = jnp.sum(counts * one_hot, axis=1, keepdims=True)
    slot_col = ids.astype(F32) * 16.0 + rank
    slot_lane = jnp.sum(
        jnp.where(iota((96, 128), 0) == iota((96, 128), 1), slot_col, 0.0), axis=0, keepdims=True
    )

    for copy in cache_copies:
        copy.wait()

    limit = jnp.minimum(len_ref[0] - ctx * CACHE, CACHE)
    scale = HEAD ** (-0.5)

    def attend(blocks):
        count = len(blocks)
        rows = 32 * count
        row = iota((rows, KEYS), 0)
        lane = iota((rows, KEYS), 1)
        r = row & 31
        tok = r
        for edge in (6, 12, 18, 24):
            tok = tok - jnp.where(r >= edge, 6, 0)
        for i, block in enumerate(blocks):
            tok = tok + jnp.where((row >> 5) == i, block * TOK, 0)
        new_ok = (lane >= CACHE) & (lane < CACHE + TOK) & (ctx * TOK + lane - CACHE <= tok)
        bias[0:rows, :] = jnp.where((lane < limit) | new_ok, 0.0, NEG)

        def group(g, carry):
            q = jnp.concatenate([qg[block, g] for block in blocks], axis=0)
            scores = lax.dot_general(
                q, kx[g], (((1,), (1,)), ((), ())), preferred_element_type=F32
            )
            scores = scores * scale + bias[0:rows, :]
            top = jnp.maximum(jnp.max(scores, axis=1, keepdims=True), FLOOR)
            top = top.astype(BF16).astype(F32)
            weights = jnp.exp(scores - top).astype(BF16)
            sums = jnp.dot(weights, vx[g], preferred_element_type=F32)
            shape = (count, 32, HEAD)
            weighted = sums[:, 0:HEAD].reshape(shape)
            total = sums[:, HEAD : 2 * HEAD].reshape(shape)
            tops = jnp.broadcast_to(top, (rows, HEAD)).reshape(shape)
            on = (iota(shape, 2) & 31) == iota(shape, 1)
            top_row = jnp.sum(jnp.where(on, tops, 0.0), axis=1, keepdims=True)
            total_row = jnp.sum(jnp.where(on, total, 0.0), axis=1, keepdims=True)
            at_row = iota(shape, 1)
            packed = jnp.where(
                at_row == 30, top_row, jnp.where(at_row == 31, total_row, weighted)
            ).astype(BF16)
            for i, block in enumerate(blocks):
                pw[block, g] = packed[i]
            return carry

        lax.fori_loop(0, GROUPS, group, 0, unroll=4)

    scatters = []

    def pair_of(dy):
        return pl.ds(lax.rem(y + dy + NY, NY) * 2, 2)

    def ship(src, dst, sem, d):
        copy = remote(src, dst, sem, at(dy=d))
        copy.start()
        scatters.append(copy)
        return copy

    def ship_near(src, dst, base):
        up = ship(src.at[pair_of(1)], dst.at[1], base, 1)
        down = ship(src.at[pair_of(-1)], dst.at[2], base + 1, -1)
        return [up, down]

    def ship_three(src, dst, base):
        up = ship(src.at[pair_of(3)], dst.at[0], base + 2, 1)
        down = ship(src.at[pair_of(-3)], dst.at[1], base + 3, -1)
        return up, down

    def ship_four(src, dst, base):
        up = ship(src.at[block_of(4, 0)], dst.at[0], base + 4, 2)
        down = ship(src.at[block_of(4, 1)], dst.at[1], base + 5, -2)
        return up, down

    far = {}

    empty_row = iota((3, 32, HEAD), 1)
    empty = jnp.where(empty_row == 30, FLOOR, 0.0).astype(BF16)

    def settle_rin(g, carry):
        for i in range(3):
            for a in range(2):
                rin[5 + i, a, g] = empty[i]
        return carry

    lax.fori_loop(0, GROUPS, settle_rin, 0)
    ring.pass_on(1, 0)
    attend([block_of(0, 0), block_of(-1, 0), block_of(1, 0)])
    pl.semaphore_wait(know.at[0], 6)
    tell(1, beside_x + beside_z)
    ring.pass_on(2, 0)
    near.wait_recv()
    opposite.start()
    ring.go(1, 1)
    weight_copies = []
    for i, (src, dst) in enumerate(parts):
        weight_copies.append(remote(src, dst, WEIGHTS + i, at(flip=True)))
        weight_copies[i].start()
    attend([block_of(-2, 0), block_of(2, 0), block_of(0, 1)])
    pl.semaphore_wait(know.at[1], 4)
    tell(2, beside_x)
    rin[0] = pw[pair_of(0)]
    ring.pass_on(3, 0, (0,))
    ring.got(3, 0, (1,))
    ring.pass_on(1, 1)
    opposite.wait_recv()
    beyond = []
    for way, sign in ((0, 1), (1, -1)):
        block = qg.at[block_of(4, 1)]
        copy = remote(block, block, Q_AG + 2 + (way * 4 + 2) * 2 + 1, at(dy=sign))
        copy.start()
        beyond.append(copy)
    attend([block_of(-3, 0), block_of(3, 0), block_of(-1, 1), block_of(1, 1)])
    pl.semaphore_wait(know.at[2], 2)
    ship_near(pw, rin, Q_RS)
    ring.got(4, 0, (0,))
    for copy in beyond:
        copy.wait_recv()
    attend([block_of(4, 0), block_of(4, 1), block_of(-3, 1), block_of(3, 1)])
    far[3] = ship_three(pw, r3, Q_RS)
    far[4] = ship_four(pw, r4, Q_RS)
    ring.got(2, 1)
    attend([block_of(-2, 1), block_of(2, 1)])
    ring.end()
    for copy in beyond + [near, opposite, res_copy, logit_copy]:
        copy.wait_send()

    def merge(stack, count, normalize):
        wide = stack.astype(F32)
        tops = wide[:, 30, :]
        totals = wide[:, 31, :]
        top = jnp.max(tops, axis=0, keepdims=True)
        factor = jnp.exp(tops - top)
        total = jnp.sum(factor * totals, axis=0, keepdims=True)
        if normalize:
            factor = factor / total
        lane = iota((32, 128), 1)
        row = iota((32, 128), 0)
        on = ((lane & 31) == row) & (row < 30)
        merged = jnp.zeros((32, HEAD), F32)
        for part in range(count // 4):
            spread = jnp.zeros((32, 128), F32)
            for i in range(4):
                spread = jnp.where((lane >> 5) == i, factor[4 * part + i : 4 * part + i + 1], spread)
            spread = jnp.where(on, spread, 0.0)
            high = spread.astype(BF16)
            low = (spread - high.astype(F32)).astype(BF16)
            rows = stack[4 * part : 4 * part + 4].reshape(128, HEAD)
            merged = merged + jnp.dot(high, rows, preferred_element_type=F32)
            merged = merged + jnp.dot(low, rows, preferred_element_type=F32)
        return merged, top, total

    def merged_block(stack, count):
        merged, top, total = merge(stack, count, False)
        at_row = iota((32, HEAD), 0)
        return jnp.where(at_row == 30, top, jnp.where(at_row == 31, total, merged)).astype(BF16)

    for side in (0, 1):
        far[3][side].wait_recv()
        for a in (1 - side, side):
            if a == side:
                far[4][side].wait_recv()

            def group(g, carry, side=side, a=a):
                position = zh if a == 0 else 1 - zh
                own = pw[block_of(2 - 4 * side, a), g]
                third = r3[side, position, g]
                fourth = r4[side, g] if a == side else empty[0]
                stack = jnp.concatenate([own[None], third[None], fourth[None], empty[0:1]], axis=0)
                mg[side, a, g] = merged_block(stack, 4)
                return carry

            lax.fori_loop(0, GROUPS, group, 0, unroll=8)
            position = zh if a == 0 else 1 - zh
            ship(
                mg.at[side, a], rin.at[3 + side, position], Q_RS + 6 + 2 * side + a, 2 - 4 * side
            )
    for copy in scatters:
        copy.wait_send()
    for copy in scatters:
        if not any(copy is other for other in far[3] + far[4]):
            copy.wait_recv()
    scatters.clear()

    def merge_y(block):
        def group(g, carry):
            za[block, g] = merged_block(rin[:, block, g], NY)
            return carry

        lax.fori_loop(0, GROUPS, group, 0, unroll=8)

    across = []
    for a in (1, 0):
        position = zh if a == 0 else 1 - zh
        merge_y(position)
        copy = remote(za.at[position], zi.at[position], Q_Z + a, at(dz=4))
        copy.start()
        across.append(copy)

    def norm(position, logits, state_ref):
        def group(g, carry):
            stack = jnp.concatenate([za[position, g][None], zi[position, g][None], empty[0:2]], axis=0)
            merged, _, _ = merge(stack, 4, True)
            attf[g] = merged
            return carry

        lax.fori_loop(0, GROUPS, group, 0, unroll=8)
        for g in range(GROUPS):
            for j in range(PER_GROUP):
                h = g * PER_GROUP + j
                cols = slice(h * HEAD, (h + 1) * HEAD)
                state = xrow[0:TOK, cols] + attf[g, j * TOK : (j + 1) * TOK, :]
                state_ref[0:TOK, cols] = state.astype(BF16).astype(F32)
        state = state_ref[0:TOK, :]
        inv_rms = lax.rsqrt(jnp.mean(state * state, axis=1, keepdims=True) + 1e-05)
        logit = jnp.broadcast_to(logits, (TOK, 128))
        logit = jnp.sum(
            jnp.where(iota((TOK, 128), 0) == iota((TOK, 128), 1), logit, 0.0), axis=1, keepdims=True
        )
        gate = 1.0 / (1.0 + jnp.exp(-logit))
        xrow[0:TOK, :] = state * inv_rms * gain_ref[...].reshape(1, WIDTH).astype(F32) * gate
        pack()
        xg[y * 2 + position] = xf[...].astype(BF16)

    ring = Ring(xg, X_AG)
    xrow[0:TOK, :] = res_ref[0].astype(F32)
    across[0].wait_recv()
    norm(zh, lown[0:1, :], hid)
    ring.go(1, 0)
    res_copy.wait_recv()
    logit_copy.wait_recv()
    xf[...] = rfar[...].astype(F32)
    unpack()
    across[1].wait_recv()
    norm(1 - zh, lfar[0:1, :], hid2)
    ring.go(1, 1)
    for d in (1, 2):
        ring.pass_on(d, 0)
        ring.pass_on(d, 1)
    ring.pass_on(3, 0, (0,))
    ring.pass_on(3, 1, (1,))
    ring.got(3, 0, (1,))
    ring.got(3, 1, (0,))
    ring.got(4, 0, (0,))
    ring.got(4, 1, (1,))
    ring.end()
    for copy in across:
        copy.wait_send()

    rows_in = [xg[:, :, k * PART : (k + 1) * PART].reshape(256, PART) for k in range(3)]
    lanes = iota((96, 256), 1)
    lane_slots = []
    for k in range(3):
        tok, _ = item_of(lanes, k)
        lane_slots.append(
            jnp.sum(jnp.where(iota((96, 256), 0) == tok, slot_col, 0.0), axis=0, keepdims=True)
        )
    for j in range(3):
        for half in range(2):
            target, eighth_row = slot_of(iota((256, 256), 0), j, half)
            target = target.astype(F32)
            total = jnp.zeros((256, PART), F32)
            for k in thirds_for(j, half):
                _, eighth_lane = item_of(iota((256, 256), 1), k)
                pick = (lane_slots[k] == target) & (eighth_lane == eighth_row)
                pick = jnp.where(pick, 1.0, 0.0).astype(BF16)
                total = total + jnp.dot(pick, rows_in[k], preferred_element_type=F32)
            start = j * QUART + half * PART
            sb[:, :, start : start + PART] = total.astype(BF16).reshape(16, 16, PART)

    own_block = pltpu.make_async_copy(sb.at[expert], rb.at[0, 0], local.at[24])
    own_block.start()

    def parity(cls):
        return lax.rem(y + cls, 2)

    def routes(cls):
        if cls == 0:
            for dx in (1, 2, 3):
                yield 0, dx, dx - 1
        else:
            for i in (0, 1):
                dz = CLASSES[cls] if cls < 3 else 2 - 4 * i
                yield dz, 2 * i + parity(cls), 1 + 2 * cls + i

    sent = [[], [], [], []]
    for cls in (1, 2, 0, 3):
        for dz, dx, index in routes(cls):
            to = lax.rem(zl + dz + 4, 4) * 4 + lax.rem(x + dx, 4)
            copy = remote(sb.at[to], rb.at[cls, dx], GO + index, at(dz=dz, dx=dx))
            copy.start()
            sent[cls].append(copy)

    for copy in copies + weight_copies:
        copy.wait()

    def experts(rows):
        n = rows.shape[0]
        main = jnp.dot(rows, wgu[0 : 3 * QUART, :], preferred_element_type=F32)
        r = iota((n, 512), 0) & 15
        tail = None
        for j in (2, 1, 0):
            part = jnp.dot(
                rows[:, j * QUART : (j + 1) * QUART],
                wgu[3 * QUART : 4 * QUART, :],
                preferred_element_type=F32,
            )
            part = pltpu.roll(part, n - 12 + 4 * j, 0)
            tail = part if tail is None else jnp.where(r < 4 * (j + 1), part, tail)
        both = main + tail
        gate_out, up_out = both[:, 0:256], both[:, 256:512]
        act = gate_out / (1.0 + jnp.exp(-gate_out)) * up_out
        r = iota((n, 256), 0) & 15
        act = jnp.where(r < 12, act, 0.0).astype(BF16).astype(F32)
        results = []
        for j in range(3):
            late = jnp.where(r >= 12, pltpu.roll(act, 12 - 4 * j, 0), 0.0)
            left = jnp.concatenate([act, late], axis=1).astype(BF16)
            results.append(jnp.dot(left, wdx[j], preferred_element_type=F32).astype(BF16))
        return results

    back = []
    swaps = {}
    partial = {}

    def swap(cls):
        swaps[cls] = []
        for i, copy in enumerate(sent[cls]):
            copy.wait_recv()
            block = rb.at[cls, 2 * i + parity(cls)]
            onward = remote(block, block, GO_Y + 2 * (cls - 1) + i, at(dy=1 - 2 * i))
            onward.start()
            swaps[cls].append(onward)

    def run(first, count):
        rows = rb[first : first + count].reshape(64 * count, 3 * QUART)
        for j, part in enumerate(experts(rows)):
            pp[first : first + count, :, :, j * QUART : (j + 1) * QUART] = part.reshape(
                count, 4, 16, QUART
            )

    def send_back(cls):
        for dz, dx, index in routes(cls):
            copy = remote(pp.at[cls, dx], rtn.at[expert], BACK + index, at(dz=-dz, dx=-dx))
            copy.start()
            back.append(copy)

    def give(cls):
        partial[cls] = []
        for i in (0, 1):
            block = pp.at[cls, 2 * i + 1 - parity(cls)]
            copy = remote(
                block, yq.at[cls - 1, i], BACK_Y + 2 * (cls - 1) + i, at(dy=2 * i - 1)
            )
            copy.start()
            partial[cls].append(copy)

    def add_planes(cls):
        for i in (0, 1):
            partial[cls][i].wait_recv()
            dx = 2 * i + parity(cls)
            total = pp[cls, dx].astype(F32) + yq[cls - 1, i].astype(F32)
            pp[cls, dx] = total.astype(BF16)
        send_back(cls)

    swap(1)
    swap(2)
    for copy in sent[0]:
        copy.wait_recv()
    own_block.wait()
    run(0, 1)
    send_back(0)
    rtn[expert] = pp[0, 0]
    swap(3)
    for cls in (1, 2):
        for copy in swaps[cls]:
            copy.wait_recv()
    run(1, 2)
    give(1)
    give(2)
    for copy in swaps[3]:
        copy.wait_recv()
    run(3, 1)
    give(3)
    add_planes(1)
    add_planes(2)
    add_planes(3)

    for cls in range(4):
        for copy in sent[cls] + swaps.get(cls, []) + partial.get(cls, []):
            copy.wait_send()
    for copy in back:
        copy.wait()

    due = []
    lanes = iota((256, 128), 1)
    for k in range(3):
        tok, _ = item_of(iota((256, 128), 0), k)
        row_slots = jnp.sum(jnp.where(lanes == tok, slot_lane, 0.0), axis=1, keepdims=True)
        _, eighth_row = item_of(iota((256, 256), 0), k)
        total = jnp.zeros((256, PART), F32)
        for j in range(3):
            for half in range(2):
                if k not in thirds_for(j, half):
                    continue
                target, eighth_lane = slot_of(iota((256, 256), 1), j, half)
                pick = (row_slots == target.astype(F32)) & (eighth_lane == eighth_row)
                pick = jnp.where(pick, 1.0, 0.0).astype(BF16)
                start = j * QUART + half * PART
                source = rtn[:, :, start : start + PART].reshape(256, PART)
                total = total + jnp.dot(pick, source, preferred_element_type=F32)
        rsb[k] = total.astype(BF16).reshape(16, 16, PART)
        base = Y_RS + 11 * k
        far[3, k] = ship_three(rsb.at[k], f3.at[k], base)
        far[4, k] = ship_four(rsb.at[k], f4.at[k], base)
        due.append([])
        due[k] += ship_near(rsb.at[k], rsi.at[k], base)
        rsi[k, 0] = rsb[k, pair_of(0)]

    for k in range(3):
        for side in (0, 1):
            far[3, k][side].wait_recv()
            for a in (1 - side, side):
                position = zh if a == 0 else 1 - zh
                total = rsb[k, block_of(2 - 4 * side, a)].astype(F32)
                total = total + f3[k, side, position].astype(F32)
                if a == side:
                    far[4, k][side].wait_recv()
                    total = total + f4[k, side].astype(F32)
                fm[k, side, a] = total.astype(BF16)
                copy = ship(
                    fm.at[k, side, a],
                    rsi.at[k, 3 + side, position],
                    Y_RS + 11 * k + 6 + 2 * side + a,
                    2 - 4 * side,
                )
                due[k].append(copy)

    def add_up(k, block):
        total = rsi[k, 0, block].astype(F32)
        for i in range(1, 5):
            total = total + rsi[k, i, block].astype(F32)
        return total

    across = []
    for k in range(3):
        for copy in due[k]:
            copy.wait_recv()
        zo2[k] = add_up(k, 1 - zh).astype(BF16)
        across.append(remote(zo2.at[k], zi2.at[k], Y_RS + 11 * k + 10, at(dz=4)))
        across[k].start()
    for k in range(3):
        total = add_up(k, zh)
        across[k].wait_recv()
        xf[:, k * PART : (k + 1) * PART] = total + zi2[k].astype(F32)
    unpack()
    out_ref[0] = (hid[0:TOK, :] + xrow[0:TOK, :]).astype(BF16)
    for copy in scatters + across:
        copy.wait_send()


def body(
    queries,
    new_kv,
    cached_key_value,
    cache_len,
    residual,
    norm_gain,
    route_logit,
    route_id,
    w_gate,
    w_up,
    w_down,
):
    vmem = pl.BlockSpec(memory_space=pltpu.VMEM)
    smem = pl.BlockSpec(memory_space=pltpu.SMEM)
    hbm = pl.BlockSpec(memory_space=pl.ANY)
    block = (GROUPS, 32, HEAD)
    slots = (16, 16, 3 * QUART)
    return pl.pallas_call(
        kernel,
        out_shape=jax.ShapeDtypeStruct((1, TOK, WIDTH), BF16),
        in_specs=[vmem, vmem, hbm, smem, vmem, vmem, vmem, vmem, hbm, hbm, hbm],
        out_specs=vmem,
        scratch_shapes=[
            pltpu.VMEM(block, F32),
            pltpu.VMEM((16,) + block, BF16),
            pltpu.VMEM((16,) + block, BF16),
            pltpu.VMEM((NY, 2) + block, BF16),
            pltpu.VMEM((2,) + block, BF16),
            pltpu.VMEM((2,) + block, BF16),
            pltpu.VMEM((2, 2) + block, BF16),
            pltpu.VMEM((2,) + block, BF16),
            pltpu.VMEM((2, 2) + block, BF16),
            pltpu.VMEM(block, F32),
            pltpu.VMEM((16, 3 * PART), BF16),
            pltpu.VMEM((16, 3 * PART), BF16),
            pltpu.VMEM((8, 128), F32),
            pltpu.VMEM((8, 128), F32),
            pltpu.VMEM((8, WIDTH), F32),
            pltpu.VMEM((8, WIDTH), F32),
            pltpu.VMEM((8, WIDTH), F32),
            pltpu.VMEM((16, 3 * PART), F32),
            pltpu.VMEM((16, 16, 3 * PART), BF16),
            pltpu.VMEM(slots, BF16),
            pltpu.VMEM((4, 4, 16, 3 * QUART), BF16),
            pltpu.VMEM((4, 4, 16, 3 * QUART), BF16),
            pltpu.VMEM((3, 2, 16, 3 * QUART), BF16),
            pltpu.VMEM(slots, BF16),
            pltpu.VMEM((3, 16, 16, PART), BF16),
            pltpu.VMEM((3, 5, 2, 16, PART), BF16),
            pltpu.VMEM((3, 2, 2, 16, PART), BF16),
            pltpu.VMEM((3, 2, 16, PART), BF16),
            pltpu.VMEM((3, 2, 2, 16, PART), BF16),
            pltpu.VMEM((3, 16, PART), BF16),
            pltpu.VMEM((3, 16, PART), BF16),
            pltpu.VMEM((WIDTH, 512), BF16),
            pltpu.VMEM((3, 512, QUART), BF16),
            pltpu.VMEM((GROUPS, KEYS, HEAD), BF16),
            pltpu.VMEM((GROUPS, KEYS, 2 * HEAD), BF16),
            pltpu.VMEM((2, 16, GROUPS * HEAD), F32),
            pltpu.VMEM((128, KEYS), F32),
            pltpu.SemaphoreType.DMA((N_SEM,)),
            pltpu.SemaphoreType.DMA((N_SEM,)),
            pltpu.SemaphoreType.DMA((26,)),
            pltpu.SemaphoreType.REGULAR((3,)),
        ],
        compiler_params=pltpu.CompilerParams(
            collective_id=0, has_side_effects=True, vmem_limit_bytes=56 * 1024 * 1024
        ),
    )(
        queries,
        jnp.transpose(new_kv, (1, 2, 0, 3)),
        cached_key_value,
        cache_len,
        residual,
        norm_gain,
        route_logit,
        jnp.transpose(route_id, (0, 2, 1)),
        w_gate,
        w_up,
        w_down,
    )


def solution(mesh):
    placed = (
        P("ep", "ctx", None),
        P(None, "ep", "ctx", None),
        P(None, "ep", "ctx", None),
        P("ep"),
        P("ep", "ctx", None),
        P(),
        P("ep", "ctx"),
        P("ep", None, None),
        P("ep", None, "ctx"),
        P("ep", None, "ctx"),
        P("ep", "ctx", None),
    )
    return jax.shard_map(
        body, mesh=mesh, in_specs=placed, out_specs=P("ep", "ctx", None), check_vma=False
    )
```

```python
import jax
import jax.numpy as jnp
from jax import lax
from jax.experimental import pallas as pl
from jax.experimental.pallas import tpu as pltpu
from jax.sharding import PartitionSpec as P

MESH = pl.DeviceIdType.MESH
BF16 = jnp.bfloat16
F32 = jnp.float32

GROUPS = 8
PER_GROUP = 5
HEAD = 128
TOK = 6
WIDTH = 5120
CACHE = 256
KEYS = 384
NY = 8
PART = 640
QUART = 1280
NEG = -1e30
FLOOR = -1e29

Q_AG = 0
Z_RES = 18
Q_RS = 20
Q_Z = 30
X_AG = 32
GO = 48
GO_Y = 56
WEIGHTS = 64
BACK_Y = 72
BACK = 80
Y_RS = 88
N_SEM = 121
CLASSES = (0, 1, -1, 2)
ORDER = (1, 2, 3, 0)


def iota(shape, dim):
    return lax.broadcasted_iota(jnp.int32, shape, dim)


def item_of(index, third):
    rho = index & 15
    late = rho - 12 + 4 * third
    tok = jnp.where(rho < 6, rho, jnp.where(rho < 12, rho - 6, jnp.where(late < 6, late, late - 6)))
    eighth = jnp.where(
        rho < 6, 2 * third, jnp.where(rho < 12, 2 * third + 1, jnp.where(late < 6, 6, 7))
    )
    return (index >> 4) * TOK + tok, eighth


def slot_of(index, third, half):
    rho = index & 15
    slot = jnp.where(rho < 12, rho, rho - 12 + 4 * third)
    eighth = jnp.where(rho < 12, 2 * third + half, 6 + half)
    return (index >> 4) * 16 + slot, eighth


def thirds_for(third, half):
    return sorted({third, half, half + 1})


def kernel(
    q_ref,
    new_ref,
    cache_ref,
    len_ref,
    res_ref,
    gain_ref,
    logit_ref,
    rid_ref,
    wg_ref,
    wu_ref,
    wd_ref,
    out_ref,
    qf,
    qg,
    pw,
    rin,
    za,
    zi,
    r3,
    r4,
    mg,
    attf,
    rown,
    rfar,
    lown,
    lfar,
    hid,
    hid2,
    xrow,
    xf,
    xg,
    sb,
    rb,
    pp,
    yq,
    rtn,
    rsb,
    rsi,
    f3,
    f4,
    fm,
    zo2,
    zi2,
    wgu,
    wdx,
    kx,
    vx,
    newf,
    bias,
    send,
    recv,
    local,
    know,
):
    ctx = lax.axis_index("ctx")
    ep = lax.axis_index("ep")
    y, zh = lax.div(ctx, 2), lax.rem(ctx, 2)
    zl, x, core = lax.div(ep, 8), lax.rem(lax.div(ep, 2), 4), lax.rem(ep, 2)
    z = zh * 4 + zl
    expert = zl * 4 + x

    def at(dy=0, dz=0, dx=0, flip=False):
        ny = lax.rem(y + dy + NY, NY)
        nz = lax.rem(z + dz + 8, 8)
        nx = lax.rem(x + dx + 4, 4)
        nc = 1 - core if flip else core
        return (ny * 2 + lax.div(nz, 4), lax.rem(nz, 4) * 8 + nx * 2 + nc)

    def remote(src, dst, sem, device):
        return pltpu.make_async_remote_copy(
            src_ref=src,
            dst_ref=dst,
            send_sem=send.at[sem],
            recv_sem=recv.at[sem],
            device_id=device,
            device_id_type=MESH,
        )

    def of_core(start):
        return pl.ds(pl.multiple_of(start + core * 128, 128), 128)

    parts = [
        (wg_ref.at[0], wgu.at[:, of_core(0)]),
        (wu_ref.at[0], wgu.at[:, of_core(256)]),
    ]
    for j in range(3):
        parts.append((wd_ref.at[0, :, j * QUART : (j + 1) * QUART], wdx.at[j, of_core(0)]))
        parts.append((wd_ref.at[0, :, 3 * QUART : 4 * QUART], wdx.at[j, of_core(256)]))
    copies = [
        pltpu.make_async_copy(src, dst, local.at[i]) for i, (src, dst) in enumerate(parts)
    ]
    cache_copies = []
    for g in range(GROUPS):
        cols = slice(g * HEAD, (g + 1) * HEAD)
        cache_copies.append(
            pltpu.make_async_copy(
                cache_ref.at[0, 0, :, cols], kx.at[g, 0:CACHE], local.at[8 + 2 * g]
            )
        )
        cache_copies.append(
            pltpu.make_async_copy(
                cache_ref.at[1, 0, :, cols], vx.at[g, 0:CACHE, 0:HEAD], local.at[9 + 2 * g]
            )
        )
    for copy in cache_copies + copies:
        copy.start()

    barrier = pltpu.get_barrier_semaphore()
    beside_x = [at(dx=1), at(dx=-1)]
    beside_z = [at(dz=1), at(dz=-1)]
    beside_y = [at(dy=1), at(dy=-1)]
    partners = [at(dz=4), at(dy=4)] + beside_y + beside_x + beside_z + [at(flip=True)]
    for device in partners:
        pl.semaphore_signal(barrier, inc=1, device_id=device, device_id_type=MESH)

    def tell(step, devices):
        for device in devices:
            pl.semaphore_signal(know.at[step], inc=1, device_id=device, device_id_type=MESH)

    qf[...] = jnp.zeros_like(qf)
    queries = q_ref[0].astype(F32)
    for g in range(GROUPS):
        for j in range(PER_GROUP):
            h = g * PER_GROUP + j
            qf[g, j * TOK : (j + 1) * TOK, :] = queries[:, h * HEAD : (h + 1) * HEAD]
    qg[ctx] = qf[...].astype(BF16)

    pl.semaphore_wait(barrier, len(partners))

    def block_of(dy, a):
        return lax.rem(y + dy + NY, NY) * 2 + (zh if a == 0 else 1 - zh)

    class Ring:
        def __init__(self, buf, base):
            self.buf, self.base, self.copies = buf, base, {}

        def copy(self, way, d, a):
            if (way, d, a) not in self.copies:
                sign = 1 if way == 0 else -1
                block = self.buf.at[block_of(-sign * (d - 1), a)]
                sem = self.base + (way * 4 + d - 1) * 2 + a
                self.copies[way, d, a] = remote(block, block, sem, at(dy=sign))
            return self.copies[way, d, a]

        def go(self, d, a, ways=(0, 1)):
            for way in ways:
                self.copy(way, d, a).start()

        def got(self, d, a, ways=(0, 1)):
            for way in ways:
                self.copy(way, d, a).wait_recv()

        def pass_on(self, d, a, ways=(0, 1)):
            for way in ways:
                self.copy(way, d, a).wait_recv()
                self.copy(way, d + 1, a).start()

        def end(self):
            for copy in self.copies.values():
                copy.wait_send()

    own = qg.at[ctx]
    ring = Ring(qg, Q_AG + 2)
    ring.go(1, 0)
    near = remote(own, own, Q_AG, at(dz=4))
    near.start()
    partner_block = qg.at[block_of(0, 1)]
    opposite = remote(partner_block, partner_block, Q_AG + 1, at(dy=4))
    tell(0, beside_y + beside_x + beside_z)

    def pieces():
        for e in range(6):
            yield (e % 2 * 6, e // 2 * PART), (0, e * PART), 6
        yield (12, 0), (0, 6 * PART), 4
        yield (12, PART), (4, 6 * PART), 2
        yield (14, PART), (0, 7 * PART), 2
        yield (12, 2 * PART), (2, 7 * PART), 4

    def pack():
        for (pr, pc), (wr, wc), n in pieces():
            xf[pr : pr + n, pc : pc + PART] = xrow[wr : wr + n, wc : wc + PART]

    def unpack():
        for (pr, pc), (wr, wc), n in pieces():
            xrow[wr : wr + n, wc : wc + PART] = xf[pr : pr + n, pc : pc + PART]

    xrow[0:TOK, :] = res_ref[0].astype(F32)
    pack()
    rown[...] = xf[...].astype(BF16)
    lown[...] = jnp.zeros_like(lown)
    lown[0:1, 0:TOK] = logit_ref[...]
    res_copy = remote(rown, rfar, Z_RES, at(dz=4))
    res_copy.start()
    logit_copy = remote(lown, lfar, Z_RES + 1, at(dz=4))
    logit_copy.start()
    rtn[...] = jnp.zeros_like(rtn)

    newf[...] = jnp.zeros_like(newf)
    fresh = new_ref[0].astype(F32)
    newf[0, 0:TOK, :] = fresh[:, 0, :]
    newf[1, 0:TOK, :] = fresh[:, 1, :]
    for g in range(GROUPS):
        cols = slice(g * HEAD, (g + 1) * HEAD)
        kx[g, CACHE : CACHE + 16, :] = newf[0, :, cols].astype(BF16)
        vx[g, CACHE : CACHE + 16, 0:HEAD] = newf[1, :, cols].astype(BF16)
        kx[g, CACHE + 16 : KEYS, :] = jnp.zeros((KEYS - CACHE - 16, HEAD), BF16)
        vx[g, CACHE + 16 : KEYS, 0:HEAD] = jnp.zeros((KEYS - CACHE - 16, HEAD), BF16)
        vx[g, :, HEAD : 2 * HEAD] = jnp.ones((KEYS, HEAD), BF16)

    ids = jnp.sum(
        jnp.where(iota((96, 96), 0) == iota((96, 96), 1), rid_ref[0], 0), axis=1, keepdims=True
    )
    one_hot = (ids == iota((96, 128), 1)).astype(F32)
    before = (iota((96, 96), 1) < iota((96, 96), 0)).astype(BF16)
    counts = jnp.dot(before, one_hot.astype(BF16), preferred_element_type=F32)
    rank = jnp.sum(counts * one_hot, axis=1, keepdims=True)
    slot_col = ids.astype(F32) * 16.0 + rank
    slot_lane = jnp.sum(
        jnp.where(iota((96, 128), 0) == iota((96, 128), 1), slot_col, 0.0), axis=0, keepdims=True
    )

    for copy in cache_copies:
        copy.wait()

    limit = jnp.minimum(len_ref[0] - ctx * CACHE, CACHE)
    scale = HEAD ** (-0.5)

    def attend(blocks):
        count = len(blocks)
        rows = 32 * count
        row = iota((rows, KEYS), 0)
        lane = iota((rows, KEYS), 1)
        r = row & 31
        tok = r
        for edge in (6, 12, 18, 24):
            tok = tok - jnp.where(r >= edge, 6, 0)
        for i, block in enumerate(blocks):
            tok = tok + jnp.where((row >> 5) == i, block * TOK, 0)
        new_ok = (lane >= CACHE) & (lane < CACHE + TOK) & (ctx * TOK + lane - CACHE <= tok)
        bias[0:rows, :] = jnp.where((lane < limit) | new_ok, 0.0, NEG)

        def group(g, carry):
            q = jnp.concatenate([qg[block, g] for block in blocks], axis=0)
            scores = lax.dot_general(
                q, kx[g], (((1,), (1,)), ((), ())), preferred_element_type=F32
            )
            scores = scores * scale + bias[0:rows, :]
            top = jnp.maximum(jnp.max(scores, axis=1, keepdims=True), FLOOR)
            top = top.astype(BF16).astype(F32)
            weights = jnp.exp(scores - top).astype(BF16)
            sums = jnp.dot(weights, vx[g], preferred_element_type=F32)
            shape = (count, 32, HEAD)
            weighted = sums[:, 0:HEAD].reshape(shape)
            total = sums[:, HEAD : 2 * HEAD].reshape(shape)
            tops = jnp.broadcast_to(top, (rows, HEAD)).reshape(shape)
            on = (iota(shape, 2) & 31) == iota(shape, 1)
            top_row = jnp.sum(jnp.where(on, tops, 0.0), axis=1, keepdims=True)
            total_row = jnp.sum(jnp.where(on, total, 0.0), axis=1, keepdims=True)
            at_row = iota(shape, 1)
            packed = jnp.where(
                at_row == 30, top_row, jnp.where(at_row == 31, total_row, weighted)
            ).astype(BF16)
            for i, block in enumerate(blocks):
                pw[block, g] = packed[i]
            return carry

        lax.fori_loop(0, GROUPS, group, 0, unroll=4)

    scatters = []

    def pair_of(dy):
        return pl.ds(lax.rem(y + dy + NY, NY) * 2, 2)

    def ship(src, dst, sem, d):
        copy = remote(src, dst, sem, at(dy=d))
        copy.start()
        scatters.append(copy)
        return copy

    def ship_near(src, dst, base):
        up = ship(src.at[pair_of(1)], dst.at[1], base, 1)
        down = ship(src.at[pair_of(-1)], dst.at[2], base + 1, -1)
        return [up, down]

    def ship_three(src, dst, base):
        up = ship(src.at[pair_of(3)], dst.at[0], base + 2, 1)
        down = ship(src.at[pair_of(-3)], dst.at[1], base + 3, -1)
        return up, down

    def ship_four(src, dst, base):
        up = ship(src.at[block_of(4, 0)], dst.at[0], base + 4, 2)
        down = ship(src.at[block_of(4, 1)], dst.at[1], base + 5, -2)
        return up, down

    far = {}

    empty_row = iota((3, 32, HEAD), 1)
    empty = jnp.where(empty_row == 30, FLOOR, 0.0).astype(BF16)

    def settle_rin(g, carry):
        for i in range(3):
            for a in range(2):
                rin[5 + i, a, g] = empty[i]
        return carry

    lax.fori_loop(0, GROUPS, settle_rin, 0)
    ring.pass_on(1, 0)
    attend([block_of(0, 0), block_of(-1, 0), block_of(1, 0)])
    pl.semaphore_wait(know.at[0], 6)
    tell(1, beside_x + beside_z)
    ring.pass_on(2, 0)
    near.wait_recv()
    opposite.start()
    ring.go(1, 1)
    weight_copies = []
    for i, (src, dst) in enumerate(parts):
        weight_copies.append(remote(src, dst, WEIGHTS + i, at(flip=True)))
        weight_copies[i].start()
    attend([block_of(-2, 0), block_of(2, 0), block_of(0, 1)])
    pl.semaphore_wait(know.at[1], 4)
    tell(2, beside_x)
    rin[0] = pw[pair_of(0)]
    ring.pass_on(3, 0, (0,))
    ring.got(3, 0, (1,))
    ring.pass_on(1, 1)
    opposite.wait_recv()
    beyond = []
    for way, sign in ((0, 1), (1, -1)):
        block = qg.at[block_of(4, 1)]
        copy = remote(block, block, Q_AG + 2 + (way * 4 + 2) * 2 + 1, at(dy=sign))
        copy.start()
        beyond.append(copy)
    attend([block_of(-3, 0), block_of(3, 0), block_of(-1, 1), block_of(1, 1)])
    pl.semaphore_wait(know.at[2], 2)
    ship_near(pw, rin, Q_RS)
    ring.got(4, 0, (0,))
    for copy in beyond:
        copy.wait_recv()
    attend([block_of(4, 0), block_of(4, 1), block_of(-3, 1), block_of(3, 1)])
    far[3] = ship_three(pw, r3, Q_RS)
    far[4] = ship_four(pw, r4, Q_RS)
    ring.got(2, 1)
    attend([block_of(-2, 1), block_of(2, 1)])
    ring.end()
    for copy in beyond + [near, opposite, res_copy, logit_copy]:
        copy.wait_send()

    def merge(stack, count, normalize):
        wide = stack.astype(F32)
        tops = wide[:, 30, :]
        totals = wide[:, 31, :]
        top = jnp.max(tops, axis=0, keepdims=True)
        factor = jnp.exp(tops - top)
        total = jnp.sum(factor * totals, axis=0, keepdims=True)
        if normalize:
            factor = factor / total
        lane = iota((32, 128), 1)
        row = iota((32, 128), 0)
        on = ((lane & 31) == row) & (row < 30)
        merged = jnp.zeros((32, HEAD), F32)
        for part in range(count // 4):
            spread = jnp.zeros((32, 128), F32)
            for i in range(4):
                spread = jnp.where((lane >> 5) == i, factor[4 * part + i : 4 * part + i + 1], spread)
            spread = jnp.where(on, spread, 0.0)
            high = spread.astype(BF16)
            low = (spread - high.astype(F32)).astype(BF16)
            rows = stack[4 * part : 4 * part + 4].reshape(128, HEAD)
            merged = merged + jnp.dot(high, rows, preferred_element_type=F32)
            merged = merged + jnp.dot(low, rows, preferred_element_type=F32)
        return merged, top, total

    def merged_block(stack, count):
        merged, top, total = merge(stack, count, False)
        at_row = iota((32, HEAD), 0)
        return jnp.where(at_row == 30, top, jnp.where(at_row == 31, total, merged)).astype(BF16)

    for side in (0, 1):
        far[3][side].wait_recv()
        for a in (1 - side, side):
            if a == side:
                far[4][side].wait_recv()

            def group(g, carry, side=side, a=a):
                position = zh if a == 0 else 1 - zh
                own = pw[block_of(2 - 4 * side, a), g]
                third = r3[side, position, g]
                fourth = r4[side, g] if a == side else empty[0]
                stack = jnp.concatenate([own[None], third[None], fourth[None], empty[0:1]], axis=0)
                mg[side, a, g] = merged_block(stack, 4)
                return carry

            lax.fori_loop(0, GROUPS, group, 0, unroll=8)
            position = zh if a == 0 else 1 - zh
            ship(
                mg.at[side, a], rin.at[3 + side, position], Q_RS + 6 + 2 * side + a, 2 - 4 * side
            )
    for copy in scatters:
        copy.wait_send()
    for copy in scatters:
        if not any(copy is other for other in far[3] + far[4]):
            copy.wait_recv()
    scatters.clear()

    def merge_y(block):
        def group(g, carry):
            za[block, g] = merged_block(rin[:, block, g], NY)
            return carry

        lax.fori_loop(0, GROUPS, group, 0, unroll=8)

    across = []
    for a in (1, 0):
        position = zh if a == 0 else 1 - zh
        merge_y(position)
        copy = remote(za.at[position], zi.at[position], Q_Z + a, at(dz=4))
        copy.start()
        across.append(copy)

    def norm(position, logits, state_ref):
        def group(g, carry):
            stack = jnp.concatenate([za[position, g][None], zi[position, g][None], empty[0:2]], axis=0)
            merged, _, _ = merge(stack, 4, True)
            attf[g] = merged
            return carry

        lax.fori_loop(0, GROUPS, group, 0, unroll=8)
        for g in range(GROUPS):
            for j in range(PER_GROUP):
                h = g * PER_GROUP + j
                cols = slice(h * HEAD, (h + 1) * HEAD)
                state = xrow[0:TOK, cols] + attf[g, j * TOK : (j + 1) * TOK, :]
                state_ref[0:TOK, cols] = state.astype(BF16).astype(F32)
        state = state_ref[0:TOK, :]
        inv_rms = lax.rsqrt(jnp.mean(state * state, axis=1, keepdims=True) + 1e-05)
        logit = jnp.broadcast_to(logits, (TOK, 128))
        logit = jnp.sum(
            jnp.where(iota((TOK, 128), 0) == iota((TOK, 128), 1), logit, 0.0), axis=1, keepdims=True
        )
        gate = 1.0 / (1.0 + jnp.exp(-logit))
        xrow[0:TOK, :] = state * inv_rms * gain_ref[...].reshape(1, WIDTH).astype(F32) * gate
        pack()
        xg[y * 2 + position] = xf[...].astype(BF16)

    ring = Ring(xg, X_AG)
    xrow[0:TOK, :] = res_ref[0].astype(F32)
    across[0].wait_recv()
    norm(zh, lown[0:1, :], hid)
    ring.go(1, 0)
    res_copy.wait_recv()
    logit_copy.wait_recv()
    xf[...] = rfar[...].astype(F32)
    unpack()
    across[1].wait_recv()
    norm(1 - zh, lfar[0:1, :], hid2)
    ring.go(1, 1)
    for d in (1, 2):
        ring.pass_on(d, 0)
        ring.pass_on(d, 1)
    ring.pass_on(3, 0, (0,))
    ring.pass_on(3, 1, (1,))
    ring.got(3, 0, (1,))
    ring.got(3, 1, (0,))
    ring.got(4, 0, (0,))
    ring.got(4, 1, (1,))
    ring.end()
    for copy in across:
        copy.wait_send()

    rows_in = [xg[:, :, k * PART : (k + 1) * PART].reshape(256, PART) for k in range(3)]
    lanes = iota((96, 256), 1)
    lane_slots = []
    for k in range(3):
        tok, _ = item_of(lanes, k)
        lane_slots.append(
            jnp.sum(jnp.where(iota((96, 256), 0) == tok, slot_col, 0.0), axis=0, keepdims=True)
        )
    for j in range(3):
        for half in range(2):
            target, eighth_row = slot_of(iota((256, 256), 0), j, half)
            target = target.astype(F32)
            total = jnp.zeros((256, PART), F32)
            for k in thirds_for(j, half):
                _, eighth_lane = item_of(iota((256, 256), 1), k)
                pick = (lane_slots[k] == target) & (eighth_lane == eighth_row)
                pick = jnp.where(pick, 1.0, 0.0).astype(BF16)
                total = total + jnp.dot(pick, rows_in[k], preferred_element_type=F32)
            start = j * QUART + half * PART
            sb[:, :, start : start + PART] = total.astype(BF16).reshape(16, 16, PART)

    own_block = pltpu.make_async_copy(sb.at[expert], rb.at[0, 0], local.at[24])
    own_block.start()

    def parity(cls):
        return lax.rem(y + cls, 2)

    def routes(cls):
        for i in (0, 1):
            dz = CLASSES[cls] if cls < 3 else 2 - 4 * i
            yield dz, 2 * i + parity(cls), 2 * cls + i

    odd, even = parity(0) == 1, parity(0) == 0

    def where_sent(cls, i, act, plane=odd):
        if (cls, i) == (0, 0):
            pl.when(plane)(act)
        else:
            act()

    sent = [[], [], [], []]
    for cls in ORDER:
        for i, (dz, dx, index) in enumerate(routes(cls)):
            to = lax.rem(zl + dz + 4, 4) * 4 + lax.rem(x + dx, 4)
            copy = remote(sb.at[to], rb.at[cls, dx], GO + index, at(dz=dz, dx=dx))
            where_sent(cls, i, copy.start)
            sent[cls].append(copy)

    for copy in copies + weight_copies:
        copy.wait()

    def experts(rows):
        n = rows.shape[0]
        main = jnp.dot(rows, wgu[0 : 3 * QUART, :], preferred_element_type=F32)
        r = iota((n, 512), 0) & 15
        tail = None
        for j in (2, 1, 0):
            part = jnp.dot(
                rows[:, j * QUART : (j + 1) * QUART],
                wgu[3 * QUART : 4 * QUART, :],
                preferred_element_type=F32,
            )
            part = pltpu.roll(part, n - 12 + 4 * j, 0)
            tail = part if tail is None else jnp.where(r < 4 * (j + 1), part, tail)
        both = main + tail
        gate_out, up_out = both[:, 0:256], both[:, 256:512]
        act = gate_out / (1.0 + jnp.exp(-gate_out)) * up_out
        r = iota((n, 256), 0) & 15
        act = jnp.where(r < 12, act, 0.0).astype(BF16).astype(F32)
        results = []
        for j in range(3):
            late = jnp.where(r >= 12, pltpu.roll(act, 12 - 4 * j, 0), 0.0)
            left = jnp.concatenate([act, late], axis=1).astype(BF16)
            results.append(jnp.dot(left, wdx[j], preferred_element_type=F32).astype(BF16))
        return results

    back = {}
    swaps = {}
    partial = {}

    def swap(cls):
        swaps[cls] = []
        for i, copy in enumerate(sent[cls]):
            block = rb.at[cls, 2 * i + parity(cls)]
            onward = remote(block, block, GO_Y + 2 * cls + i, at(dy=1 - 2 * i))

            def pass_on(copy=copy, onward=onward):
                copy.wait_recv()
                onward.start()

            where_sent(cls, i, pass_on)
            swaps[cls].append(onward)

    def swapped(cls):
        for i, onward in enumerate(swaps[cls]):
            where_sent(cls, i, onward.wait_recv, even)

    def run(first, count):
        rows = rb[first : first + count].reshape(64 * count, 3 * QUART)
        for j, part in enumerate(experts(rows)):
            pp[first : first + count, :, :, j * QUART : (j + 1) * QUART] = part.reshape(
                count, 4, 16, QUART
            )

    def give(cls):
        partial[cls] = []
        for i in (0, 1):
            block = pp.at[cls, 2 * i + 1 - parity(cls)]
            copy = remote(block, yq.at[cls, i], BACK_Y + 2 * cls + i, at(dy=2 * i - 1))
            where_sent(cls, i, copy.start, even)
            partial[cls].append(copy)

    def send_back(cls):
        back[cls] = []
        for i, (dz, dx, index) in enumerate(routes(cls)):
            copy = remote(pp.at[cls, dx], rtn.at[expert], BACK + index, at(dz=-dz, dx=-dx))

            def add_planes(i=i, dx=dx, copy=copy):
                partial[cls][i].wait_recv()
                total = pp[cls, dx].astype(F32) + yq[cls, i].astype(F32)
                pp[cls, dx] = total.astype(BF16)
                copy.start()

            where_sent(cls, i, add_planes)
            back[cls].append(copy)

    own_block.wait()
    for cls in ORDER:
        swap(cls)
    swapped(1)
    swapped(2)
    run(1, 2)
    give(1)
    give(2)
    swapped(3)
    run(3, 1)
    give(3)
    swapped(0)
    run(0, 1)
    give(0)
    rtn[expert] = pp[0, 0]
    for cls in ORDER:
        send_back(cls)

    for cls in range(4):
        for i in (0, 1):
            where_sent(cls, i, sent[cls][i].wait_send)
            where_sent(cls, i, swaps[cls][i].wait_send)
            where_sent(cls, i, partial[cls][i].wait_send, even)
            where_sent(cls, i, back[cls][i].wait)

    due = []
    lanes = iota((256, 128), 1)
    for k in range(3):
        tok, _ = item_of(iota((256, 128), 0), k)
        row_slots = jnp.sum(jnp.where(lanes == tok, slot_lane, 0.0), axis=1, keepdims=True)
        _, eighth_row = item_of(iota((256, 256), 0), k)
        total = jnp.zeros((256, PART), F32)
        for j in range(3):
            for half in range(2):
                if k not in thirds_for(j, half):
                    continue
                target, eighth_lane = slot_of(iota((256, 256), 1), j, half)
                pick = (row_slots == target.astype(F32)) & (eighth_lane == eighth_row)
                pick = jnp.where(pick, 1.0, 0.0).astype(BF16)
                start = j * QUART + half * PART
                source = rtn[:, :, start : start + PART].reshape(256, PART)
                total = total + jnp.dot(pick, source, preferred_element_type=F32)
        rsb[k] = total.astype(BF16).reshape(16, 16, PART)
        base = Y_RS + 11 * k
        far[3, k] = ship_three(rsb.at[k], f3.at[k], base)
        far[4, k] = ship_four(rsb.at[k], f4.at[k], base)
        due.append([])
        due[k] += ship_near(rsb.at[k], rsi.at[k], base)
        rsi[k, 0] = rsb[k, pair_of(0)]

    for k in range(3):
        for side in (0, 1):
            far[3, k][side].wait_recv()
            for a in (1 - side, side):
                position = zh if a == 0 else 1 - zh
                total = rsb[k, block_of(2 - 4 * side, a)].astype(F32)
                total = total + f3[k, side, position].astype(F32)
                if a == side:
                    far[4, k][side].wait_recv()
                    total = total + f4[k, side].astype(F32)
                fm[k, side, a] = total.astype(BF16)
                copy = ship(
                    fm.at[k, side, a],
                    rsi.at[k, 3 + side, position],
                    Y_RS + 11 * k + 6 + 2 * side + a,
                    2 - 4 * side,
                )
                due[k].append(copy)

    def add_up(k, block):
        total = rsi[k, 0, block].astype(F32)
        for i in range(1, 5):
            total = total + rsi[k, i, block].astype(F32)
        return total

    across = []
    for k in range(3):
        for copy in due[k]:
            copy.wait_recv()
        zo2[k] = add_up(k, 1 - zh).astype(BF16)
        across.append(remote(zo2.at[k], zi2.at[k], Y_RS + 11 * k + 10, at(dz=4)))
        across[k].start()
    for k in range(3):
        total = add_up(k, zh)
        across[k].wait_recv()
        xf[:, k * PART : (k + 1) * PART] = total + zi2[k].astype(F32)
    unpack()
    out_ref[0] = (hid[0:TOK, :] + xrow[0:TOK, :]).astype(BF16)
    for copy in scatters + across:
        copy.wait_send()


def body(
    queries,
    new_kv,
    cached_key_value,
    cache_len,
    residual,
    norm_gain,
    route_logit,
    route_id,
    w_gate,
    w_up,
    w_down,
):
    vmem = pl.BlockSpec(memory_space=pltpu.VMEM)
    smem = pl.BlockSpec(memory_space=pltpu.SMEM)
    hbm = pl.BlockSpec(memory_space=pl.ANY)
    block = (GROUPS, 32, HEAD)
    slots = (16, 16, 3 * QUART)
    return pl.pallas_call(
        kernel,
        out_shape=jax.ShapeDtypeStruct((1, TOK, WIDTH), BF16),
        in_specs=[vmem, vmem, hbm, smem, vmem, vmem, vmem, vmem, hbm, hbm, hbm],
        out_specs=vmem,
        scratch_shapes=[
            pltpu.VMEM(block, F32),
            pltpu.VMEM((16,) + block, BF16),
            pltpu.VMEM((16,) + block, BF16),
            pltpu.VMEM((NY, 2) + block, BF16),
            pltpu.VMEM((2,) + block, BF16),
            pltpu.VMEM((2,) + block, BF16),
            pltpu.VMEM((2, 2) + block, BF16),
            pltpu.VMEM((2,) + block, BF16),
            pltpu.VMEM((2, 2) + block, BF16),
            pltpu.VMEM(block, F32),
            pltpu.VMEM((16, 3 * PART), BF16),
            pltpu.VMEM((16, 3 * PART), BF16),
            pltpu.VMEM((8, 128), F32),
            pltpu.VMEM((8, 128), F32),
            pltpu.VMEM((8, WIDTH), F32),
            pltpu.VMEM((8, WIDTH), F32),
            pltpu.VMEM((8, WIDTH), F32),
            pltpu.VMEM((16, 3 * PART), F32),
            pltpu.VMEM((16, 16, 3 * PART), BF16),
            pltpu.VMEM(slots, BF16),
            pltpu.VMEM((4, 4, 16, 3 * QUART), BF16),
            pltpu.VMEM((4, 4, 16, 3 * QUART), BF16),
            pltpu.VMEM((4, 2, 16, 3 * QUART), BF16),
            pltpu.VMEM(slots, BF16),
            pltpu.VMEM((3, 16, 16, PART), BF16),
            pltpu.VMEM((3, 5, 2, 16, PART), BF16),
            pltpu.VMEM((3, 2, 2, 16, PART), BF16),
            pltpu.VMEM((3, 2, 16, PART), BF16),
            pltpu.VMEM((3, 2, 2, 16, PART), BF16),
            pltpu.VMEM((3, 16, PART), BF16),
            pltpu.VMEM((3, 16, PART), BF16),
            pltpu.VMEM((WIDTH, 512), BF16),
            pltpu.VMEM((3, 512, QUART), BF16),
            pltpu.VMEM((GROUPS, KEYS, HEAD), BF16),
            pltpu.VMEM((GROUPS, KEYS, 2 * HEAD), BF16),
            pltpu.VMEM((2, 16, GROUPS * HEAD), F32),
            pltpu.VMEM((128, KEYS), F32),
            pltpu.SemaphoreType.DMA((N_SEM,)),
            pltpu.SemaphoreType.DMA((N_SEM,)),
            pltpu.SemaphoreType.DMA((26,)),
            pltpu.SemaphoreType.REGULAR((3,)),
        ],
        compiler_params=pltpu.CompilerParams(
            collective_id=0, has_side_effects=True, vmem_limit_bytes=56 * 1024 * 1024
        ),
    )(
        queries,
        jnp.transpose(new_kv, (1, 2, 0, 3)),
        cached_key_value,
        cache_len,
        residual,
        norm_gain,
        route_logit,
        jnp.transpose(route_id, (0, 2, 1)),
        w_gate,
        w_up,
        w_down,
    )


def solution(mesh):
    placed = (
        P("ep", "ctx", None),
        P(None, "ep", "ctx", None),
        P(None, "ep", "ctx", None),
        P("ep"),
        P("ep", "ctx", None),
        P(),
        P("ep", "ctx"),
        P("ep", None, None),
        P("ep", None, "ctx"),
        P("ep", None, "ctx"),
        P("ep", "ctx", None),
    )
    return jax.shard_map(
        body, mesh=mesh, in_specs=placed, out_specs=P("ep", "ctx", None), check_vma=False
    )
```

```python
import jax
import jax.numpy as jnp
from jax import lax
from jax.experimental import pallas as pl
from jax.experimental.pallas import tpu as pltpu
from jax.sharding import PartitionSpec as P

MESH = pl.DeviceIdType.MESH
BF16 = jnp.bfloat16
F32 = jnp.float32

GROUPS = 8
PER_GROUP = 5
HEAD = 128
TOK = 6
WIDTH = 5120
CACHE = 256
KEYS = 384
NY = 8
PART = 640
QUART = 1280
NEG = -1e30
FLOOR = -1e29

Q_AG = 0
Z_RES = 18
Q_RS = 20
Q_Z = 30
X_AG = 32
GO = 48
GO_Y = 56
WEIGHTS = 64
BACK_Y = 72
BACK = 80
Y_RS = 88
N_SEM = 121
CLASSES = (0, 1, -1, 2)
ORDER = (1, 2, 3, 0)


def iota(shape, dim):
    return lax.broadcasted_iota(jnp.int32, shape, dim)


def item_of(index, third):
    rho = index & 15
    late = rho - 12 + 4 * third
    tok = jnp.where(rho < 6, rho, jnp.where(rho < 12, rho - 6, jnp.where(late < 6, late, late - 6)))
    eighth = jnp.where(
        rho < 6, 2 * third, jnp.where(rho < 12, 2 * third + 1, jnp.where(late < 6, 6, 7))
    )
    return (index >> 4) * TOK + tok, eighth


def slot_of(index, third, half):
    rho = index & 15
    slot = jnp.where(rho < 12, rho, rho - 12 + 4 * third)
    eighth = jnp.where(rho < 12, 2 * third + half, 6 + half)
    return (index >> 4) * 16 + slot, eighth


def thirds_for(third, half):
    return sorted({third, half, half + 1})


def kernel(
    q_ref,
    new_ref,
    cache_ref,
    len_ref,
    res_ref,
    gain_ref,
    logit_ref,
    rid_ref,
    wg_ref,
    wu_ref,
    wd_ref,
    out_ref,
    qf,
    qg,
    pw,
    rin,
    za,
    zi,
    r3,
    r4,
    mg,
    attf,
    rown,
    rfar,
    lown,
    lfar,
    hid,
    hid2,
    xrow,
    xf,
    xg,
    sb,
    rb,
    pp,
    yq,
    rtn,
    rsb,
    rsi,
    f3,
    f4,
    fm,
    zo2,
    zi2,
    wgu,
    wdx,
    kx,
    vx,
    newf,
    bias,
    send,
    recv,
    local,
    know,
):
    ctx = lax.axis_index("ctx")
    ep = lax.axis_index("ep")
    y, zh = lax.div(ctx, 2), lax.rem(ctx, 2)
    zl, x, core = lax.div(ep, 8), lax.rem(lax.div(ep, 2), 4), lax.rem(ep, 2)
    z = zh * 4 + zl
    expert = zl * 4 + x

    def at(dy=0, dz=0, dx=0, flip=False):
        ny = lax.rem(y + dy + NY, NY)
        nz = lax.rem(z + dz + 8, 8)
        nx = lax.rem(x + dx + 4, 4)
        nc = 1 - core if flip else core
        return (ny * 2 + lax.div(nz, 4), lax.rem(nz, 4) * 8 + nx * 2 + nc)

    def remote(src, dst, sem, device):
        return pltpu.make_async_remote_copy(
            src_ref=src,
            dst_ref=dst,
            send_sem=send.at[sem],
            recv_sem=recv.at[sem],
            device_id=device,
            device_id_type=MESH,
        )

    def of_core(start):
        return pl.ds(pl.multiple_of(start + core * 128, 128), 128)

    parts = [
        (wg_ref.at[0], wgu.at[:, of_core(0)]),
        (wu_ref.at[0], wgu.at[:, of_core(256)]),
    ]
    for j in range(3):
        parts.append((wd_ref.at[0, :, j * QUART : (j + 1) * QUART], wdx.at[j, of_core(0)]))
        parts.append((wd_ref.at[0, :, 3 * QUART : 4 * QUART], wdx.at[j, of_core(256)]))
    copies = [
        pltpu.make_async_copy(src, dst, local.at[i]) for i, (src, dst) in enumerate(parts)
    ]
    cache_copies = []
    for g in range(GROUPS):
        cols = slice(g * HEAD, (g + 1) * HEAD)
        cache_copies.append(
            pltpu.make_async_copy(
                cache_ref.at[0, 0, :, cols], kx.at[g, 0:CACHE], local.at[8 + 2 * g]
            )
        )
        cache_copies.append(
            pltpu.make_async_copy(
                cache_ref.at[1, 0, :, cols], vx.at[g, 0:CACHE, 0:HEAD], local.at[9 + 2 * g]
            )
        )
    for copy in cache_copies + copies:
        copy.start()

    barrier = pltpu.get_barrier_semaphore()
    beside_x = [at(dx=1), at(dx=-1)]
    beside_z = [at(dz=1), at(dz=-1)]
    beside_y = [at(dy=1), at(dy=-1)]
    partners = [at(dz=4), at(dy=4)] + beside_y + beside_x + beside_z + [at(flip=True)]
    for device in partners:
        pl.semaphore_signal(barrier, inc=1, device_id=device, device_id_type=MESH)

    def tell(step, devices):
        for device in devices:
            pl.semaphore_signal(know.at[step], inc=1, device_id=device, device_id_type=MESH)

    qf[...] = jnp.zeros_like(qf)
    queries = q_ref[0].astype(F32)
    for g in range(GROUPS):
        for j in range(PER_GROUP):
            h = g * PER_GROUP + j
            qf[g, j * TOK : (j + 1) * TOK, :] = queries[:, h * HEAD : (h + 1) * HEAD]
    qg[ctx] = qf[...].astype(BF16)

    pl.semaphore_wait(barrier, len(partners))

    def block_of(dy, a):
        return lax.rem(y + dy + NY, NY) * 2 + (zh if a == 0 else 1 - zh)

    class Ring:
        def __init__(self, buf, base):
            self.buf, self.base, self.copies = buf, base, {}

        def copy(self, way, d, a):
            if (way, d, a) not in self.copies:
                sign = 1 if way == 0 else -1
                block = self.buf.at[block_of(-sign * (d - 1), a)]
                sem = self.base + (way * 4 + d - 1) * 2 + a
                self.copies[way, d, a] = remote(block, block, sem, at(dy=sign))
            return self.copies[way, d, a]

        def go(self, d, a, ways=(0, 1)):
            for way in ways:
                self.copy(way, d, a).start()

        def got(self, d, a, ways=(0, 1)):
            for way in ways:
                self.copy(way, d, a).wait_recv()

        def pass_on(self, d, a, ways=(0, 1)):
            for way in ways:
                self.copy(way, d, a).wait_recv()
                self.copy(way, d + 1, a).start()

        def end(self):
            for copy in self.copies.values():
                copy.wait_send()

    own = qg.at[ctx]
    ring = Ring(qg, Q_AG + 2)
    ring.go(1, 0)
    near = remote(own, own, Q_AG, at(dz=4))
    near.start()
    partner_block = qg.at[block_of(0, 1)]
    opposite = remote(partner_block, partner_block, Q_AG + 1, at(dy=4))
    tell(0, beside_y + beside_x + beside_z)

    def pieces():
        for e in range(6):
            yield (e % 2 * 6, e // 2 * PART), (0, e * PART), 6
        yield (12, 0), (0, 6 * PART), 4
        yield (12, PART), (4, 6 * PART), 2
        yield (14, PART), (0, 7 * PART), 2
        yield (12, 2 * PART), (2, 7 * PART), 4

    def pack():
        for (pr, pc), (wr, wc), n in pieces():
            xf[pr : pr + n, pc : pc + PART] = xrow[wr : wr + n, wc : wc + PART]

    def unpack():
        for (pr, pc), (wr, wc), n in pieces():
            xrow[wr : wr + n, wc : wc + PART] = xf[pr : pr + n, pc : pc + PART]

    xrow[0:TOK, :] = res_ref[0].astype(F32)
    pack()
    rown[...] = xf[...].astype(BF16)
    lown[...] = jnp.zeros_like(lown)
    lown[0:1, 0:TOK] = logit_ref[...]
    res_copy = remote(rown, rfar, Z_RES, at(dz=4))
    res_copy.start()
    logit_copy = remote(lown, lfar, Z_RES + 1, at(dz=4))
    logit_copy.start()
    rtn[...] = jnp.zeros_like(rtn)

    newf[...] = jnp.zeros_like(newf)
    fresh = new_ref[0].astype(F32)
    newf[0, 0:TOK, :] = fresh[:, 0, :]
    newf[1, 0:TOK, :] = fresh[:, 1, :]
    for g in range(GROUPS):
        cols = slice(g * HEAD, (g + 1) * HEAD)
        kx[g, CACHE : CACHE + 16, :] = newf[0, :, cols].astype(BF16)
        vx[g, CACHE : CACHE + 16, 0:HEAD] = newf[1, :, cols].astype(BF16)
        kx[g, CACHE + 16 : KEYS, :] = jnp.zeros((KEYS - CACHE - 16, HEAD), BF16)
        vx[g, CACHE + 16 : KEYS, 0:HEAD] = jnp.zeros((KEYS - CACHE - 16, HEAD), BF16)
        vx[g, :, HEAD : 2 * HEAD] = jnp.ones((KEYS, HEAD), BF16)

    ids = jnp.sum(
        jnp.where(iota((96, 96), 0) == iota((96, 96), 1), rid_ref[0], 0), axis=1, keepdims=True
    )
    one_hot = (ids == iota((96, 128), 1)).astype(F32)
    before = (iota((96, 96), 1) < iota((96, 96), 0)).astype(BF16)
    counts = jnp.dot(before, one_hot.astype(BF16), preferred_element_type=F32)
    rank = jnp.sum(counts * one_hot, axis=1, keepdims=True)
    slot_col = ids.astype(F32) * 16.0 + rank
    slot_lane = jnp.sum(
        jnp.where(iota((96, 128), 0) == iota((96, 128), 1), slot_col, 0.0), axis=0, keepdims=True
    )

    for copy in cache_copies:
        copy.wait()

    limit = jnp.minimum(len_ref[0] - ctx * CACHE, CACHE)
    scale = HEAD ** (-0.5)

    def attend(blocks):
        count = len(blocks)
        rows = 32 * count
        row = iota((rows, KEYS), 0)
        lane = iota((rows, KEYS), 1)
        r = row & 31
        tok = r
        for edge in (6, 12, 18, 24):
            tok = tok - jnp.where(r >= edge, 6, 0)
        for i, block in enumerate(blocks):
            tok = tok + jnp.where((row >> 5) == i, block * TOK, 0)
        new_ok = (lane >= CACHE) & (lane < CACHE + TOK) & (ctx * TOK + lane - CACHE <= tok)
        bias[0:rows, :] = jnp.where((lane < limit) | new_ok, 0.0, NEG)

        def group(g, carry):
            q = jnp.concatenate([qg[block, g] for block in blocks], axis=0)
            scores = lax.dot_general(
                q, kx[g], (((1,), (1,)), ((), ())), preferred_element_type=F32
            )
            scores = scores * scale + bias[0:rows, :]
            top = jnp.maximum(jnp.max(scores, axis=1, keepdims=True), FLOOR)
            top = top.astype(BF16).astype(F32)
            weights = jnp.exp(scores - top).astype(BF16)
            sums = jnp.dot(weights, vx[g], preferred_element_type=F32)
            shape = (count, 32, HEAD)
            weighted = sums[:, 0:HEAD].reshape(shape)
            total = sums[:, HEAD : 2 * HEAD].reshape(shape)
            tops = jnp.broadcast_to(top, (rows, HEAD)).reshape(shape)
            on = (iota(shape, 2) & 31) == iota(shape, 1)
            top_row = jnp.sum(jnp.where(on, tops, 0.0), axis=1, keepdims=True)
            total_row = jnp.sum(jnp.where(on, total, 0.0), axis=1, keepdims=True)
            at_row = iota(shape, 1)
            packed = jnp.where(
                at_row == 30, top_row, jnp.where(at_row == 31, total_row, weighted)
            ).astype(BF16)
            for i, block in enumerate(blocks):
                pw[block, g] = packed[i]
            return carry

        lax.fori_loop(0, GROUPS, group, 0, unroll=4)

    scatters = []

    def pair_of(dy):
        return pl.ds(lax.rem(y + dy + NY, NY) * 2, 2)

    def ship(src, dst, sem, d):
        copy = remote(src, dst, sem, at(dy=d))
        copy.start()
        scatters.append(copy)
        return copy

    def ship_near(src, dst, base):
        up = ship(src.at[pair_of(1)], dst.at[1], base, 1)
        down = ship(src.at[pair_of(-1)], dst.at[2], base + 1, -1)
        return [up, down]

    def ship_three(src, dst, base):
        up = ship(src.at[pair_of(3)], dst.at[0], base + 2, 1)
        down = ship(src.at[pair_of(-3)], dst.at[1], base + 3, -1)
        return up, down

    def ship_four(src, dst, base):
        up = ship(src.at[block_of(4, 0)], dst.at[0], base + 4, 2)
        down = ship(src.at[block_of(4, 1)], dst.at[1], base + 5, -2)
        return up, down

    far = {}

    empty_row = iota((3, 32, HEAD), 1)
    empty = jnp.where(empty_row == 30, FLOOR, 0.0).astype(BF16)

    def settle_rin(g, carry):
        for i in range(3):
            for a in range(2):
                rin[5 + i, a, g] = empty[i]
        return carry

    lax.fori_loop(0, GROUPS, settle_rin, 0)
    ring.pass_on(1, 0)
    attend([block_of(0, 0), block_of(-1, 0), block_of(1, 0)])
    pl.semaphore_wait(know.at[0], 6)
    tell(1, beside_x + beside_z)
    ring.pass_on(2, 0)
    near.wait_recv()
    opposite.start()
    ring.go(1, 1)
    weight_copies = []
    for i, (src, dst) in enumerate(parts):
        weight_copies.append(remote(src, dst, WEIGHTS + i, at(flip=True)))
        weight_copies[i].start()
    attend([block_of(-2, 0), block_of(2, 0), block_of(0, 1)])
    pl.semaphore_wait(know.at[1], 4)
    tell(2, beside_x)
    rin[0] = pw[pair_of(0)]
    ring.pass_on(3, 0, (0,))
    ring.got(3, 0, (1,))
    ring.pass_on(1, 1)
    opposite.wait_recv()
    beyond = []
    for way, sign in ((0, 1), (1, -1)):
        block = qg.at[block_of(4, 1)]
        copy = remote(block, block, Q_AG + 2 + (way * 4 + 2) * 2 + 1, at(dy=sign))
        copy.start()
        beyond.append(copy)
    attend([block_of(-3, 0), block_of(3, 0), block_of(-1, 1), block_of(1, 1)])
    pl.semaphore_wait(know.at[2], 2)
    ship_near(pw, rin, Q_RS)
    ring.got(4, 0, (0,))
    for copy in beyond:
        copy.wait_recv()
    attend([block_of(4, 0), block_of(4, 1), block_of(-3, 1), block_of(3, 1)])
    far[3] = ship_three(pw, r3, Q_RS)
    far[4] = ship_four(pw, r4, Q_RS)
    ring.got(2, 1)
    attend([block_of(-2, 1), block_of(2, 1)])
    ring.end()
    for copy in beyond + [near, opposite, res_copy, logit_copy]:
        copy.wait_send()

    def merge(stack, count, normalize):
        wide = stack.astype(F32)
        tops = wide[:, 30, :]
        totals = wide[:, 31, :]
        top = jnp.max(tops, axis=0, keepdims=True)
        factor = jnp.exp(tops - top)
        total = jnp.sum(factor * totals, axis=0, keepdims=True)
        if normalize:
            factor = factor / total
        lane = iota((32, 128), 1)
        row = iota((32, 128), 0)
        on = ((lane & 31) == row) & (row < 30)
        merged = jnp.zeros((32, HEAD), F32)
        for part in range(count // 4):
            spread = jnp.zeros((32, 128), F32)
            for i in range(4):
                spread = jnp.where((lane >> 5) == i, factor[4 * part + i : 4 * part + i + 1], spread)
            spread = jnp.where(on, spread, 0.0)
            high = spread.astype(BF16)
            low = (spread - high.astype(F32)).astype(BF16)
            rows = stack[4 * part : 4 * part + 4].reshape(128, HEAD)
            merged = merged + jnp.dot(high, rows, preferred_element_type=F32)
            merged = merged + jnp.dot(low, rows, preferred_element_type=F32)
        return merged, top, total

    def merged_block(stack, count):
        merged, top, total = merge(stack, count, False)
        at_row = iota((32, HEAD), 0)
        return jnp.where(at_row == 30, top, jnp.where(at_row == 31, total, merged)).astype(BF16)

    for side in (0, 1):
        far[3][side].wait_recv()
        for a in (1 - side, side):
            if a == side:
                far[4][side].wait_recv()

            def group(g, carry, side=side, a=a):
                position = zh if a == 0 else 1 - zh
                own = pw[block_of(2 - 4 * side, a), g]
                third = r3[side, position, g]
                fourth = r4[side, g] if a == side else empty[0]
                stack = jnp.concatenate([own[None], third[None], fourth[None], empty[0:1]], axis=0)
                mg[side, a, g] = merged_block(stack, 4)
                return carry

            lax.fori_loop(0, GROUPS, group, 0, unroll=8)
            position = zh if a == 0 else 1 - zh
            ship(
                mg.at[side, a], rin.at[3 + side, position], Q_RS + 6 + 2 * side + a, 2 - 4 * side
            )
    for copy in scatters:
        copy.wait_send()
    for copy in scatters:
        if not any(copy is other for other in far[3] + far[4]):
            copy.wait_recv()
    scatters.clear()

    def merge_y(block):
        def group(g, carry):
            za[block, g] = merged_block(rin[:, block, g], NY)
            return carry

        lax.fori_loop(0, GROUPS, group, 0, unroll=8)

    across = []
    for a in (1, 0):
        position = zh if a == 0 else 1 - zh
        merge_y(position)
        copy = remote(za.at[position], zi.at[position], Q_Z + a, at(dz=4))
        copy.start()
        across.append(copy)

    def norm(position, logits, state_ref):
        def group(g, carry):
            stack = jnp.concatenate([za[position, g][None], zi[position, g][None], empty[0:2]], axis=0)
            merged, _, _ = merge(stack, 4, True)
            attf[g] = merged
            return carry

        lax.fori_loop(0, GROUPS, group, 0, unroll=8)
        for g in range(GROUPS):
            for j in range(PER_GROUP):
                h = g * PER_GROUP + j
                cols = slice(h * HEAD, (h + 1) * HEAD)
                state = xrow[0:TOK, cols] + attf[g, j * TOK : (j + 1) * TOK, :]
                state_ref[0:TOK, cols] = state.astype(BF16).astype(F32)
        state = state_ref[0:TOK, :]
        inv_rms = lax.rsqrt(jnp.mean(state * state, axis=1, keepdims=True) + 1e-05)
        logit = jnp.broadcast_to(logits, (TOK, 128))
        logit = jnp.sum(
            jnp.where(iota((TOK, 128), 0) == iota((TOK, 128), 1), logit, 0.0), axis=1, keepdims=True
        )
        gate = 1.0 / (1.0 + jnp.exp(-logit))
        xrow[0:TOK, :] = state * inv_rms * gain_ref[...].reshape(1, WIDTH).astype(F32) * gate
        pack()
        xg[y * 2 + position] = xf[...].astype(BF16)

    ring = Ring(xg, X_AG)
    xrow[0:TOK, :] = res_ref[0].astype(F32)
    across[0].wait_recv()
    norm(zh, lown[0:1, :], hid)
    ring.go(1, 0)
    res_copy.wait_recv()
    logit_copy.wait_recv()
    xf[...] = rfar[...].astype(F32)
    unpack()
    across[1].wait_recv()
    norm(1 - zh, lfar[0:1, :], hid2)
    ring.go(1, 1)
    for d in (1, 2):
        ring.pass_on(d, 0)
        ring.pass_on(d, 1)
    ring.pass_on(3, 0, (0,))
    ring.pass_on(3, 1, (1,))
    ring.got(3, 0, (1,))
    ring.got(3, 1, (0,))
    ring.got(4, 0, (0,))
    ring.got(4, 1, (1,))
    ring.end()
    for copy in across:
        copy.wait_send()

    rows_in = [xg[:, :, k * PART : (k + 1) * PART].reshape(256, PART) for k in range(3)]
    lanes = iota((96, 256), 1)
    lane_slots = []
    for k in range(3):
        tok, _ = item_of(lanes, k)
        lane_slots.append(
            jnp.sum(jnp.where(iota((96, 256), 0) == tok, slot_col, 0.0), axis=0, keepdims=True)
        )
    def make_slots(cls):
        first = lax.rem(zl + CLASSES[cls] + 4, 4) * 64
        for j in range(3):
            for half in range(2):
                target, eighth_row = slot_of(iota((64, 256), 0), j, half)
                target = (target + first).astype(F32)
                total = jnp.zeros((64, PART), F32)
                for k in thirds_for(j, half):
                    _, eighth_lane = item_of(iota((64, 256), 1), k)
                    pick = (lane_slots[k] == target) & (eighth_lane == eighth_row)
                    pick = jnp.where(pick, 1.0, 0.0).astype(BF16)
                    total = total + jnp.dot(pick, rows_in[k], preferred_element_type=F32)
                start = j * QUART + half * PART
                sb[cls, :, :, start : start + PART] = total.astype(BF16).reshape(4, 16, PART)

    def parity(cls):
        return lax.rem(y + cls, 2)

    def routes(cls):
        for i in (0, 1):
            dz = CLASSES[cls] if cls < 3 else 2 - 4 * i
            yield dz, 2 * i + parity(cls), 2 * cls + i

    odd, even = parity(0) == 1, parity(0) == 0

    def where_sent(cls, i, act, plane=odd):
        if (cls, i) == (0, 0):
            pl.when(plane)(act)
        else:
            act()

    sent = [[], [], [], []]
    for cls in ORDER:
        make_slots(cls)
        for i, (dz, dx, index) in enumerate(routes(cls)):
            copy = remote(sb.at[cls, lax.rem(x + dx, 4)], rb.at[cls, dx], GO + index, at(dz=dz, dx=dx))
            where_sent(cls, i, copy.start)
            sent[cls].append(copy)
    own_block = pltpu.make_async_copy(sb.at[0, x], rb.at[0, 0], local.at[24])
    own_block.start()

    for copy in copies + weight_copies:
        copy.wait()

    def experts(rows):
        n = rows.shape[0]
        main = jnp.dot(rows, wgu[0 : 3 * QUART, :], preferred_element_type=F32)
        r = iota((n, 512), 0) & 15
        tail = None
        for j in (2, 1, 0):
            part = jnp.dot(
                rows[:, j * QUART : (j + 1) * QUART],
                wgu[3 * QUART : 4 * QUART, :],
                preferred_element_type=F32,
            )
            part = pltpu.roll(part, n - 12 + 4 * j, 0)
            tail = part if tail is None else jnp.where(r < 4 * (j + 1), part, tail)
        both = main + tail
        gate_out, up_out = both[:, 0:256], both[:, 256:512]
        act = gate_out / (1.0 + jnp.exp(-gate_out)) * up_out
        r = iota((n, 256), 0) & 15
        act = jnp.where(r < 12, act, 0.0).astype(BF16).astype(F32)
        results = []
        for j in range(3):
            late = jnp.where(r >= 12, pltpu.roll(act, 12 - 4 * j, 0), 0.0)
            left = jnp.concatenate([act, late], axis=1).astype(BF16)
            results.append(jnp.dot(left, wdx[j], preferred_element_type=F32).astype(BF16))
        return results

    back = {}
    swaps = {}
    partial = {}

    def swap(cls):
        swaps[cls] = []
        for i, copy in enumerate(sent[cls]):
            block = rb.at[cls, 2 * i + parity(cls)]
            onward = remote(block, block, GO_Y + 2 * cls + i, at(dy=1 - 2 * i))

            def pass_on(copy=copy, onward=onward):
                copy.wait_recv()
                onward.start()

            where_sent(cls, i, pass_on)
            swaps[cls].append(onward)

    def swapped(cls):
        for i, onward in enumerate(swaps[cls]):
            where_sent(cls, i, onward.wait_recv, even)

    def run(first, count):
        rows = rb[first : first + count].reshape(64 * count, 3 * QUART)
        for j, part in enumerate(experts(rows)):
            pp[first : first + count, :, :, j * QUART : (j + 1) * QUART] = part.reshape(
                count, 4, 16, QUART
            )

    def give(cls):
        partial[cls] = []
        for i in (0, 1):
            block = pp.at[cls, 2 * i + 1 - parity(cls)]
            copy = remote(block, yq.at[cls, i], BACK_Y + 2 * cls + i, at(dy=2 * i - 1))
            where_sent(cls, i, copy.start, even)
            partial[cls].append(copy)

    def send_back(cls):
        back[cls] = []
        for i, (dz, dx, index) in enumerate(routes(cls)):
            copy = remote(pp.at[cls, dx], rtn.at[expert], BACK + index, at(dz=-dz, dx=-dx))

            def add_planes(i=i, dx=dx, copy=copy):
                partial[cls][i].wait_recv()
                total = pp[cls, dx].astype(F32) + yq[cls, i].astype(F32)
                pp[cls, dx] = total.astype(BF16)
                copy.start()

            where_sent(cls, i, add_planes)
            back[cls].append(copy)

    own_block.wait()
    for cls in ORDER:
        swap(cls)
    swapped(1)
    swapped(2)
    run(1, 2)
    give(1)
    give(2)
    swapped(3)
    run(3, 1)
    give(3)
    swapped(0)
    run(0, 1)
    give(0)
    rtn[expert] = pp[0, 0]
    for cls in ORDER:
        send_back(cls)

    for cls in range(4):
        for i in (0, 1):
            where_sent(cls, i, sent[cls][i].wait_send)
            where_sent(cls, i, swaps[cls][i].wait_send)
            where_sent(cls, i, partial[cls][i].wait_send, even)
            where_sent(cls, i, back[cls][i].wait)

    due = []
    lanes = iota((256, 128), 1)
    for k in range(3):
        tok, _ = item_of(iota((256, 128), 0), k)
        row_slots = jnp.sum(jnp.where(lanes == tok, slot_lane, 0.0), axis=1, keepdims=True)
        _, eighth_row = item_of(iota((256, 256), 0), k)
        total = jnp.zeros((256, PART), F32)
        for j in range(3):
            for half in range(2):
                if k not in thirds_for(j, half):
                    continue
                target, eighth_lane = slot_of(iota((256, 256), 1), j, half)
                pick = (row_slots == target.astype(F32)) & (eighth_lane == eighth_row)
                pick = jnp.where(pick, 1.0, 0.0).astype(BF16)
                start = j * QUART + half * PART
                source = rtn[:, :, start : start + PART].reshape(256, PART)
                total = total + jnp.dot(pick, source, preferred_element_type=F32)
        rsb[k] = total.astype(BF16).reshape(16, 16, PART)
        base = Y_RS + 11 * k
        far[3, k] = ship_three(rsb.at[k], f3.at[k], base)
        far[4, k] = ship_four(rsb.at[k], f4.at[k], base)
        due.append([])
        due[k] += ship_near(rsb.at[k], rsi.at[k], base)
        rsi[k, 0] = rsb[k, pair_of(0)]

    for k in range(3):
        for side in (0, 1):
            far[3, k][side].wait_recv()
            for a in (1 - side, side):
                position = zh if a == 0 else 1 - zh
                total = rsb[k, block_of(2 - 4 * side, a)].astype(F32)
                total = total + f3[k, side, position].astype(F32)
                if a == side:
                    far[4, k][side].wait_recv()
                    total = total + f4[k, side].astype(F32)
                fm[k, side, a] = total.astype(BF16)
                copy = ship(
                    fm.at[k, side, a],
                    rsi.at[k, 3 + side, position],
                    Y_RS + 11 * k + 6 + 2 * side + a,
                    2 - 4 * side,
                )
                due[k].append(copy)

    def add_up(k, block):
        total = rsi[k, 0, block].astype(F32)
        for i in range(1, 5):
            total = total + rsi[k, i, block].astype(F32)
        return total

    across = []
    for k in range(3):
        for copy in due[k]:
            copy.wait_recv()
        zo2[k] = add_up(k, 1 - zh).astype(BF16)
        across.append(remote(zo2.at[k], zi2.at[k], Y_RS + 11 * k + 10, at(dz=4)))
        across[k].start()
    for k in range(3):
        total = add_up(k, zh)
        across[k].wait_recv()
        xf[:, k * PART : (k + 1) * PART] = total + zi2[k].astype(F32)
    unpack()
    out_ref[0] = (hid[0:TOK, :] + xrow[0:TOK, :]).astype(BF16)
    for copy in scatters + across:
        copy.wait_send()


def body(
    queries,
    new_kv,
    cached_key_value,
    cache_len,
    residual,
    norm_gain,
    route_logit,
    route_id,
    w_gate,
    w_up,
    w_down,
):
    vmem = pl.BlockSpec(memory_space=pltpu.VMEM)
    smem = pl.BlockSpec(memory_space=pltpu.SMEM)
    hbm = pl.BlockSpec(memory_space=pl.ANY)
    block = (GROUPS, 32, HEAD)
    slots = (16, 16, 3 * QUART)
    return pl.pallas_call(
        kernel,
        out_shape=jax.ShapeDtypeStruct((1, TOK, WIDTH), BF16),
        in_specs=[vmem, vmem, hbm, smem, vmem, vmem, vmem, vmem, hbm, hbm, hbm],
        out_specs=vmem,
        scratch_shapes=[
            pltpu.VMEM(block, F32),
            pltpu.VMEM((16,) + block, BF16),
            pltpu.VMEM((16,) + block, BF16),
            pltpu.VMEM((NY, 2) + block, BF16),
            pltpu.VMEM((2,) + block, BF16),
            pltpu.VMEM((2,) + block, BF16),
            pltpu.VMEM((2, 2) + block, BF16),
            pltpu.VMEM((2,) + block, BF16),
            pltpu.VMEM((2, 2) + block, BF16),
            pltpu.VMEM(block, F32),
            pltpu.VMEM((16, 3 * PART), BF16),
            pltpu.VMEM((16, 3 * PART), BF16),
            pltpu.VMEM((8, 128), F32),
            pltpu.VMEM((8, 128), F32),
            pltpu.VMEM((8, WIDTH), F32),
            pltpu.VMEM((8, WIDTH), F32),
            pltpu.VMEM((8, WIDTH), F32),
            pltpu.VMEM((16, 3 * PART), F32),
            pltpu.VMEM((16, 16, 3 * PART), BF16),
            pltpu.VMEM((4, 4, 16, 3 * QUART), BF16),
            pltpu.VMEM((4, 4, 16, 3 * QUART), BF16),
            pltpu.VMEM((4, 4, 16, 3 * QUART), BF16),
            pltpu.VMEM((4, 2, 16, 3 * QUART), BF16),
            pltpu.VMEM(slots, BF16),
            pltpu.VMEM((3, 16, 16, PART), BF16),
            pltpu.VMEM((3, 5, 2, 16, PART), BF16),
            pltpu.VMEM((3, 2, 2, 16, PART), BF16),
            pltpu.VMEM((3, 2, 16, PART), BF16),
            pltpu.VMEM((3, 2, 2, 16, PART), BF16),
            pltpu.VMEM((3, 16, PART), BF16),
            pltpu.VMEM((3, 16, PART), BF16),
            pltpu.VMEM((WIDTH, 512), BF16),
            pltpu.VMEM((3, 512, QUART), BF16),
            pltpu.VMEM((GROUPS, KEYS, HEAD), BF16),
            pltpu.VMEM((GROUPS, KEYS, 2 * HEAD), BF16),
            pltpu.VMEM((2, 16, GROUPS * HEAD), F32),
            pltpu.VMEM((128, KEYS), F32),
            pltpu.SemaphoreType.DMA((N_SEM,)),
            pltpu.SemaphoreType.DMA((N_SEM,)),
            pltpu.SemaphoreType.DMA((26,)),
            pltpu.SemaphoreType.REGULAR((3,)),
        ],
        compiler_params=pltpu.CompilerParams(
            collective_id=0, has_side_effects=True, vmem_limit_bytes=56 * 1024 * 1024
        ),
    )(
        queries,
        jnp.transpose(new_kv, (1, 2, 0, 3)),
        cached_key_value,
        cache_len,
        residual,
        norm_gain,
        route_logit,
        jnp.transpose(route_id, (0, 2, 1)),
        w_gate,
        w_up,
        w_down,
    )


def solution(mesh):
    placed = (
        P("ep", "ctx", None),
        P(None, "ep", "ctx", None),
        P(None, "ep", "ctx", None),
        P("ep"),
        P("ep", "ctx", None),
        P(),
        P("ep", "ctx"),
        P("ep", None, None),
        P("ep", None, "ctx"),
        P("ep", None, "ctx"),
        P("ep", "ctx", None),
    )
    return jax.shard_map(
        body, mesh=mesh, in_specs=placed, out_specs=P("ep", "ctx", None), check_vma=False
    )
```
